32 devices in a mesh: row: 4 (over y, x), head: 4 (over z), seq: 2 (over core).
Axes of the slice: x: 2, y: 2, z: 4, core: 2. Of those that a mesh axis runs over, the one named last changes fastest.
Arguments:
- tokens: bfloat16 [16, 512, 768], P(('row', 'seq'), 'head'), may hold values from -6 to 6
- lengths: int32 [16], P(('row', 'seq')), may hold values from 461 to 512, as said below
- cotangent: bfloat16 [16, 512, 768], P(('row', 'seq'), 'head'), may hold values from -6 to 6
- t_query: bfloat16 [768, 768], P(None, 'head'), may hold values from -0.21875 to 0.21875
- t_query_bias: float32 [768], P('head'), may hold values from -3 to 3
- t_key: bfloat16 [768, 768], P(None, 'head'), may hold values from -0.21875 to 0.21875
- t_value: bfloat16 [768, 768], P(None, 'head'), may hold values from -0.21875 to 0.21875
- t_value_bias: float32 [768], P('head'), may hold values from -3 to 3
- t_attn_out: bfloat16 [768, 768], P('head'), may hold values from -0.875 to 0.875
- t_attn_bias: float32 [768], replicated, may hold values from -3 to 3
- t_norm1_gain: float32 [768], replicated, may hold values from 0.1 to 1.9
- t_norm1_bias: float32 [768], replicated, may hold values from -2 to 2
- t_ffn_in: bfloat16 [768, 3072], P(None, ('head', 'seq')), may hold values from -0.21875 to 0.21875
- t_ffn_in_bias: bfloat16 [3072], P(('head', 'seq')), may hold values from -3 to 3
- t_ffn_out: bfloat16 [3072, 768], P(('head', 'seq')), may hold values from -0.109375 to 0.109375
- t_ffn_out_bias: float32 [768], replicated, may hold values from -3 to 3
- t_norm2_gain: float32 [768], replicated, may hold values from 0.1 to 1.9
- t_norm2_bias: float32 [768], replicated, may hold values from -2 to 2
- s_query: bfloat16 [768, 384], replicated, may hold values from -0.21875 to 0.21875
- s_query_bias: float32 [384], replicated, may hold values from -3 to 3
- s_key: bfloat16 [768, 384], replicated, may hold values from -0.21875 to 0.21875
- s_value: bfloat16 [768, 384], replicated, may hold values from -0.21875 to 0.21875
- s_value_bias: float32 [384], replicated, may hold values from -3 to 3
- s_attn_out: bfloat16 [384, 768], replicated, may hold values from -1.25 to 1.25
- s_attn_bias: float32 [768], replicated, may hold values from -3 to 3
- s_norm1_gain: float32 [768], replicated, may hold values from 0.1 to 1.9
- s_norm1_bias: float32 [768], replicated, may hold values from -2 to 2
- s_ffn_in: bfloat16 [768, 1536], P(None, ('head', 'seq')), may hold values from -0.21875 to 0.21875
- s_ffn_in_bias: bfloat16 [1536], P(('head', 'seq')), may hold values from -3 to 3
- s_ffn_out: bfloat16 [1536, 768], P(('head', 'seq')), may hold values from -0.15625 to 0.15625
- s_ffn_out_bias: float32 [768], replicated, may hold values from -3 to 3
- s_norm2_gain: float32 [768], replicated, may hold values from 0.1 to 1.9
- s_norm2_bias: float32 [768], replicated, may hold values from -2 to 2
Outputs:
- output: float32 [16, 512, 768], P(('row', 'seq'), 'head')
- input_grad: float32 [16, 512, 768], P(('row', 'seq'), 'head')
- grad_t_query: float32 [768, 768], P(None, 'head')
- grad_t_query_bias: float32 [768], P('head')
- grad_t_key: float32 [768, 768], P(None, 'head')
- grad_t_value: float32 [768, 768], P(None, 'head')
- grad_t_value_bias: float32 [768], P('head')
- grad_t_attn_out: float32 [768, 768], P('head')
- grad_t_attn_bias: float32 [768], replicated
- grad_t_norm1_gain: float32 [768], replicated
- grad_t_norm1_bias: float32 [768], replicated
- grad_t_ffn_in: float32 [768, 3072], P(None, ('head', 'seq'))
- grad_t_ffn_in_bias: float32 [3072], P(('head', 'seq'))
- grad_t_ffn_out: float32 [3072, 768], P(('head', 'seq'))
- grad_t_ffn_out_bias: float32 [768], replicated
- grad_t_norm2_gain: float32 [768], replicated
- grad_t_norm2_bias: float32 [768], replicated
- grad_s_query: float32 [768, 384], replicated
- grad_s_query_bias: float32 [384], replicated
- grad_s_key: float32 [768, 384], replicated
- grad_s_value: float32 [768, 384], replicated
- grad_s_value_bias: float32 [384], replicated
- grad_s_attn_out: float32 [384, 768], replicated
- grad_s_attn_bias: float32 [768], replicated
- grad_s_norm1_gain: float32 [768], replicated
- grad_s_norm1_bias: float32 [768], replicated
- grad_s_ffn_in: float32 [768, 1536], P(None, ('head', 'seq'))
- grad_s_ffn_in_bias: float32 [1536], P(('head', 'seq'))
- grad_s_ffn_out: float32 [1536, 768], P(('head', 'seq'))
- grad_s_ffn_out_bias: float32 [768], replicated
- grad_s_norm2_gain: float32 [768], replicated
- grad_s_norm2_bias: float32 [768], replicated
The draws below stay inside these ranges and needn't reach their ends.
Inputs may be any that keep to these rules, and one draw needn't show every extreme that they name: `lengths`: in each block of 2 consecutive sequences one sequence has length 512.
All inputs are finite; a program needn't handle non-finite values.
Results may differ from the reference program's by a relative error of at most 0.034.
Values may be sent and summed in bfloat16 or wider, within the bound.
A program may use at most 256 MiB of HBM per device.

```python
import math
import jax
import jax.numpy as jnp
from jax import lax

D = 768
HEADS = 12
HD = 64
FF = 3072
S_HEADS = 6
FS = 1536
LEN = 512
SEQ_DEV = 2
NSEQ = 16


def draw_lengths(key, part):
    key = jax.random.fold_in(key, 11)
    base_key, pick_key = jax.random.split(key)
    drawn = jax.random.randint(base_key, (NSEQ,), LEN - LEN // 10, LEN + 1)
    picked = jax.random.randint(pick_key, (NSEQ // SEQ_DEV,), 0, SEQ_DEV)
    full_mark = (jnp.arange(SEQ_DEV)[None, :] == picked[:, None]).reshape(NSEQ)
    return jnp.where(full_mark, LEN, drawn).astype(jnp.int32)


def steps_of(own_key, shape, shards, smallest, top_value):
    def one(axis_at, shards_of):
        steps = jax.random.uniform(jax.random.fold_in(jax.random.fold_in(own_key, 6), axis_at), (shards_of,), jnp.float32, smallest / len(shards), top_value / len(shards))
        return jnp.repeat(jnp.exp(steps), shape[axis_at] // shards_of).reshape((-1,) + (1,) * (len(shape) - axis_at - 1))

    factor_of = one(*shards[0])
    for cut in shards[1:]:
        factor_of = factor_of * one(*cut)
    return factor_of


def normal_values(rng, dims, scale, most, cuts=(), kind=jnp.bfloat16):
    values = jax.random.normal(rng, dims, jnp.float32) * scale
    if len(cuts) > 0:
        values = steps_of(rng, dims, cuts, -0.22, 0.18) * values
    return jnp.clip(values, min=-most, max=most).astype(kind)


def setup_inputs(seed: int = 0) -> dict:
    key_of = jax.random.split(jax.random.key(seed), 34)
    return {
        "tokens": normal_values(key_of[0], (NSEQ, LEN, D), 1.0, 6.0, ((0, 8), (1, 4))),
        "lengths": draw_lengths(jax.random.fold_in(key_of[33], 71), 0),
        "cotangent": normal_values(key_of[2], (NSEQ, LEN, D), 1.0, 6.0, ((0, 8), (1, 4))),
        "t_query": normal_values(key_of[3], (D, HEADS * HD), D ** -0.5, 0.21875, ((1, 4),)),
        "t_query_bias": normal_values(key_of[4], (HEADS * HD,), 0.5, 3.0, ((0, 4),), jnp.float32),
        "t_key": normal_values(key_of[5], (D, HEADS * HD), D ** -0.5, 0.21875, ((1, 4),)),
        "t_value": normal_values(key_of[6], (D, HEADS * HD), D ** -0.5, 0.21875, ((1, 4),)),
        "t_value_bias": normal_values(key_of[7], (HEADS * HD,), 0.5, 3.0, ((0, 4),), jnp.float32),
        "t_attn_out": normal_values(key_of[8], (HEADS * HD, D), (HEADS * HD // 16) ** -0.5, 0.875, ((0, 4),)),
        "t_attn_bias": normal_values(key_of[9], (D,), 0.5, 3.0, (), jnp.float32),
        "t_norm1_gain": jnp.clip(1.0 + 0.18 * jax.random.normal(key_of[10], (D,), jnp.float32), 0.1, 1.9),
        "t_norm1_bias": normal_values(key_of[11], (D,), 0.3, 2.0, (), jnp.float32),
        "t_ffn_in": normal_values(key_of[12], (D, FF), D ** -0.5, 0.21875, ((1, 8),)),
        "t_ffn_in_bias": normal_values(key_of[13], (FF,), 0.5, 3.0, ((0, 8),)),
        "t_ffn_out": normal_values(key_of[14], (FF, D), FF ** -0.5, 0.109375, ((0, 8),)),
        "t_ffn_out_bias": normal_values(key_of[15], (D,), 0.5, 3.0, (), jnp.float32),
        "t_norm2_gain": jnp.clip(1.0 + 0.18 * jax.random.normal(key_of[16], (D,), jnp.float32), 0.1, 1.9),
        "t_norm2_bias": normal_values(key_of[17], (D,), 0.3, 2.0, (), jnp.float32),
        "s_query": normal_values(key_of[18], (D, S_HEADS * HD), D ** -0.5, 0.21875),
        "s_query_bias": normal_values(key_of[19], (S_HEADS * HD,), 0.5, 3.0, (), jnp.float32),
        "s_key": normal_values(key_of[20], (D, S_HEADS * HD), D ** -0.5, 0.21875),
        "s_value": normal_values(key_of[21], (D, S_HEADS * HD), D ** -0.5, 0.21875),
        "s_value_bias": normal_values(key_of[22], (S_HEADS * HD,), 0.5, 3.0, (), jnp.float32),
        "s_attn_out": normal_values(key_of[23], (S_HEADS * HD, D), (S_HEADS * HD // 16) ** -0.5, 1.25),
        "s_attn_bias": normal_values(key_of[24], (D,), 0.5, 3.0, (), jnp.float32),
        "s_norm1_gain": jnp.clip(1.0 + 0.18 * jax.random.normal(key_of[25], (D,), jnp.float32), 0.1, 1.9),
        "s_norm1_bias": normal_values(key_of[26], (D,), 0.3, 2.0, (), jnp.float32),
        "s_ffn_in": normal_values(key_of[27], (D, FS), D ** -0.5, 0.21875, ((1, 8),)),
        "s_ffn_in_bias": normal_values(key_of[28], (FS,), 0.5, 3.0, ((0, 8),)),
        "s_ffn_out": normal_values(key_of[29], (FS, D), FS ** -0.5, 0.15625, ((0, 8),)),
        "s_ffn_out_bias": normal_values(key_of[30], (D,), 0.5, 3.0, (), jnp.float32),
        "s_norm2_gain": jnp.clip(1.0 + 0.18 * jax.random.normal(key_of[31], (D,), jnp.float32), 0.1, 1.9),
        "s_norm2_bias": normal_values(key_of[32], (D,), 0.3, 2.0, (), jnp.float32),
    }


@jax.custom_vjp
def low(v):
    return lax.optimization_barrier(v.astype(jnp.bfloat16)).astype(jnp.float32)

@jax.custom_vjp
def low_back(v):
    return v

def low_keep(v):
    return (low(v), None)

def low_pass(kept, grad):
    return (grad,)

def back_keep(v):
    return (v, None)

def back_low(kept, grad):
    return (low(grad),)
low.defvjp(low_keep, low_pass)
low_back.defvjp(back_keep, back_low)
EPSILON = 1e-05
HIGHEST = lax.Precision.HIGHEST

def layer_norm(values, gain, shift):
    center = values - lax.optimization_barrier(jnp.mean(values, axis=-1, keepdims=True))
    spread = lax.optimization_barrier(jnp.mean(center * center, axis=-1, keepdims=True))
    return center * lax.rsqrt(spread + EPSILON) * gain + shift

def smooth_gate(pre):
    return 0.5 * pre * (1.0 + jnp.tanh(0.7978845608028654 * (pre + 0.044715 * pre * pre * pre)))

def attend_one(packed):
    queries, keys_in, values, length = packed
    scores = jnp.einsum('qhe,khe->hqk', queries, keys_in, precision=HIGHEST) / math.sqrt(HD)
    allowed = jnp.arange(LEN, dtype=jnp.int32) < length
    scores = low_back(jnp.where(allowed[None, None, :], scores, -1000000000.0))
    top_score = lax.optimization_barrier(jnp.max(scores, axis=-1, keepdims=True))
    expo = jnp.exp(scores - top_score)
    probs = expo / lax.optimization_barrier(jnp.sum(expo, axis=-1, keepdims=True))
    return jnp.einsum('hqk,khe->qhe', low(probs), values, precision=HIGHEST)

def block(inputs, weights, lengths, head_count):
    w_query, b_query, w_key, w_value, b_value, w_out, b_out, gain_one, shift_one, ffn_in, ffn_in_bias, ffn_out, ffn_out_bias, gain_two, shift_two = weights
    seq_count = inputs.shape[0]
    rounded = low(inputs)
    queries = low_back(low(jnp.dot(rounded, w_query, precision=HIGHEST) + b_query))
    keys_in = low_back(low(jnp.dot(rounded, w_key, precision=HIGHEST)))
    values = low_back(low(jnp.dot(rounded, w_value, precision=HIGHEST) + b_value))
    shape = (seq_count, LEN, head_count, HD)
    mixed = lax.map(jax.checkpoint(attend_one), (queries.reshape(shape), keys_in.reshape(shape), values.reshape(shape), lengths))
    mixed = low_back(low(mixed.reshape(seq_count, LEN, head_count * HD)))
    attn = low_back(jnp.dot(mixed, w_out, precision=HIGHEST) + b_out)
    normed = low(layer_norm(rounded + attn, gain_one, shift_one))
    pre = low_back(jnp.dot(normed, ffn_in, precision=HIGHEST) + ffn_in_bias)
    hidden = low(smooth_gate(pre))
    ffn = low_back(jnp.dot(hidden, ffn_out, precision=HIGHEST) + ffn_out_bias)
    return layer_norm(normed + ffn, gain_two, shift_two)

def reference(tokens, lengths, cotangent, t_query, t_query_bias, t_key, t_value, t_value_bias, t_attn_out, t_attn_bias, t_norm1_gain, t_norm1_bias, t_ffn_in, t_ffn_in_bias, t_ffn_out, t_ffn_out_bias, t_norm2_gain, t_norm2_bias, s_query, s_query_bias, s_key, s_value, s_value_bias, s_attn_out, s_attn_bias, s_norm1_gain, s_norm1_bias, s_ffn_in, s_ffn_in_bias, s_ffn_out, s_ffn_out_bias, s_norm2_gain, s_norm2_bias):
    teacher = tuple((weight.astype(jnp.float32) for weight in (t_query, t_query_bias, t_key, t_value, t_value_bias, t_attn_out, t_attn_bias, t_norm1_gain, t_norm1_bias, t_ffn_in, t_ffn_in_bias, t_ffn_out, t_ffn_out_bias, t_norm2_gain, t_norm2_bias)))
    student = tuple((weight.astype(jnp.float32) for weight in (s_query, s_query_bias, s_key, s_value, s_value_bias, s_attn_out, s_attn_bias, s_norm1_gain, s_norm1_bias, s_ffn_in, s_ffn_in_bias, s_ffn_out, s_ffn_out_bias, s_norm2_gain, s_norm2_bias)))

    def forward(inputs, teacher_weights, student_weights):
        middle = block(inputs, teacher_weights, lengths, HEADS)
        return block(middle, student_weights, lengths, S_HEADS)
    output, pull = jax.vjp(forward, tokens.astype(jnp.float32), teacher, student)
    grad_in, grad_t, grad_s = pull(cotangent.astype(jnp.float32))
    return (output, grad_in, grad_t[0], grad_t[1], grad_t[2], grad_t[3], grad_t[4], grad_t[5], grad_t[6], grad_t[7], grad_t[8], grad_t[9], grad_t[10], grad_t[11], grad_t[12], grad_t[13], grad_t[14], grad_s[0], grad_s[1], grad_s[2], grad_s[3], grad_s[4], grad_s[5], grad_s[6], grad_s[7], grad_s[8], grad_s[9], grad_s[10], grad_s[11], grad_s[12], grad_s[13], grad_s[14])
```

```python
import functools

import jax
import jax.numpy as jnp
from jax import lax
from jax.experimental import pallas as pl
from jax.experimental.pallas import tpu as pltpu
from jax.sharding import PartitionSpec as P

MESH = pl.DeviceIdType.MESH
F32 = jnp.float32
BF = jnp.bfloat16
EPS = 1e-5
MASKED = -1000000000.0
VMEM_LIMIT = 63 << 20


class Place:
    def __init__(self):
        self.r = lax.axis_index("row")
        self.z = lax.axis_index("head")
        self.s = lax.axis_index("seq")
        self.c = lax.rem(self.s, 2)

    def core(self):
        return (self.r, self.z, self.s + 1 - 2 * self.c)

    def line_index(self, step):
        return lax.rem(self.z + step + 4, 4)

    def line(self, step):
        return (self.r, self.line_index(step), self.s)

    def plane_index(self, k):
        if k == 1:
            return self.r + 1 - 2 * lax.rem(self.r, 2)
        if k == 2:
            return lax.rem(self.r + 2, 4)
        return 3 - self.r

    def plane(self, k):
        return (self.plane_index(k), self.z, self.s)


def greet(me):
    barrier = pltpu.get_barrier_semaphore()
    others = [me.core()] + [me.line(i) for i in (1, 2, 3)] + [me.plane(k) for k in (1, 2, 3)]
    for other in others:
        pl.semaphore_signal(barrier, inc=1, device_id=other, device_id_type=MESH)
    pl.semaphore_wait(barrier, len(others))


def remote(src, dst, send_sem, recv_sem, device):
    return pltpu.make_async_remote_copy(
        src_ref=src, dst_ref=dst, send_sem=send_sem, recv_sem=recv_sem, device_id=device, device_id_type=MESH
    )


def rows_of(index, count):
    return pl.ds(pl.multiple_of(index * count, 16), count)


def gather_kernel(*refs):
    me = Place()
    r, z, s, c = me.r, me.z, me.s, me.c
    (tok, cot, lens, pack, tq, tk, tv, to, ti, tf, si, sf) = refs[:12]
    (X, CT, LN, BP, WQ, WK, WV, WO, WI, WF, SI, SF) = refs[12:24]
    (zs, zr, ps, pr, ls, xs, xr, fs, fr) = refs[24:]
    greet(me)
    owner = z // 2 == c

    seqs = [(tok, X), (cot, CT)]
    for a, (src, dst) in enumerate(seqs):
        for j in range(2):
            target = 2 * c + j

            @pl.when(target != z)
            def _():
                remote(src.at[j], dst.at[z], xs.at[a, j], xr.at[a, z], (r, target, s)).start()

            @pl.when(target == z)
            def _():
                pltpu.make_async_copy(src.at[j], dst.at[z], xr.at[a, z]).start()

    shards = [(tq, WQ, 2), (tk, WK, 2), (tv, WV, 2), (to, WO, 2), (ti, WI, 4), (tf, WF, 4), (si, SI, 4), (sf, SF, 4)]

    def when_unit(count, cond):
        return (lambda f: pl.when(cond)(f)) if count == 2 else (lambda f: f())

    for w, (src, dst, count) in enumerate(shards):
        piece = rows_of(r, src.shape[0] // 4)
        slot = z % 2 if count == 2 else z

        @when_unit(count, owner)
        def _():
            pltpu.make_async_copy(src, dst.at[slot], ls.at[w]).start()
            for d in (1, 2, 3):
                remote(src.at[piece], dst.at[slot, piece], zs.at[w, d - 1], zr.at[w, d - 1], me.line(d)).start()

    own_pack = pltpu.make_async_copy(pack, BP.at[z], ls.at[8])
    own_pack.start()
    for d in (1, 2, 3):
        remote(pack, BP.at[z], zs.at[8, d - 1], zr.at[8, d - 1], me.line(d)).start()

    @pl.when(owner)
    def _():
        mine = pltpu.make_async_copy(lens.at[z % 2], LN, ls.at[9])
        mine.start()
        remote(lens.at[z % 2], LN, fs.at[2, 0], fr.at[2, 0], me.core()).start()
        for a, (src, dst) in enumerate(seqs):
            pltpu.make_async_copy(src.at[0], dst.at[z], xr.at[a, z]).wait()
            remote(dst.at[z], dst.at[z], fs.at[a, 0], fr.at[a, z], me.core()).start()
            for d in (1, 2, 3):
                frm = me.line_index(-d)
                remote(src.at[0], dst.at[frm], xs.at[a, 0], xr.at[a, frm], me.core()).wait_recv()
                remote(dst.at[frm], dst.at[frm], fs.at[a, d], fr.at[a, frm], me.core()).start()
        mine.wait()

    for w, (src, dst, count) in enumerate(shards):
        piece = rows_of(r, src.shape[0] // 4)
        for d in (1, 2, 3):
            frm = me.line_index(-d)
            slot = frm % 2 if count == 2 else frm

            @when_unit(count, frm // 2 == c)
            def _():
                part = dst.at[slot, piece]
                remote(part, part, zs.at[w, d - 1], zr.at[w, d - 1], me.core()).wait_recv()
                for k in (1, 2, 3):
                    remote(part, part, ps.at[w, d - 1, k - 1], pr.at[w, d - 1, k - 1], me.plane(k)).start()

    for w, (src, dst, count) in enumerate(shards):
        piece = rows_of(r, src.shape[0] // 4)
        slot_own = z % 2 if count == 2 else z

        @when_unit(count, owner)
        def _():
            pltpu.make_async_copy(src, dst.at[slot_own], ls.at[w]).wait()
            for d in (1, 2, 3):
                remote(src.at[piece], dst.at[slot_own, piece], zs.at[w, d - 1], zr.at[w, d - 1], me.line(d)).wait_send()

        for d in (1, 2, 3):
            frm = me.line_index(-d)
            slot = frm % 2 if count == 2 else frm

            @when_unit(count, frm // 2 == c)
            def _():
                for k in (1, 2, 3):
                    theirs = dst.at[slot, rows_of(me.plane_index(k), src.shape[0] // 4)]
                    remote(theirs, theirs, ps.at[w, d - 1, k - 1], pr.at[w, d - 1, k - 1], me.plane(k)).wait()

    own_pack.wait()
    for d in (1, 2, 3):
        remote(pack, BP.at[me.line_index(-d)], zs.at[8, d - 1], zr.at[8, d - 1], me.line(d)).wait()
    for a, (src, dst) in enumerate(seqs):
        for j in range(2):

            @pl.when(2 * c + j != z)
            def _():
                remote(src.at[j], dst.at[z], xs.at[a, j], xr.at[a, z], me.core()).wait_send()

    @pl.when(owner)
    def _():
        remote(lens.at[0], LN, fs.at[2, 0], fr.at[2, 0], me.core()).wait_send()
        for a, (src, dst) in enumerate(seqs):
            for d in range(4):
                remote(dst.at[0], dst.at[0], fs.at[a, d], fr.at[a, 0], me.core()).wait_send()

    @pl.when(jnp.logical_not(owner))
    def _():
        remote(lens.at[0], LN, fs.at[2, 0], fr.at[2, 0], me.core()).wait_recv()
        for a, (src, dst) in enumerate(seqs):
            for d in range(4):
                remote(dst.at[d], dst.at[d], fs.at[a, d], fr.at[a, d], me.core()).wait_recv()


def nn(a, b):
    return lax.dot_general(a, b, (((1,), (0,)), ((), ())), preferred_element_type=F32)


def nt(a, b):
    return lax.dot_general(a, b, (((1,), (1,)), ((), ())), preferred_element_type=F32)


def tn(a, b):
    return lax.dot_general(a, b, (((0,), (0,)), ((), ())), preferred_element_type=F32)


def norm_parts(value):
    center = value - jnp.mean(value, axis=-1, keepdims=True)
    spread = jnp.mean(center * center, axis=-1, keepdims=True)
    rstd = lax.rsqrt(spread + EPS)
    return center * rstd, rstd


def norm_grad(xh, rstd, gain, dy):
    scaled = dy * gain
    mean_one = jnp.mean(scaled, axis=-1, keepdims=True)
    mean_two = jnp.mean(scaled * xh, axis=-1, keepdims=True)
    return (scaled - mean_one - xh * mean_two) * rstd


def col_sum(value):
    return jnp.sum(value, axis=0, keepdims=True)


class Swap:
    def __init__(self, me, send, recv, ssem, rsem, chunks):
        self.me, self.send, self.recv, self.ssem, self.rsem = me, send, recv, ssem, rsem
        self.rows = send.shape[1] // chunks
        self.chunks = chunks
        self.turn = 0

    def copy(self, slot, i):
        rows = rows_of(i, self.rows)
        return remote(
            self.send.at[slot, rows],
            self.recv.at[slot, rows],
            self.ssem.at[slot, i],
            self.rsem.at[slot, i],
            self.me.core(),
        )

    def run(self, part, between, post):
        slot = self.turn % 2
        self.turn += 1

        @pl.loop(0, self.chunks)
        def _(i):
            rows = rows_of(i, self.rows)
            self.send[slot, rows] = part(rows).astype(BF)
            self.copy(slot, i).start()

        if between is not None:
            between()

        @pl.loop(0, self.chunks)
        def _(i):
            rows = rows_of(i, self.rows)
            self.copy(slot, i).wait()
            total = self.send[slot, rows].astype(F32) + self.recv[slot, rows].astype(F32)
            post(i, rows, total)


class Layer:
    def __init__(self, **kw):
        self.__dict__.update(kw)


def head_mask(layer, i, c):
    h = lax.rem(i, 3)
    half = jnp.where(h == 2, layer.third(c), lax.rem(h, 2))
    lane = lax.broadcasted_iota(jnp.int32, (1, 128), 1) // 64
    mask = jnp.where(lane == half, 1.0, 0.0).astype(BF)
    return i // 3, pl.ds(pl.multiple_of((h // 2) * 128, 128), 128), mask


def forward(layer, me, swap, bias_row, prm, done):
    L, c = layer, me.c
    units = L.q.shape[0]

    @pl.loop(0, units)
    def _(u):
        x = L.x[...]
        n = L.wq.shape[2]
        L.q[u, :, :n] = ((nn(x, L.wq[u]) + L.bias_q(u)).astype(BF) * 0.125).astype(BF)
        L.k[u, :, :n] = nn(x, L.wk[u]).astype(BF)
        L.v[u, :, :n] = (nn(x, L.wv[u]) + L.bias_v(u)).astype(BF)
        if n < 256:
            pad = jnp.zeros((x.shape[0], 256 - n), BF)
            L.q[u, :, n:] = pad
            L.k[u, :, n:] = pad
            L.v[u, :, n:] = pad
        L.o[u] = jnp.zeros(L.o.shape[1:], BF)

    @pl.loop(0, 3 * units)
    def _(i):
        u, cols, mask = head_mask(L, i, c)
        k = L.k[u, :, cols]
        v = L.v[u, :, cols] * mask
        for ch in range(4):
            rows = pl.ds(ch * 128, 128)
            scores = nt(L.q[u, rows, cols] * mask, k) + bias_row[0:1, :]
            top = jnp.max(scores, axis=-1, keepdims=True)
            expo = jnp.exp(scores - top)
            inv = 1.0 / jnp.sum(expo, axis=-1, keepdims=True)
            probs = (expo * inv).astype(BF)
            L.p[i, rows] = probs
            L.o[u, rows, cols] = L.o[u, rows, cols] + nn(probs, v).astype(BF)

    def attn_part(rows):
        n = L.wo.shape[1]
        total = nn(L.o[0, rows, :n], L.wo[0])
        for u in range(1, units):
            total = total + nn(L.o[u, rows, :n], L.wo[u])
        return total

    def attn_post(i, rows, total):
        value = L.x[rows].astype(F32) + total + prm[L.prow : L.prow + 1, :]
        xh, rstd = norm_parts(value)
        L.xh1[rows] = xh
        L.rs1[rows] = rstd
        L.a[rows] = (xh * prm[L.prow + 1 : L.prow + 2, :] + prm[L.prow + 2 : L.prow + 3, :]).astype(BF)

    swap.run(attn_part, None, attn_post)

    @pl.loop(0, 4)
    def _(j):
        pre = nn(L.a[...], L.wi[j]) + L.bias_i(j)
        sq = pre * pre
        t = jnp.tanh(0.7978845608028654 * pre * (1.0 + 0.044715 * sq))
        half = 0.5 * (1.0 + t)
        L.g[j] = (pre * half).astype(BF)
        slope = half + 0.5 * pre * (1.0 - t * t) * (0.7978845608028654 + 0.7978845608028654 * 0.134145 * sq)
        L.gp[j] = slope.astype(BF)

    def ffn_part(rows):
        total = nn(L.g[0, rows], L.wf[0])
        for j in range(1, 4):
            total = total + nn(L.g[j, rows], L.wf[j])
        return total

    def ffn_post(i, rows, total):
        value = L.a[rows].astype(F32) + total + prm[L.prow + 3 : L.prow + 4, :]
        xh, rstd = norm_parts(value)
        L.xh2[rows] = xh
        L.rs2[rows] = rstd
        done(rows, xh * prm[L.prow + 4 : L.prow + 5, :] + prm[L.prow + 5 : L.prow + 6, :])

    swap.run(ffn_part, None, ffn_post)


def backward(layer, me, swap, prm, sums, upstream, done):
    L, c = layer, me.c
    units = L.q.shape[0]
    prow = L.prow
    n_rows = L.x.shape[0]
    for i in range(6):
        sums[prow + i : prow + i + 1, :] = jnp.zeros((1, 768), F32)

    @pl.loop(0, n_rows // 128)
    def _(i):
        rows = rows_of(i, 128)
        dy = upstream(rows)
        xh = L.xh2[rows]
        sums[prow + 4 : prow + 5, :] += col_sum(dy * xh)
        sums[prow + 5 : prow + 6, :] += col_sum(dy)
        df = norm_grad(xh, L.rs2[rows], prm[prow + 4 : prow + 5, :], dy)
        low = df.astype(BF)
        sums[prow + 3 : prow + 4, :] += col_sum(low.astype(F32))
        L.df[rows] = df
        L.dr[rows] = low

    @pl.loop(0, 4)
    def _(j):
        dpre = (nt(L.dr[...], L.wf[j]) * L.gp[j].astype(F32)).astype(BF)
        L.gp[j] = dpre
        n = dpre.shape[1]
        sums[pl.ds(L.brow + j, 1), :n] = col_sum(dpre.astype(F32))

    def ffn_part(rows):
        total = nt(L.gp[0, rows], L.wi[0])
        for j in range(1, 4):
            total = total + nt(L.gp[j, rows], L.wi[j])
        return total

    def ffn_weights():
        @pl.loop(0, 4)
        def _(j):
            L.gwf[j] = tn(L.g[j], L.dr[...]).astype(BF)
            L.gwi[j] = tn(L.a[...], L.gp[j]).astype(BF)

    def ffn_post(i, rows, total):
        da = L.df[rows] + total
        xh = L.xh1[rows]
        sums[prow + 1 : prow + 2, :] += col_sum(da * xh)
        sums[prow + 2 : prow + 3, :] += col_sum(da)
        dh = norm_grad(xh, L.rs1[rows], prm[prow + 1 : prow + 2, :], da)
        low = dh.astype(BF)
        sums[prow : prow + 1, :] += col_sum(low.astype(F32))
        L.df[rows] = dh
        L.dr[rows] = low

    swap.run(ffn_part, ffn_weights, ffn_post)

    @pl.loop(0, units)
    def _(u):
        n = L.wo.shape[1]
        L.do[u, :, :n] = nt(L.dr[...], L.wo[u]).astype(BF)
        if n < 256:
            L.do[u, :, n:] = jnp.zeros((n_rows, 256 - n), BF)
        for ref in (L.dq, L.dk, L.dv):
            ref[u] = jnp.zeros(ref.shape[1:], BF)

    @pl.loop(0, 3 * units)
    def _(i):
        u, cols, mask = head_mask(L, i, c)
        k = L.k[u, :, cols] * mask
        v = L.v[u, :, cols]
        for ch in range(4):
            rows = pl.ds(ch * 128, 128)
            d_probs = nt(L.do[u, rows, cols] * mask, v)
            probs = L.p[i, rows].astype(F32)
            both = probs * d_probs
            d_scores = (both - probs * jnp.sum(both, axis=-1, keepdims=True)).astype(BF)
            L.ds[rows] = d_scores
            L.dq[u, rows, cols] = L.dq[u, rows, cols] + (nn(d_scores, k) * 0.125).astype(BF)
        L.dv[u, :, cols] = L.dv[u, :, cols] + tn(L.p[i], L.do[u, :, cols] * mask).astype(BF)
        L.dk[u, :, cols] = L.dk[u, :, cols] + tn(L.ds[...], L.q[u, :, cols] * mask).astype(BF)

    def attn_part(rows):
        n = L.wq.shape[2]
        total = None
        for u in range(units):
            for grad, weight in ((L.dq, L.wq), (L.dk, L.wk), (L.dv, L.wv)):
                term = nt(grad[u, rows, :n], weight[u])
                total = term if total is None else total + term
        return total

    def attn_weights():
        @pl.loop(0, units)
        def _(u):
            n = L.gwo.shape[1]
            L.gwo[u] = tn(L.o[u, :, :n], L.dr[...]).astype(BF)
            x = L.x[...]
            for grad, out in ((L.dq, L.gwq), (L.dk, L.gwk), (L.dv, L.gwv)):
                out[u] = tn(x, grad[u, :, :n]).astype(BF)
            sums[pl.ds(L.qrow + u, 1), :256] = col_sum(L.dq[u].astype(F32))
            sums[pl.ds(L.qrow + units + u, 1), :256] = col_sum(L.dv[u].astype(F32))

    def attn_post(i, rows, total):
        done(rows, L.df[rows] + total)

    swap.run(attn_part, attn_weights, attn_post)


def compute_kernel(*refs):
    me = Place()
    c = me.c
    (X, CT, LN, PRM, BP, WQ, WK, WV, WO, WI, WF, SQ, SK, SV, SO, SI, SF) = refs[:17]
    (Y, DX, SM, GQ, GK, GV, GO, GI, GF, GSQ, GSK, GSV, GSO, GSI, GSF) = refs[17:32]
    (
        bias_row, send, recv, ssem, rsem,
        q, k, v, o, p, xh1, rs1, a, g, gp, xh2, rs2, df, dr, do, dq, dk, dv, ds,
        wsq, wsk, wsv, wso, x2, q2, k2, v2, o2, p2, xh12, rs12, a2, g2, gp2, xh22, rs22, dx2,
    ) = refs[32:]

    barrier = pltpu.get_barrier_semaphore()
    pl.semaphore_signal(barrier, inc=1, device_id=me.core(), device_id_type=MESH)
    pl.semaphore_wait(barrier, 1)

    n_keys = X.shape[0]
    position = lax.broadcasted_iota(jnp.int32, (8, n_keys), 1).astype(F32)
    bias_row[...] = jnp.where(position < LN[0:8, 0:1], 0.0, MASKED)
    SM[...] = jnp.zeros(SM.shape, F32)
    first = pl.ds(pl.multiple_of(c * 256, 128), 128)
    for src, dst in ((SQ, wsq), (SK, wsk), (SV, wsv)):
        dst[0, :, 0:128] = src[:, first]
        dst[0, :, 128:256] = src[:, 128:256]
    wso[0, 0:128, :] = SO[first, :]
    wso[0, 128:256, :] = SO[128:256, :]
    s_bias = pl.ds(pl.multiple_of(c * 256, 128), 128)
    v_bias = pl.ds(pl.multiple_of(384 + c * 256, 128), 128)

    teacher = Layer(
        x=X, wq=WQ, wk=WK, wv=WV, wo=WO, wi=WI, wf=WF, q=q, k=k, v=v, o=o, p=p, xh1=xh1, rs1=rs1, a=a, g=g, gp=gp,
        xh2=xh2, rs2=rs2, df=df, dr=dr, do=do, dq=dq, dk=dk, dv=dv, ds=ds, prow=0, qrow=12, brow=16,
        gwq=GQ, gwk=GK, gwv=GV, gwo=GO, gwi=GI, gwf=GF,
        bias_q=lambda u: BP[2 * c + u, 0:1, 0:192],
        bias_v=lambda u: BP[2 * c + u, 3:4, 0:192],
        bias_i=lambda j: BP[j, 1:2, :],
        third=lambda c: 0,
    )
    student = Layer(
        x=x2, wq=wsq, wk=wsk, wv=wsv, wo=wso, wi=SI, wf=SF, q=q2, k=k2, v=v2, o=o2, p=p2, xh1=xh12, rs1=rs12, a=a2,
        g=g2, gp=gp2, xh2=xh22, rs2=rs22, df=df, dr=dr, do=do, dq=dq, dk=dk, dv=dv, ds=ds, prow=6, qrow=24, brow=20,
        gwq=GSQ, gwk=GSK, gwv=GSV, gwo=GSO, gwi=GSI, gwf=GSF,
        bias_q=lambda u: jnp.concatenate([PRM[12:13, s_bias], PRM[12:13, 128:256]], axis=1),
        bias_v=lambda u: jnp.concatenate([PRM[12:13, v_bias], PRM[12:13, 512:640]], axis=1),
        bias_i=lambda j: BP[j, 2:3, 0 : SI.shape[2]],
        third=lambda c: c,
    )
    swap = Swap(me, send, recv, ssem, rsem, 4)

    def to_student(rows, value):
        x2[rows] = value.astype(BF)

    def to_output(rows, value):
        Y[rows] = value.astype(BF)

    def between(rows, value):
        dx2[rows] = value

    def to_grad(rows, value):
        DX[rows] = value.astype(BF)

    forward(teacher, me, swap, bias_row, PRM, to_student)
    forward(student, me, swap, bias_row, PRM, to_output)
    backward(student, me, swap, PRM, SM, lambda rows: CT[rows].astype(F32), between)
    backward(teacher, me, swap, PRM, SM, lambda rows: dx2[rows], to_grad)


def add_up(refs):
    total = refs[0][...].astype(F32)
    for ref in refs[1:]:
        total = total + ref[...].astype(F32)
    return total


def reduce_kernel(*refs):
    me = Place()
    r, z, s, c = me.r, me.z, me.s, me.c
    names = 12
    Y, DX, SM = refs[:3]
    grads = refs[3 : 3 + names]
    YO, DO, SUMS = refs[3 + names : 6 + names]
    outs = refs[6 + names : 6 + 2 * names]
    rest = refs[6 + 2 * names :]
    R1, S1, R2, S2 = rest[:names], rest[names : 2 * names], rest[2 * names : 3 * names], rest[3 * names : 4 * names]
    (s1s, s1r, s2s, s2r, s3s, s3r, cs, cr, ys, yr, sml, sms, smr, zs3, zr3) = rest[4 * names :]
    greet(me)
    owner = z // 2 == c

    def kind(w):
        return 0 if w < 4 else (1 if w < 8 else 2)

    for w in range(names):
        quarter = grads[w].shape[1] // 4
        for k in (1, 2, 3):
            part = grads[w].at[:, rows_of(me.plane_index(k), quarter)]
            remote(part, R1[w].at[k - 1], s1s.at[w, k - 1], s1r.at[w, k - 1], me.plane(k)).start()

    @pl.when(owner)
    def _():
        for a, (src, dst) in enumerate(((Y, YO), (DX, DO))):
            pltpu.make_async_copy(src.at[rows_of(z, 128)], dst.at[z % 2], yr.at[a, z % 2]).start()
            for d in (1, 2, 3):
                remote(
                    src.at[rows_of(me.line_index(d), 128)], dst.at[z % 2], ys.at[a, d - 1], yr.at[a, z % 2], me.line(d)
                ).start()

    sml[0] = SM[...]
    for d in (1, 2, 3):
        remote(sml.at[0], sml.at[d], sms.at[d - 1], smr.at[d - 1], me.line(d)).start()
    for d in (1, 2, 3):
        remote(sml.at[0], sml.at[d], sms.at[d - 1], smr.at[d - 1], me.line(d)).wait()
    sml[4] = add_up([sml.at[i] for i in range(4)])
    for k in (1, 2, 3):
        remote(sml.at[4], sml.at[4 + k], sms.at[2 + k], smr.at[2 + k], me.plane(k)).start()
    for k in (1, 2, 3):
        remote(sml.at[4], sml.at[4 + k], sms.at[2 + k], smr.at[2 + k], me.plane(k)).wait()
    SUMS[0] = add_up([sml.at[4 + i] for i in range(4)])
    other_sums = remote(SUMS.at[0], SUMS.at[1], sms.at[6], smr.at[6], me.core())
    other_sums.start()

    for w in range(names):
        quarter = grads[w].shape[1] // 4
        own = grads[w].at[:, rows_of(r, quarter)]
        for k in (1, 2, 3):
            remote(own, R1[w].at[k - 1], s1s.at[w, k - 1], s1r.at[w, k - 1], me.plane(k)).wait()
        S1[w][...] = add_up([own] + [R1[w].at[k] for k in range(3)]).astype(BF)
        if kind(w) == 0:
            for u in range(2):
                target = 2 * c + u

                @pl.when(target != z)
                def _():
                    slot = lax.rem(target - z + 4, 4) - 1
                    remote(S1[w].at[u], R2[w].at[slot], s2s.at[w, u], s2r.at[w, slot], (r, target, s)).start()

        elif kind(w) == 1:
            for d in (1, 2, 3):
                remote(
                    S1[w].at[me.line_index(d)], R2[w].at[d - 1], s2s.at[w, d - 1], s2r.at[w, d - 1], me.line(d)
                ).start()
        else:
            sub = quarter // 4
            for d in (1, 2, 3):
                remote(
                    S1[w].at[0, rows_of(me.line_index(d), sub)],
                    R2[w].at[d - 1],
                    s2s.at[w, d - 1],
                    s2r.at[w, d - 1],
                    me.line(d),
                ).start()

    for w in range(names):
        quarter = grads[w].shape[1] // 4
        if kind(w) == 0:
            for u in range(2):

                @pl.when(2 * c + u != z)
                def _():
                    remote(S1[w].at[u], R2[w].at[0], s2s.at[w, u], s2r.at[w, 0], me.core()).wait_send()

            @pl.when(owner)
            def _():
                for d in (1, 2, 3):
                    remote(S1[w].at[0], R2[w].at[d - 1], s2s.at[w, 0], s2r.at[w, d - 1], me.core()).wait_recv()
                mine = rows_of(r, quarter)
                outs[w][mine] = add_up([S1[w].at[z % 2]] + [R2[w].at[d] for d in range(3)]).astype(BF)
                for k in (1, 2, 3):
                    remote(
                        outs[w].at[mine], outs[w].at[mine], s3s.at[w, k - 1], s3r.at[w, k - 1], me.plane(k)
                    ).start()

        elif kind(w) == 1:
            for d in (1, 2, 3):
                remote(S1[w].at[0], R2[w].at[d - 1], s2s.at[w, d - 1], s2r.at[w, d - 1], me.line(d)).wait()
            mine = rows_of(r, quarter)
            outs[w][mine] = add_up([S1[w].at[z]] + [R2[w].at[d] for d in range(3)]).astype(BF)
            for k in (1, 2, 3):
                remote(outs[w].at[mine], outs[w].at[mine], s3s.at[w, k - 1], s3r.at[w, k - 1], me.plane(k)).start()
        else:
            sub = quarter // 4
            for d in (1, 2, 3):
                remote(
                    S1[w].at[0, rows_of(0, sub)], R2[w].at[d - 1], s2s.at[w, d - 1], s2r.at[w, d - 1], me.line(d)
                ).wait()
            mine = rows_of(r * 4 + z, sub)
            outs[w][0, mine] = add_up([S1[w].at[0, rows_of(z, sub)]] + [R2[w].at[d] for d in range(3)]).astype(BF)
            for d in (1, 2, 3):
                remote(
                    outs[w].at[0, mine], outs[w].at[0, mine], zs3.at[w - 8, d - 1], zr3.at[w - 8, d - 1], me.line(d)
                ).start()

    for w in range(8, names):
        quarter = grads[w].shape[1] // 4
        sub = quarter // 4
        for d in (1, 2, 3):
            theirs = rows_of(r * 4 + me.line_index(-d), sub)
            remote(
                outs[w].at[0, theirs], outs[w].at[0, theirs], zs3.at[w - 8, d - 1], zr3.at[w - 8, d - 1], me.line(d)
            ).wait()
        mine = rows_of(r, quarter)
        for k in (1, 2, 3):
            remote(
                outs[w].at[0, mine], outs[w].at[0, mine], s3s.at[w, k - 1], s3r.at[w, k - 1], me.plane(k)
            ).start()

    for w in range(names):
        quarter = grads[w].shape[1] // 4

        def gathered(ref):
            for k in (1, 2, 3):
                theirs = rows_of(me.plane_index(k), quarter)
                remote(ref.at[theirs], ref.at[theirs], s3s.at[w, k - 1], s3r.at[w, k - 1], me.plane(k)).wait()

        if kind(w) == 0:

            @pl.when(owner)
            def _():
                gathered(outs[w])
                remote(outs[w], outs[w], cs.at[w], cr.at[w], me.core()).start()

        elif kind(w) == 1:
            gathered(outs[w])
        else:
            gathered(outs[w].at[0])
            remote(outs[w].at[0], outs[w].at[1], cs.at[w], cr.at[w], me.core()).start()
    for w in range(names):
        if kind(w) == 0:

            @pl.when(owner)
            def _():
                remote(outs[w], outs[w], cs.at[w], cr.at[w], me.core()).wait_send()

            @pl.when(jnp.logical_not(owner))
            def _():
                remote(outs[w], outs[w], cs.at[w], cr.at[w], me.core()).wait_recv()

        elif kind(w) == 2:
            remote(outs[w].at[0], outs[w].at[1], cs.at[w], cr.at[w], me.core()).wait()
    other_sums.wait()

    @pl.when(owner)
    def _():
        for a, (src, dst) in enumerate(((Y, YO), (DX, DO))):
            for d in (1, 2, 3):
                remote(src.at[rows_of(0, 128)], dst.at[0], ys.at[a, d - 1], yr.at[a, 0], me.core()).wait_send()

    for a, (src, dst) in enumerate(((Y, YO), (DX, DO))):
        for j in range(2):
            chip = 2 * c + j

            @pl.when(chip == z)
            def _():
                pltpu.make_async_copy(src.at[rows_of(0, 128)], dst.at[j], yr.at[a, j]).wait()

            @pl.when(chip != z)
            def _():
                remote(src.at[rows_of(0, 128)], dst.at[j], ys.at[a, 0], yr.at[a, j], me.core()).wait_recv()


def final_kernel(*refs):
    z = lax.axis_index("head")
    c = lax.rem(lax.axis_index("seq"), 2)
    YO, DO, SUMS = refs[:3]
    grads = refs[3:15]
    outs = refs[15:]
    outs[0][...] = YO[...].astype(F32)
    outs[1][...] = DO[...].astype(F32)

    def whole(at, w):
        outs[at][...] = grads[w][...].astype(F32)

    whole(2, 0)
    whole(4, 1)
    whole(5, 2)
    whole(7, 3)
    whole(11, 4)
    whole(13, 5)
    whole(26, 6)
    whole(28, 7)
    near = pl.ds(pl.multiple_of(c * 256, 128), 128)
    far = pl.ds(pl.multiple_of((1 - c) * 256, 128), 128)
    for at, w in ((17, 8), (19, 9), (20, 10)):
        g = grads[w]
        outs[at][:, near] = g[0, :, 0:128].astype(F32)
        outs[at][:, far] = g[1, :, 0:128].astype(F32)
        outs[at][:, 128:256] = g[0, :, 128:256].astype(F32) + g[1, :, 128:256].astype(F32)
    g = grads[11]
    outs[22][near, :] = g[0, 0:128, :].astype(F32)
    outs[22][far, :] = g[1, 0:128, :].astype(F32)
    outs[22][128:256, :] = g[0, 128:256, :].astype(F32) + g[1, 128:256, :].astype(F32)

    for i, at in enumerate((8, 9, 10, 14, 15, 16, 23, 24, 25, 29, 30, 31)):
        outs[at][...] = SUMS[0, i : i + 1, :]
    side = jnp.where(z // 2 == c, 0, 1)
    outs[3][...] = SUMS[side, pl.ds(12 + z % 2, 1), 0:192]
    outs[6][...] = SUMS[side, pl.ds(14 + z % 2, 1), 0:192]
    outs[12][...] = SUMS[0, pl.ds(16 + z, 1), 0 : outs[12].shape[1]]
    outs[27][...] = SUMS[0, pl.ds(20 + z, 1), 0 : outs[27].shape[1]]
    for at, row in ((18, 24), (21, 25)):
        outs[at][:, near] = SUMS[0, row : row + 1, 0:128]
        outs[at][:, far] = SUMS[1, row : row + 1, 0:128]
        outs[at][:, 128:256] = SUMS[0, row : row + 1, 128:256] + SUMS[1, row : row + 1, 128:256]


ANYWHERE = pl.BlockSpec(memory_space=pl.ANY)
IN_VMEM = pl.BlockSpec(memory_space=pltpu.VMEM)


def shape(*dims, kind=BF):
    return jax.ShapeDtypeStruct(dims, kind)


def body(
    tokens, lengths, cotangent,
    t_query, t_query_bias, t_key, t_value, t_value_bias, t_attn_out, t_attn_bias, t_norm1_gain, t_norm1_bias,
    t_ffn_in, t_ffn_in_bias, t_ffn_out, t_ffn_out_bias, t_norm2_gain, t_norm2_bias,
    s_query, s_query_bias, s_key, s_value, s_value_bias, s_attn_out, s_attn_bias, s_norm1_gain, s_norm1_bias,
    s_ffn_in, s_ffn_in_bias, s_ffn_out, s_ffn_out_bias, s_norm2_gain, s_norm2_bias,
):
    seq_size = lax.axis_size("seq")
    outer = seq_size // 2
    groups = [[2 * y + core for y in range(outer)] for core in range(2)]

    def widen(value, axis):
        if outer == 1:
            return value
        return lax.all_gather(value, "seq", axis=axis, tiled=True, axis_index_groups=groups)

    t_ffn_in, t_ffn_in_bias, t_ffn_out = widen(t_ffn_in, 1), widen(t_ffn_in_bias, 0), widen(t_ffn_out, 0)
    s_ffn_in, s_ffn_in_bias, s_ffn_out = widen(s_ffn_in, 1), widen(s_ffn_in_bias, 0), widen(s_ffn_out, 0)

    def wide(value, width):
        return jnp.pad(value.astype(F32), (0, width - value.shape[0]))

    n_in, n_s = t_ffn_in.shape[1], s_ffn_in.shape[1]
    pack = jnp.stack([wide(v, n_in) for v in (t_query_bias, t_ffn_in_bias, s_ffn_in_bias, t_value_bias)])
    pack = jnp.pad(pack, ((0, 4), (0, 0)))
    lens = jnp.broadcast_to(lengths.astype(F32)[:, None, None], (2, 8, 128))
    params = jnp.stack(
        [
            t_attn_bias, t_norm1_gain, t_norm1_bias, t_ffn_out_bias, t_norm2_gain, t_norm2_bias,
            s_attn_bias, s_norm1_gain, s_norm1_bias, s_ffn_out_bias, s_norm2_gain, s_norm2_bias,
            jnp.concatenate([s_query_bias, s_value_bias]),
        ]
    )
    params = jnp.pad(params, ((0, 3), (0, 0)))

    dma = pltpu.SemaphoreType.DMA
    gathered = pl.pallas_call(
        gather_kernel,
        out_shape=[
            shape(4, 128, 768), shape(4, 128, 768), shape(8, 128, kind=F32), shape(4, 8, n_in, kind=F32),
            shape(2, 768, 192), shape(2, 768, 192), shape(2, 768, 192), shape(2, 192, 768),
            shape(4, 768, n_in), shape(4, n_in, 768), shape(4, 768, n_s), shape(4, n_s, 768),
        ],
        in_specs=[ANYWHERE] * 12,
        out_specs=[ANYWHERE] * 12,
        scratch_shapes=[
            dma((9, 3)), dma((9, 3)), dma((8, 3, 3)), dma((8, 3, 3)), dma((10,)), dma((2, 2)), dma((2, 4)), dma((3, 4)), dma((3, 4)),
        ],
        compiler_params=pltpu.CompilerParams(collective_id=0, has_side_effects=True),
        name="gather",
    )(tokens, cotangent, lens, pack, t_query, t_key, t_value, t_attn_out, t_ffn_in, t_ffn_out, s_ffn_in, s_ffn_out)
    (X, CT, LN, BP, WQ, WK, WV, WO, WI, WF, SI, SF) = gathered

    n = 512
    act = lambda *dims, kind=BF: pltpu.VMEM(dims, kind)
    results = pl.pallas_call(
        compute_kernel,
        out_shape=[
            shape(n, 768), shape(n, 768), shape(32, 768, kind=F32),
            shape(2, 768, 192), shape(2, 768, 192), shape(2, 768, 192), shape(2, 192, 768),
            shape(4, 768, n_in), shape(4, n_in, 768),
            shape(1, 768, 256), shape(1, 768, 256), shape(1, 768, 256), shape(1, 256, 768),
            shape(4, 768, n_s), shape(4, n_s, 768),
        ],
        in_specs=[IN_VMEM] * 17,
        out_specs=[IN_VMEM] * 15,
        scratch_shapes=[
            act(8, n, kind=F32), act(2, n, 768), act(2, n, 768), dma((2, 4)), dma((2, 4)),
            act(2, n, 256), act(2, n, 256), act(2, n, 256), act(2, n, 256), act(6, n, n),
            act(n, 768, kind=F32), act(n, 1, kind=F32), act(n, 768), act(4, n, n_in), act(4, n, n_in),
            act(n, 768, kind=F32), act(n, 1, kind=F32), act(n, 768, kind=F32), act(n, 768),
            act(2, n, 256), act(2, n, 256), act(2, n, 256), act(2, n, 256), act(n, n),
            act(1, 768, 256), act(1, 768, 256), act(1, 768, 256), act(1, 256, 768),
            act(n, 768), act(1, n, 256), act(1, n, 256), act(1, n, 256), act(1, n, 256), act(3, n, n),
            act(n, 768, kind=F32), act(n, 1, kind=F32), act(n, 768), act(4, n, n_s), act(4, n, n_s),
            act(n, 768, kind=F32), act(n, 1, kind=F32), act(n, 768, kind=F32),
        ],
        compiler_params=pltpu.CompilerParams(collective_id=1, has_side_effects=True, vmem_limit_bytes=VMEM_LIMIT),
        name="compute",
    )(
        X.reshape(n, 768), CT.reshape(n, 768), LN, params, BP, WQ, WK, WV, WO, WI, WF,
        s_query, s_key, s_value, s_attn_out, SI, SF,
    )
    (Y, DX, SM, GQ, GK, GV, GO, GI, GF, GSQ, GSK, GSV, GSO, GSI, GSF) = results

    grads = (GQ, GK, GV, GO, GI, GF, GSI, GSF, GSQ, GSK, GSV, GSO)
    names = len(grads)

    def one(g):
        count, rows, cols = g.shape
        return rows // 4, cols, count

    r1 = [pltpu.VMEM((3, one(g)[2], one(g)[0], one(g)[1]), BF) for g in grads]
    s1 = [pltpu.VMEM((one(g)[2], one(g)[0], one(g)[1]), BF) for g in grads]
    pieces = [(one(g)[0] if w < 8 else one(g)[0] // 4, one(g)[1]) for w, g in enumerate(grads)]
    r2 = [pltpu.VMEM((3,) + p, BF) for p in pieces]
    s2 = [pltpu.VMEM(p if w < 0 else (16, 128), BF) for w, p in enumerate(pieces)]
    reduced = pl.pallas_call(
        reduce_kernel,
        out_shape=[shape(2, 128, 768), shape(2, 128, 768), shape(2, 32, 768, kind=F32)]
        + [shape(*g.shape[1:]) if w < 8 else shape(2, *g.shape[1:]) for w, g in enumerate(grads)],
        in_specs=[IN_VMEM] * (3 + names),
        out_specs=[IN_VMEM] * (3 + names),
        scratch_shapes=r1 + s1 + r2 + s2
        + [
            dma((names, 3)), dma((names, 3)), dma((names, 3)), dma((names, 3)), dma((names, 3)), dma((names, 3)),
            dma((names,)), dma((names,)), dma((2, 3)), dma((2, 2)),
            pltpu.VMEM((8, 32, 768), F32), dma((7,)), dma((7,)), dma((4, 3)), dma((4, 3)),
        ],
        compiler_params=pltpu.CompilerParams(collective_id=2, has_side_effects=True, vmem_limit_bytes=VMEM_LIMIT),
        name="reduce",
    )(Y, DX, SM, *grads)
    reduced = list(reduced)

    if outer > 1:
        reduced[2] = lax.psum(reduced[2].reshape(2, 32, 768), "seq", axis_index_groups=groups)
        reduced[3:] = [
            lax.psum(g.astype(F32), "seq", axis_index_groups=groups).astype(BF) for g in reduced[3:]
        ]

    f = functools.partial(shape, kind=F32)
    final_shapes = [
        f(2, 128, 768), f(2, 128, 768),
        f(768, 192), f(1, 192), f(768, 192), f(768, 192), f(1, 192), f(192, 768),
        f(1, 768), f(1, 768), f(1, 768), f(768, n_in), f(1, n_in), f(n_in, 768), f(1, 768), f(1, 768), f(1, 768),
        f(768, 384), f(1, 384), f(768, 384), f(768, 384), f(1, 384), f(384, 768),
        f(1, 768), f(1, 768), f(1, 768), f(768, n_s), f(1, n_s), f(n_s, 768), f(1, 768), f(1, 768), f(1, 768),
    ]
    outs = list(
        pl.pallas_call(
            final_kernel,
            out_shape=final_shapes,
            in_specs=[IN_VMEM] * (3 + names),
            out_specs=[IN_VMEM] * len(final_shapes),
            compiler_params=pltpu.CompilerParams(vmem_limit_bytes=VMEM_LIMIT),
            name="final",
        )(*reduced)
    )
    for i, o in enumerate(outs):
        if o.shape[0] == 1:
            outs[i] = o.reshape(-1)
    if outer > 1:
        y = lax.axis_index("seq") // 2
        for i, axis in ((11, 1), (12, 0), (13, 0), (26, 1), (27, 0), (28, 0)):
            width = outs[i].shape[axis] // outer
            outs[i] = lax.dynamic_slice_in_dim(outs[i], y * width, width, axis)
    return tuple(outs)


def solution(mesh):
    seqs = P(("row", "seq"), "head", None)
    col, line, row = P(None, "head"), P("head"), P("head", None)
    fcol, fline, frow = P(None, ("head", "seq")), P(("head", "seq")), P(("head", "seq"), None)
    rep = P()
    teacher = (col, line, col, col, line, row, rep, rep, rep, fcol, fline, frow, rep, rep, rep)
    student = (rep,) * 9 + (fcol, fline, frow, rep, rep, rep)
    return jax.shard_map(
        body,
        mesh=mesh,
        in_specs=(seqs, P(("row", "seq")), seqs) + teacher + student,
        out_specs=(seqs, seqs) + teacher + student,
        check_vma=False,
    )
```

```python
import functools

import jax
import jax.numpy as jnp
from jax import lax
from jax.experimental import pallas as pl
from jax.experimental.pallas import tpu as pltpu
from jax.sharding import PartitionSpec as P

MESH = pl.DeviceIdType.MESH
F32 = jnp.float32
BF = jnp.bfloat16
EPS = 1e-5
MASKED = -1000000000.0
VMEM_LIMIT = 63 << 20


class Place:
    def __init__(self):
        self.r = lax.axis_index("row")
        self.z = lax.axis_index("head")
        self.s = lax.axis_index("seq")
        self.c = lax.rem(self.s, 2)

    def core(self):
        return (self.r, self.z, self.s + 1 - 2 * self.c)

    def line_index(self, step):
        return lax.rem(self.z + step + 4, 4)

    def line(self, step):
        return (self.r, self.line_index(step), self.s)

    def plane_index(self, k):
        if k == 1:
            return self.r + 1 - 2 * lax.rem(self.r, 2)
        if k == 2:
            return lax.rem(self.r + 2, 4)
        return 3 - self.r

    def plane(self, k):
        return (self.plane_index(k), self.z, self.s)


def greet(me):
    barrier = pltpu.get_barrier_semaphore()
    others = [me.core()] + [me.line(i) for i in (1, 2, 3)] + [me.plane(k) for k in (1, 2, 3)]
    for other in others:
        pl.semaphore_signal(barrier, inc=1, device_id=other, device_id_type=MESH)
    pl.semaphore_wait(barrier, len(others))


def remote(src, dst, send_sem, recv_sem, device):
    return pltpu.make_async_remote_copy(
        src_ref=src, dst_ref=dst, send_sem=send_sem, recv_sem=recv_sem, device_id=device, device_id_type=MESH
    )


def rows_of(index, count, unit=16):
    return pl.ds(pl.multiple_of(index * count, unit), count)


class Gather:
    def __init__(self, me, shards, sems):
        self.me, self.shards = me, shards
        self.zs, self.zr, self.ps, self.pr, self.fs, self.fr, self.ls = sems

    def only(self, w, cond):
        return (lambda f: pl.when(cond)(f)) if self.shards[w][2] == 2 else (lambda f: f())

    def slot(self, w, index):
        return index % 2 if self.shards[w][2] == 2 else index

    def quarter(self, w, r):
        return rows_of(r, self.shards[w][0].shape[0] // 4)

    def part(self, w, frm, r, half=None):
        dst = self.shards[w][1]
        count, cols = dst.shape[1] // 4, dst.shape[2]
        slot = self.slot(w, frm)
        if half is None:
            return dst.at[slot, rows_of(r, count)]
        if cols == 768:
            return dst.at[slot, rows_of(r, count), pl.ds(half * 384, 384)]
        return dst.at[slot, rows_of(2 * r + half, count // 2)]

    def send(self, ws):
        me = self.me
        for w in ws:
            src, dst, count = self.shards[w]

            @self.only(w, me.z // 2 == me.c)
            def _():
                for d in (2, 1, 3):
                    self.line_copy(w, d).start()
                pltpu.make_async_copy(src, dst.at[self.slot(w, me.z)], self.ls.at[w]).start()

    def line_copy(self, w, d):
        me = self.me
        return remote(
            self.shards[w][0].at[self.quarter(w, me.r)],
            self.part(w, me.z, me.r),
            self.zs.at[w, d - 1],
            self.zr.at[w, d - 1],
            me.line(d),
        )

    def plane_copy(self, w, d, k):
        me = self.me
        ref = self.part(w, me.line_index(-d), me.r)
        return remote(ref, ref, self.ps.at[w, d - 1, k - 1], self.pr.at[w, d - 1, k - 1], me.plane(k))

    def on_copy(self, w, d, k):
        me = self.me
        ref = self.part(w, me.line_index(-d), me.plane_index(3 - k), k - 1)
        return remote(ref, ref, self.fs.at[w, d - 1, k - 1], self.fr.at[w, d - 1, k - 1], me.plane(k))

    def each(self, ws, step):
        for w in ws:
            for d in (1, 2, 3):

                @self.only(w, self.me.line_index(-d) // 2 == self.me.c)
                def _():
                    step(w, d)

    def to_plane(self, ws):
        def step(w, d):
            self.line_copy(w, d).wait_recv()
            self.plane_copy(w, d, 1).start()
            self.plane_copy(w, d, 2).start()

        self.each(ws, step)

    def onward(self, ws):
        def step(w, d):
            for k in (1, 2):
                self.plane_copy(w, d, k).wait_recv()
                self.on_copy(w, d, 3 - k).start()

        self.each(ws, step)

    def ready(self, ws):
        def step(w, d):
            for k in (1, 2):
                self.on_copy(w, d, k).wait_recv()

        self.each(ws, step)
        for w in ws:
            src, dst, count = self.shards[w]

            @self.only(w, self.me.z // 2 == self.me.c)
            def _():
                pltpu.make_async_copy(src, dst.at[0], self.ls.at[w]).wait()

    def drain(self, ws):
        def step(w, d):
            for k in (1, 2):
                self.plane_copy(w, d, k).wait_send()
                self.on_copy(w, d, k).wait_send()

        self.each(ws, step)
        for w in ws:

            @self.only(w, self.me.z // 2 == self.me.c)
            def _():
                for d in (1, 2, 3):
                    self.line_copy(w, d).wait_send()


HALVES, LINE, SPREAD = 0, 1, 2


class Reduce:
    def __init__(self, me, grads, outs, bufs, sems):
        self.me, self.grads, self.outs = me, grads, outs
        self.RA, self.RB, self.RC, self.RD, self.RZ, self.SUM = bufs
        (self.as_, self.ar, self.bs, self.br, self.zs, self.zr, self.gs, self.gr, self.fs, self.fr, self.ls,
         self.cs, self.cr, self.ns, self.nr) = sems
        self.mx, self.my = lax.rem(me.r, 2), me.r // 2
        self.owner = me.z // 2 == me.c

    def kind(self, w):
        return {4: 1, 2: 0, 1: 2}[self.grads[w].shape[0]]

    def quarter(self, w):
        return self.grads[w].shape[1] // 4

    def piece(self, w, t, half):
        g = self.grads[w]
        q, cols = self.quarter(w), g.shape[2]
        if cols == 384:
            return g.at[:, rows_of(2 * t + half, q // 2)]
        return g.at[:, rows_of(t, q), pl.ds(half * (cols // 2), cols // 2)]

    def first_copy(self, w, half, other):
        if half == 0:
            t, k, land = 2 * other + 1 - self.mx, 1, self.RA
        else:
            t, k, land = 2 * (1 - self.my) + other, 2, self.RB
        i = 2 * half + other
        return remote(
            self.piece(w, t, half), land[w].at[other], self.as_.at[w, i], self.ar.at[w, i], self.me.plane(k)
        )

    def start(self, ws):
        for w in ws:
            for other in (0, 1):
                for half in (0, 1):
                    self.first_copy(w, half, other).start()

    def kept(self, w, half, other):
        t = 2 * other + self.mx if half == 0 else 2 * self.my + other
        return self.piece(w, t, half)

    def second_copy(self, w, half):
        if half == 0:
            return remote(
                self.piece(w, 2 * (1 - self.my) + self.mx, 0), self.RC[w], self.bs.at[w, 0], self.br.at[w, 0], self.me.plane(2)
            )
        return remote(
            self.piece(w, 2 * self.my + 1 - self.mx, 1), self.RD[w], self.bs.at[w, 1], self.br.at[w, 1], self.me.plane(1)
        )

    def add_into(self, target, *more):
        total = target[...].astype(F32)
        for ref in more:
            total = total + ref[...].astype(F32)
        target[...] = total.astype(BF)

    def second(self, ws):
        for w in ws:
            for other in (0, 1):
                for half in (0, 1):
                    self.first_copy(w, half, other).wait()
            for half, land in ((0, self.RA), (1, self.RB)):

                @pl.loop(0, 2)
                def _(other):
                    self.add_into(self.kept(w, half, other), land[w].at[other])

                self.second_copy(w, half).start()

    def along(self, ws):
        me = self.me
        for w in ws:
            for half, land in ((0, self.RC), (1, self.RD)):
                self.second_copy(w, half).wait()
                self.add_into(self.piece(w, me.r, half), land[w])
            if self.kind(w) == 0:
                for u in range(2):

                    @pl.when(2 * me.c + u != me.z)
                    def _():
                        self.unit_copy(w, u).start()

            else:
                for d in (1, 2, 3):
                    self.line_copy(w, d).start()

    def unit_copy(self, w, u):
        me = self.me
        target = 2 * me.c + u
        slot = lax.rem(target - me.z + 3, 4)
        slot = jnp.minimum(slot, 2)
        return remote(
            self.grads[w].at[u, rows_of(me.r, self.quarter(w))],
            self.RZ[w].at[slot],
            self.zs.at[w, u],
            self.zr.at[w, slot],
            (me.r, target, me.s),
        )

    def line_copy(self, w, d):
        me = self.me
        q = self.quarter(w)
        if self.kind(w) == 1:
            src = self.grads[w].at[me.line_index(d), rows_of(me.r, q)]
        else:
            src = self.grads[w].at[0, rows_of(me.r * 4 + me.line_index(d), q // 4)]
        return remote(src, self.RZ[w].at[d - 1], self.zs.at[w, d - 1], self.zr.at[w, d - 1], me.line(d))

    def near_copy(self, w, d):
        mine = self.SUM[w].at[rows_of(self.me.z, self.quarter(w) // 4)]
        return remote(mine, mine, self.ns.at[w - 8, d - 1], self.nr.at[w - 8, d - 1], self.me.line(d))

    def out(self, w):
        return self.outs[w].at[0] if self.kind(w) == 2 else self.outs[w]

    def out_part(self, w, t, half=None):
        out, q = self.out(w), self.quarter(w)
        cols = out.shape[1]
        if half is None:
            return out.at[rows_of(t, q)]
        if cols == 384:
            return out.at[rows_of(2 * t + half, q // 2)]
        return out.at[rows_of(t, q), pl.ds(half * (cols // 2), cols // 2)]

    def plane_copy(self, w, k):
        me = self.me
        return remote(self.SUM[w], self.out_part(w, me.r), self.gs.at[w, k - 1], self.gr.at[w, k - 1], me.plane(k))

    def on_copy(self, w, k):
        ref = self.out_part(w, self.me.plane_index(3 - k), k - 1)
        return remote(ref, ref, self.fs.at[w, k - 1], self.fr.at[w, k - 1], self.me.plane(k))

    def own_copy(self, w):
        return pltpu.make_async_copy(self.SUM[w], self.out_part(w, self.me.r), self.ls.at[w])

    def core_copy(self, w):
        if self.kind(w) == 2:
            return remote(self.outs[w].at[0], self.outs[w].at[1], self.cs.at[w], self.cr.at[w], self.me.core())
        return remote(self.outs[w], self.outs[w], self.cs.at[w], self.cr.at[w], self.me.core())

    def only(self, w):
        return (lambda f: pl.when(self.owner)(f)) if self.kind(w) == 0 else (lambda f: f())

    def spread_start(self, w):
        self.own_copy(w).start()
        self.plane_copy(w, 1).start()
        self.plane_copy(w, 2).start()

    def spread(self, ws):
        me = self.me
        for w in ws:
            q = self.quarter(w)
            if self.kind(w) == 0:
                for u in range(2):

                    @pl.when(2 * me.c + u != me.z)
                    def _():
                        self.unit_copy(w, u).wait_send()

                @pl.when(self.owner)
                def _():
                    for d in (1, 2, 3):
                        remote(self.RZ[w].at[0], self.RZ[w].at[d - 1], self.zs.at[w, 0], self.zr.at[w, d - 1], me.core()).wait_recv()
                    own = self.grads[w].at[me.z % 2, rows_of(me.r, q)]
                    self.SUM[w][...] = add_up([own] + [self.RZ[w].at[d] for d in range(3)]).astype(BF)
                    self.spread_start(w)

                continue
            for d in (1, 2, 3):
                self.line_copy(w, d).wait()
            if self.kind(w) == 1:
                own = self.grads[w].at[me.z, rows_of(me.r, q)]
                self.SUM[w][...] = add_up([own] + [self.RZ[w].at[d] for d in range(3)]).astype(BF)
                self.spread_start(w)
            else:
                own = self.grads[w].at[0, rows_of(me.r * 4 + me.z, q // 4)]
                total = add_up([own] + [self.RZ[w].at[d] for d in range(3)]).astype(BF)
                self.SUM[w][rows_of(me.z, q // 4)] = total
                for d in (1, 2, 3):
                    self.near_copy(w, d).start()

    def spread_near(self, ws):
        for w in ws:
            for d in (1, 2, 3):
                self.near_copy(w, d).wait()
            self.spread_start(w)

    def onward(self, ws):
        for w in ws:

            @self.only(w)
            def _():
                for k in (1, 2):
                    self.plane_copy(w, k).wait()
                    self.on_copy(w, 3 - k).start()

    def finish(self, ws):
        for w in ws:

            @self.only(w)
            def _():
                self.own_copy(w).wait()
                for k in (1, 2):
                    self.on_copy(w, k).wait()
                if self.kind(w) != 1:
                    self.core_copy(w).start()

    def end(self, ws):
        for w in ws:
            if self.kind(w) == 0:

                @pl.when(self.owner)
                def _():
                    self.core_copy(w).wait_send()

                @pl.when(jnp.logical_not(self.owner))
                def _():
                    self.core_copy(w).wait_recv()

            elif self.kind(w) == 2:
                self.core_copy(w).wait()


def add_up(refs):
    total = refs[0][...].astype(F32)
    for ref in refs[1:]:
        total = total + ref[...].astype(F32)
    return total


def nn(a, b):
    return lax.dot_general(a, b, (((1,), (0,)), ((), ())), preferred_element_type=F32)


def nt(a, b):
    return lax.dot_general(a, b, (((1,), (1,)), ((), ())), preferred_element_type=F32)


def tn(a, b):
    return lax.dot_general(a, b, (((0,), (0,)), ((), ())), preferred_element_type=F32)


def norm_parts(value):
    center = value - jnp.mean(value, axis=-1, keepdims=True)
    spread = jnp.mean(center * center, axis=-1, keepdims=True)
    rstd = lax.rsqrt(spread + EPS)
    return center * rstd, rstd


def norm_grad(xh, rstd, gain, dy):
    scaled = dy * gain
    mean_one = jnp.mean(scaled, axis=-1, keepdims=True)
    mean_two = jnp.mean(scaled * xh, axis=-1, keepdims=True)
    return (scaled - mean_one - xh * mean_two) * rstd


def col_sum(value):
    return jnp.sum(value, axis=0, keepdims=True)


class Swap:
    def __init__(self, me, send, recv, ssem, rsem, chunks):
        self.me, self.send, self.recv, self.ssem, self.rsem = me, send, recv, ssem, rsem
        self.rows = send.shape[1] // chunks
        self.chunks = chunks
        self.turn = 0

    def copy(self, slot, i):
        rows = rows_of(i, self.rows)
        return remote(
            self.send.at[slot, rows],
            self.recv.at[slot, rows],
            self.ssem.at[slot, i],
            self.rsem.at[slot, i],
            self.me.core(),
        )

    def run(self, part, between, post):
        slot = self.turn % 2
        self.turn += 1

        @pl.loop(0, self.chunks)
        def _(i):
            rows = rows_of(i, self.rows)
            self.send[slot, rows] = part(rows).astype(BF)
            self.copy(slot, i).start()

        if between is not None:
            between()

        @pl.loop(0, self.chunks)
        def _(i):
            rows = rows_of(i, self.rows)
            self.copy(slot, i).wait()
            total = self.send[slot, rows].astype(F32) + self.recv[slot, rows].astype(F32)
            post(i, rows, total)


class Layer:
    def __init__(self, **kw):
        self.__dict__.update(kw)


def head_mask(layer, i, c):
    h = lax.rem(i, 3)
    half = jnp.where(h == 2, layer.third(c), lax.rem(h, 2))
    lane = lax.broadcasted_iota(jnp.int32, (1, 128), 1) // 64
    mask = jnp.where(lane == half, 1.0, 0.0).astype(BF)
    return i // 3, pl.ds(pl.multiple_of((h // 2) * 128, 128), 128), mask


def forward(layer, me, swap, bias_row, prm, hook, done):
    L, c = layer, me.c
    units = L.q.shape[0]

    hook("qkv")
    project = nt if L.flip_attn else nn

    @pl.loop(0, units)
    def _(u):
        x = L.x[...]
        n = L.width
        L.q[u, :, :n] = ((project(x, L.wq[u]) + L.bias_q(u)).astype(BF) * 0.125).astype(BF)
        L.k[u, :, :n] = project(x, L.wk[u]).astype(BF)
        L.v[u, :, :n] = (project(x, L.wv[u]) + L.bias_v(u)).astype(BF)
        if n < 256:
            pad = jnp.zeros((x.shape[0], 256 - n), BF)
            L.q[u, :, n:] = pad
            L.k[u, :, n:] = pad
            L.v[u, :, n:] = pad
        L.o[u] = jnp.zeros(L.o.shape[1:], BF)

    hook("heads")

    def heads(lo, hi):
        @pl.loop(lo, hi)
        def _(i):
            u, cols, mask = head_mask(L, i, c)
            k = L.k[u, :, cols]
            v = L.v[u, :, cols] * mask
            for ch in range(4):
                rows = pl.ds(ch * 128, 128)
                scores = nt(L.q[u, rows, cols] * mask, k) + bias_row[0:1, :]
                top = jnp.max(scores, axis=-1, keepdims=True)
                expo = jnp.exp(scores - top)
                inv = 1.0 / jnp.sum(expo, axis=-1, keepdims=True)
                probs = (expo * inv).astype(BF)
                L.p[i, rows] = probs
                L.o[u, rows, cols] = L.o[u, rows, cols] + nn(probs, v).astype(BF)

    heads(0, 3)
    if units == 2:
        hook("middle")
        heads(3, 6)
    hook("attn")

    def attn_part(rows):
        n = L.width
        total = nn(L.o[0, rows, :n], L.wo[0])
        for u in range(1, units):
            total = total + nn(L.o[u, rows, :n], L.wo[u])
        return total

    def attn_post(i, rows, total):
        value = L.x[rows].astype(F32) + total + prm[L.prow : L.prow + 1, :]
        xh, rstd = norm_parts(value)
        L.xh1[rows] = xh
        L.rs1[rows] = rstd
        L.a[rows] = (xh * prm[L.prow + 1 : L.prow + 2, :] + prm[L.prow + 2 : L.prow + 3, :]).astype(BF)

    swap.run(attn_part, None, attn_post)
    hook("ffn_in")
    enter = nt if L.flip_in else nn

    @pl.loop(0, 4)
    def _(j):
        pre = enter(L.a[...], L.wi[j]) + L.bias_i(j)
        sq = pre * pre
        t = jnp.tanh(0.7978845608028654 * pre * (1.0 + 0.044715 * sq))
        half = 0.5 * (1.0 + t)
        L.g[j] = (pre * half).astype(BF)
        slope = half + 0.5 * pre * (1.0 - t * t) * (0.7978845608028654 + 0.7978845608028654 * 0.134145 * sq)
        L.gp[j] = slope.astype(BF)

    hook("ffn_out")

    def ffn_part(rows):
        total = nn(L.g[0, rows], L.wf[0])
        for j in range(1, 4):
            total = total + nn(L.g[j, rows], L.wf[j])
        return total

    def ffn_post(i, rows, total):
        value = L.a[rows].astype(F32) + total + prm[L.prow + 3 : L.prow + 4, :]
        xh, rstd = norm_parts(value)
        L.xh2[rows] = xh
        L.rs2[rows] = rstd
        done(rows, xh * prm[L.prow + 4 : L.prow + 5, :] + prm[L.prow + 5 : L.prow + 6, :])

    swap.run(ffn_part, None, ffn_post)


def backward(layer, me, swap, prm, sums, upstream, hook, done):
    L, c = layer, me.c
    units = L.q.shape[0]
    prow = L.prow
    n_rows = L.x.shape[0]
    for i in range(6):
        sums[prow + i : prow + i + 1, :] = jnp.zeros((1, 768), F32)

    @pl.loop(0, n_rows // 128)
    def _(i):
        rows = rows_of(i, 128)
        dy = upstream(rows)
        xh = L.xh2[rows]
        sums[prow + 4 : prow + 5, :] += col_sum(dy * xh)
        sums[prow + 5 : prow + 6, :] += col_sum(dy)
        df = norm_grad(xh, L.rs2[rows], prm[prow + 4 : prow + 5, :], dy)
        low = df.astype(BF)
        sums[prow + 3 : prow + 4, :] += col_sum(low.astype(F32))
        L.df[rows] = df
        L.dr[rows] = low

    @pl.loop(0, 4)
    def _(j):
        dpre = (nt(L.dr[...], L.wf[j]) * L.gp[j].astype(F32)).astype(BF)
        L.gp[j] = dpre
        n = dpre.shape[1]
        sums[pl.ds(L.brow + j, 1), :n] = col_sum(dpre.astype(F32))

    leave = nn if L.flip_in else nt

    def ffn_part(rows):
        total = leave(L.gp[0, rows], L.wi[0])
        for j in range(1, 4):
            total = total + leave(L.gp[j, rows], L.wi[j])
        return total

    def ffn_weights():
        @pl.loop(0, 4)
        def _(j):
            L.wf[j] = tn(L.g[j], L.dr[...]).astype(BF)
            if L.flip_in:
                L.wi[j] = tn(L.gp[j], L.a[...]).astype(BF)
            else:
                L.wi[j] = tn(L.a[...], L.gp[j]).astype(BF)

        hook("ffn_grads")

    def ffn_post(i, rows, total):
        da = L.df[rows] + total
        xh = L.xh1[rows]
        sums[prow + 1 : prow + 2, :] += col_sum(da * xh)
        sums[prow + 2 : prow + 3, :] += col_sum(da)
        dh = norm_grad(xh, L.rs1[rows], prm[prow + 1 : prow + 2, :], da)
        low = dh.astype(BF)
        sums[prow : prow + 1, :] += col_sum(low.astype(F32))
        L.df[rows] = dh
        L.dr[rows] = low

    swap.run(ffn_part, ffn_weights, ffn_post)
    hook("attn")

    @pl.loop(0, units)
    def _(u):
        n = L.width
        L.do[u, :, :n] = nt(L.dr[...], L.wo[u]).astype(BF)
        if n < 256:
            L.do[u, :, n:] = jnp.zeros((n_rows, 256 - n), BF)
        for ref in (L.dq, L.dk, L.dv):
            ref[u] = jnp.zeros(ref.shape[1:], BF)

    @pl.loop(0, 3 * units)
    def _(i):
        u, cols, mask = head_mask(L, i, c)
        k = L.k[u, :, cols] * mask
        v = L.v[u, :, cols]
        for ch in range(4):
            rows = pl.ds(ch * 128, 128)
            d_probs = nt(L.do[u, rows, cols] * mask, v)
            probs = L.p[i, rows].astype(F32)
            both = probs * d_probs
            d_scores = (both - probs * jnp.sum(both, axis=-1, keepdims=True)).astype(BF)
            L.ds[rows] = d_scores
            L.dq[u, rows, cols] = L.dq[u, rows, cols] + (nn(d_scores, k) * 0.125).astype(BF)
        L.dv[u, :, cols] = L.dv[u, :, cols] + tn(L.p[i], L.do[u, :, cols] * mask).astype(BF)
        L.dk[u, :, cols] = L.dk[u, :, cols] + tn(L.ds[...], L.q[u, :, cols] * mask).astype(BF)

    hook("heads_done")
    back = nn if L.flip_attn else nt

    def attn_part(rows):
        n = L.width
        total = None
        for u in range(units):
            for grad, weight in ((L.dq, L.wq), (L.dk, L.wk), (L.dv, L.wv)):
                term = back(grad[u, rows, :n], weight[u])
                total = term if total is None else total + term
        return total

    def attn_weights():
        @pl.loop(0, units)
        def _(u):
            n = L.width
            L.wo[u] = tn(L.o[u, :, :n], L.dr[...]).astype(BF)
            x = L.x[...]
            for grad, out in ((L.dq, L.wq), (L.dk, L.wk), (L.dv, L.wv)):
                out[u] = (tn(grad[u, :, :n], x) if L.flip_attn else tn(x, grad[u, :, :n])).astype(BF)
            sums[pl.ds(L.qrow + u, 1), :256] = col_sum(L.dq[u].astype(F32))
            sums[pl.ds(L.qrow + units + u, 1), :256] = col_sum(L.dv[u].astype(F32))

        hook("attn_grads")

    def attn_post(i, rows, total):
        done(rows, L.df[rows] + total)

    swap.run(attn_part, attn_weights, attn_post)


class Sequences:
    def __init__(self, me, pairs, sems):
        self.me, self.pairs = me, pairs
        self.xs, self.xr, self.fs, self.fr = sems
        self.owner = me.z // 2 == me.c

    def send(self, a):
        me = self.me
        src, dst = self.pairs[a]
        for j in range(2):
            target = 2 * me.c + j

            @pl.when(target != me.z)
            def _():
                remote(src.at[j], dst.at[rows_of(me.z, 128)], self.xs.at[a, j], self.xr.at[a, me.z], (me.r, target, me.s)).start()

            @pl.when(target == me.z)
            def _():
                pltpu.make_async_copy(src.at[j], dst.at[rows_of(me.z, 128)], self.xr.at[a, me.z]).start()

    def core_copy(self, a, frm, i):
        dst = self.pairs[a][1].at[rows_of(frm, 128)]
        return remote(dst, dst, self.fs.at[a, i], self.fr.at[a, frm], self.me.core())

    def take(self, a):
        me = self.me
        src, dst = self.pairs[a]

        @pl.when(self.owner)
        def _():
            pltpu.make_async_copy(src.at[0], dst.at[rows_of(me.z, 128)], self.xr.at[a, me.z]).wait()
            self.core_copy(a, me.z, 0).start()
            for d in (1, 2, 3):
                frm = me.line_index(-d)
                remote(src.at[0], dst.at[rows_of(frm, 128)], self.xs.at[a, 0], self.xr.at[a, frm], me.core()).wait_recv()
                self.core_copy(a, frm, d).start()

        @pl.when(jnp.logical_not(self.owner))
        def _():
            for i in range(4):
                self.core_copy(a, i, i).wait_recv()

    def drain(self, a):
        me = self.me
        src, dst = self.pairs[a]
        for j in range(2):

            @pl.when(2 * me.c + j != me.z)
            def _():
                remote(src.at[j], dst.at[rows_of(me.z, 128)], self.xs.at[a, j], self.xr.at[a, me.z], me.core()).wait_send()

        @pl.when(self.owner)
        def _():
            for i in range(4):
                self.core_copy(a, i, i).wait_send()


class Home:
    def __init__(self, me, pairs, sems):
        self.me, self.pairs = me, pairs
        self.ys, self.yr = sems
        self.owner = me.z // 2 == me.c

    def send(self, a):
        me = self.me
        src, dst = self.pairs[a]

        @pl.when(self.owner)
        def _():
            pltpu.make_async_copy(src.at[rows_of(me.z, 128)], dst.at[me.z % 2], self.yr.at[a, me.z % 2]).start()
            for d in (1, 2, 3):
                remote(
                    src.at[rows_of(me.line_index(d), 128)],
                    dst.at[me.z % 2],
                    self.ys.at[a, d - 1],
                    self.yr.at[a, me.z % 2],
                    me.line(d),
                ).start()

    def drain(self, a):
        me = self.me
        src, dst = self.pairs[a]

        @pl.when(self.owner)
        def _():
            for d in (1, 2, 3):
                remote(src.at[rows_of(0, 128)], dst.at[0], self.ys.at[a, d - 1], self.yr.at[a, 0], me.core()).wait_send()

        for j in range(2):
            chip = 2 * me.c + j

            @pl.when(chip == me.z)
            def _():
                pltpu.make_async_copy(src.at[rows_of(0, 128)], dst.at[j], self.yr.at[a, j]).wait()

            @pl.when(chip != me.z)
            def _():
                remote(src.at[rows_of(0, 128)], dst.at[j], self.ys.at[a, 0], self.yr.at[a, j], me.core()).wait_recv()


def row(ref):
    return ref[...].astype(F32).reshape(1, ref.shape[0])


def main_kernel(*refs):
    me = Place()
    z, c = me.z, me.c
    lens = refs[0]
    (tok, cot, tq, tk, tv, to, ti, tf, si, sf, SQ, SK, SV, SO) = refs[1:15]
    vectors = refs[15:27]
    sqb, svb, tqb, tvb, tib, sib = refs[27:33]
    (YO, DO, SUMS) = refs[33:36]
    outs = refs[36:48]
    rest = list(refs[48:])

    def take(count):
        head, rest[:] = rest[:count], rest[count:]
        return head

    WQ, WK, WV, WO, WI, WF, SI, SF, wsq, wsk, wsv, wso = weights = take(12)
    X, CT, LN, PACK, BP, PRM, SM, sml = take(8)
    bias_row, send, recv, ssem, rsem = take(5)
    q, k, v, o, p, xh1, rs1, a, g, gp, xh2, rs2, df, dr, do, dq, dk, dv, ds = take(19)
    x2, q2, k2, v2, o2, p2, xh12, rs12, a2, g2, gp2, xh22, rs22, dx2, Y, DX = take(16)
    bufs = [take(12) for _ in range(6)]
    gather_sems = take(7)
    reduce_sems = take(15)
    seq_sems, home_sems = take(4), take(2)
    pks, pkr, lcs, lcr, sls, sms, smr = take(7)

    LN[0] = jnp.full(LN.shape[1:], lens[z % 2].astype(F32))
    PACK[...] = jnp.zeros(PACK.shape, F32)
    PACK[0:1, 0:192] = row(tqb)
    PACK[1:2, :] = row(tib)
    PACK[2:3, 0 : sib.shape[0]] = row(sib)
    PACK[3:4, 0:192] = row(tvb)
    greet(me)
    owner = z // 2 == c

    sequences = Sequences(me, ((tok, X), (cot, CT)), seq_sems)
    home = Home(me, ((Y, YO), (DX, DO)), home_sems)
    gather = Gather(
        me,
        ((tq, WQ, 2), (tk, WK, 2), (tv, WV, 2), (to, WO, 2), (ti, WI, 4), (tf, WF, 4), (si, SI, 4), (sf, SF, 4)),
        gather_sems,
    )
    G0, G1, G2, G3 = (0, 1, 2), (3, 4), (5,), (6, 7)

    sequences.send(0)
    pack_copies = [remote(PACK, BP.at[z], pks.at[d - 1], pkr.at[d - 1], me.line(d)) for d in (1, 2, 3)]
    for copy in pack_copies:
        copy.start()
    gather.send(G0)
    gather.send(G1)
    lens_copy = remote(LN.at[0], LN.at[1], lcs.at[0], lcr.at[0], me.core())

    @pl.when(owner)
    def _():
        lens_copy.start()

    first = pl.ds(pl.multiple_of(c * 256, 128), 128)
    local = []
    for i, (src, dst) in enumerate(((SQ, wsq), (SK, wsk), (SV, wsv))):
        local.append((src.at[:, first], dst.at[0, :, pl.ds(0, 128)]))
        local.append((src.at[:, pl.ds(128, 128)], dst.at[0, :, pl.ds(128, 128)]))
    local.append((SO.at[first], wso.at[0, pl.ds(0, 128)]))
    local.append((SO.at[pl.ds(128, 128)], wso.at[0, pl.ds(128, 128)]))
    local.append((PACK, BP.at[z]))
    local = [pltpu.make_async_copy(src, dst, sls.at[i]) for i, (src, dst) in enumerate(local)]
    for copy in local:
        copy.start()
    for i, ref in enumerate(vectors):
        PRM[i : i + 1, :] = row(ref)
    PRM[12:13, 0:384] = row(sqb)
    PRM[12:13, 384:768] = row(svb)
    SM[...] = jnp.zeros(SM.shape, F32)

    @pl.when(owner)
    def _():
        lens_copy.wait_send()

    @pl.when(jnp.logical_not(owner))
    def _():
        lens_copy.wait_recv()

    n_keys = X.shape[0]
    position = lax.broadcasted_iota(jnp.int32, (8, n_keys), 1).astype(F32)
    length = jnp.where(owner, LN[0], LN[1])
    bias_row[...] = jnp.where(position < length[:, 0:1], 0.0, MASKED)
    s_bias = pl.ds(pl.multiple_of(c * 256, 128), 128)
    v_bias = pl.ds(pl.multiple_of(384 + c * 256, 128), 128)

    teacher = Layer(
        x=X, wq=WQ, wk=WK, wv=WV, wo=WO, wi=WI, wf=WF, q=q, k=k, v=v, o=o, p=p, xh1=xh1, rs1=rs1, a=a, g=g, gp=gp,
        xh2=xh2, rs2=rs2, df=df, dr=dr, do=do, dq=dq, dk=dk, dv=dv, ds=ds, prow=0, qrow=12, brow=16,
        width=192, flip_attn=True, flip_in=False,
        bias_q=lambda u: BP[2 * c + u, 0:1, 0:192],
        bias_v=lambda u: BP[2 * c + u, 3:4, 0:192],
        bias_i=lambda j: BP[j, 1:2, :],
        third=lambda c: 0,
    )
    student = Layer(
        x=x2, wq=wsq, wk=wsk, wv=wsv, wo=wso, wi=SI, wf=SF, q=q2, k=k2, v=v2, o=o2, p=p2, xh1=xh12, rs1=rs12, a=a2,
        g=g2, gp=gp2, xh2=xh22, rs2=rs22, df=df, dr=dr, do=do, dq=dq, dk=dk, dv=dv, ds=ds, prow=6, qrow=24, brow=20,
        width=256, flip_attn=False, flip_in=True,
        bias_q=lambda u: jnp.concatenate([PRM[12:13, s_bias], PRM[12:13, 128:256]], axis=1),
        bias_v=lambda u: jnp.concatenate([PRM[12:13, v_bias], PRM[12:13, 512:640]], axis=1),
        bias_i=lambda j: BP[j, 2:3, 0 : SI.shape[1]],
        third=lambda c: c,
    )
    swap = Swap(me, send, recv, ssem, rsem, 4)

    def teacher_hook(name):
        if name == "qkv":
            sequences.take(0)
            gather.to_plane(G0)
            gather.onward(G0)
            gather.to_plane(G1[:1])
            for copy in pack_copies:
                copy.wait()
            for copy in local:
                copy.wait()
            gather.ready(G0)
        if name == "heads":
            gather.send(G2)
            gather.onward(G1[:1])
            gather.to_plane(G1[1:])
        if name == "middle":
            gather.onward(G1[1:])
            gather.send(G3)
            gather.to_plane(G2)
        if name == "attn":
            gather.onward(G2)
            gather.to_plane(G3)
            sequences.send(1)
            gather.ready(G1[:1])
        if name == "ffn_in":
            gather.ready(G1[1:])
        if name == "ffn_out":
            gather.onward(G3)
            gather.ready(G2)

    def student_hook(name):
        if name == "ffn_in":
            gather.ready(G3)
            sequences.take(1)

    def to_student(rows, value):
        x2[rows] = value.astype(BF)

    def to_output(rows, value):
        Y[rows] = value.astype(BF)

    def between(rows, value):
        dx2[rows] = value

    def to_grad(rows, value):
        DX[rows] = value.astype(BF)

    forward(teacher, me, swap, bias_row, PRM, teacher_hook, to_student)
    forward(student, me, swap, bias_row, PRM, student_hook, to_output)
    home.send(0)
    gather.drain(range(8))
    sequences.drain(0)
    sequences.drain(1)

    total = Reduce(me, weights, outs, bufs, reduce_sems)
    R0, R1, R2, R3 = (6, 7), (8, 9, 10, 11), (4, 5), (0, 1, 2, 3)

    def student_back(name):
        if name == "ffn_grads":
            total.start(R0)
        if name == "attn_grads":
            total.start(R1)

    def teacher_back(name):
        if name == "ffn_grads":
            total.start(R2)
            total.second(R0)
            total.second(R1)
        if name == "heads_done":
            total.along(R0)
            total.along(R1)
        if name == "attn_grads":
            total.start(R3)

    backward(student, me, swap, PRM, SM, lambda rows: CT[rows].astype(F32), student_back, between)
    backward(teacher, me, swap, PRM, SM, lambda rows: dx2[rows], teacher_back, to_grad)
    home.send(1)

    sml[0] = SM[...]
    for d in (1, 2, 3):
        remote(sml.at[0], sml.at[d], sms.at[d - 1], smr.at[d - 1], me.line(d)).start()
    total.spread(R0)
    total.spread(R1)
    total.second(R2)
    total.second(R3)
    total.spread_near(R1)
    for d in (1, 2, 3):
        remote(sml.at[0], sml.at[d], sms.at[d - 1], smr.at[d - 1], me.line(d)).wait()
    sml[4] = add_up([sml.at[i] for i in range(4)])
    for k in (1, 2, 3):
        remote(sml.at[4], sml.at[4 + k], sms.at[2 + k], smr.at[2 + k], me.plane(k)).start()
    total.onward(R0)
    total.along(R2)
    total.along(R3)
    total.onward(R1)
    for k in (1, 2, 3):
        remote(sml.at[4], sml.at[4 + k], sms.at[2 + k], smr.at[2 + k], me.plane(k)).wait()
    sml[8] = add_up([sml.at[4 + i] for i in range(4)])
    other_sums = remote(sml.at[8], sml.at[9], sms.at[6], smr.at[6], me.core())
    other_sums.start()
    total.spread(R2)
    total.finish(R0)
    total.finish(R1)
    total.spread(R3)
    total.onward(R2)
    total.onward(R3)
    other_sums.wait()
    both_sums = pltpu.make_async_copy(sml.at[pl.ds(8, 2)], SUMS, sls.at[9])
    both_sums.start()
    total.finish(R2)
    total.finish(R3)
    total.end(R1)
    total.end(R3)
    home.drain(0)
    home.drain(1)
    both_sums.wait()


def final_kernel(*refs):
    z = lax.axis_index("head")
    c = lax.rem(lax.axis_index("seq"), 2)
    YO, DO, SUMS = refs[:3]
    grads = refs[3:15]
    outs = refs[15:]
    outs[0][...] = YO[...].astype(F32)
    outs[1][...] = DO[...].astype(F32)
    for at, w in ((2, 0), (4, 1), (5, 2), (7, 3), (11, 4), (13, 5), (26, 6), (28, 7)):
        outs[at][...] = grads[w][...].astype(F32)
    near = pl.ds(pl.multiple_of(c * 256, 128), 128)
    far = pl.ds(pl.multiple_of((1 - c) * 256, 128), 128)
    for at, w in ((17, 8), (19, 9), (20, 10)):
        g = grads[w]
        outs[at][:, near] = g[0, :, 0:128].astype(F32)
        outs[at][:, far] = g[1, :, 0:128].astype(F32)
        outs[at][:, 128:256] = g[0, :, 128:256].astype(F32) + g[1, :, 128:256].astype(F32)
    g = grads[11]
    outs[22][near, :] = g[0, 0:128, :].astype(F32)
    outs[22][far, :] = g[1, 0:128, :].astype(F32)
    outs[22][128:256, :] = g[0, 128:256, :].astype(F32) + g[1, 128:256, :].astype(F32)

    def put(at, value):
        outs[at][...] = value.reshape(value.shape[1])

    for i, at in enumerate((8, 9, 10, 14, 15, 16, 23, 24, 25, 29, 30, 31)):
        put(at, SUMS[0, i : i + 1, :])
    side = jnp.where(z // 2 == c, 0, 1)
    put(3, SUMS[side, pl.ds(12 + z % 2, 1), 0:192])
    put(6, SUMS[side, pl.ds(14 + z % 2, 1), 0:192])
    put(12, SUMS[0, pl.ds(16 + z, 1), 0 : outs[12].shape[0]])
    put(27, SUMS[0, pl.ds(20 + z, 1), 0 : outs[27].shape[0]])
    for at, r in ((18, 24), (21, 25)):
        low = jnp.where(c == 0, SUMS[0, r : r + 1, 0:128], SUMS[1, r : r + 1, 0:128])
        high = jnp.where(c == 0, SUMS[1, r : r + 1, 0:128], SUMS[0, r : r + 1, 0:128])
        middle = SUMS[0, r : r + 1, 128:256] + SUMS[1, r : r + 1, 128:256]
        put(at, jnp.concatenate([low, middle, high], axis=1))


ANYWHERE = pl.BlockSpec(memory_space=pl.ANY)
IN_VMEM = pl.BlockSpec(memory_space=pltpu.VMEM)


def shape(*dims, kind=BF):
    return jax.ShapeDtypeStruct(dims, kind)


def body(
    tokens, lengths, cotangent,
    t_query, t_query_bias, t_key, t_value, t_value_bias, t_attn_out, t_attn_bias, t_norm1_gain, t_norm1_bias,
    t_ffn_in, t_ffn_in_bias, t_ffn_out, t_ffn_out_bias, t_norm2_gain, t_norm2_bias,
    s_query, s_query_bias, s_key, s_value, s_value_bias, s_attn_out, s_attn_bias, s_norm1_gain, s_norm1_bias,
    s_ffn_in, s_ffn_in_bias, s_ffn_out, s_ffn_out_bias, s_norm2_gain, s_norm2_bias,
):
    seq_size = lax.axis_size("seq")
    outer = seq_size // 2
    groups = [[2 * y + core for y in range(outer)] for core in range(2)]

    def widen(value, axis):
        if outer == 1:
            return value
        return lax.all_gather(value, "seq", axis=axis, tiled=True, axis_index_groups=groups)

    t_ffn_in, t_ffn_in_bias, t_ffn_out = widen(t_ffn_in, 1), widen(t_ffn_in_bias, 0), widen(t_ffn_out, 0)
    s_ffn_in, s_ffn_in_bias, s_ffn_out = widen(s_ffn_in, 1), widen(s_ffn_in_bias, 0), widen(s_ffn_out, 0)
    n_in, n_s = t_ffn_in.shape[1], s_ffn_in.shape[1]
    n = 4 * tokens.shape[1]

    dma = pltpu.SemaphoreType.DMA
    act = lambda *dims, kind=BF: pltpu.VMEM(dims, kind)
    wide = lambda *dims: pltpu.VMEM(dims, F32)
    weights = [
        (2, 192, 768), (2, 192, 768), (2, 192, 768), (2, 192, 768),
        (4, 768, n_in), (4, n_in, 768), (4, n_s, 768), (4, n_s, 768),
        (1, 768, 256), (1, 768, 256), (1, 768, 256), (1, 256, 768),
    ]
    names = len(weights)

    def piece(w):
        count, rows, cols = weights[w]
        return (count, rows // 8, cols) if cols == 384 else (count, rows // 4, cols // 2)

    def share(w):
        count, rows, cols = weights[w]
        return (rows // 16 if count == 1 else rows // 4, cols)

    results = pl.pallas_call(
        main_kernel,
        out_shape=[shape(2, 128, 768), shape(2, 128, 768), shape(2, 32, 768, kind=F32)]
        + [shape(2, *d[1:]) if d[0] == 1 else shape(*d[1:]) for d in weights],
        in_specs=[pl.BlockSpec(memory_space=pltpu.SMEM)] + [ANYWHERE] * 14 + [IN_VMEM] * 18,
        out_specs=[ANYWHERE] * (3 + names),
        scratch_shapes=[act(*d) for d in weights]
        + [
            act(n, 768), act(n, 768), wide(2, 8, 128), wide(8, n_in), wide(4, 8, n_in), wide(16, 768), wide(32, 768), wide(10, 32, 768),
            wide(8, n), act(2, n, 768), act(2, n, 768), dma((2, 4)), dma((2, 4)),
            act(2, n, 256), act(2, n, 256), act(2, n, 256), act(2, n, 256), act(6, n, n),
            wide(n, 768), wide(n, 1), act(n, 768), act(4, n, n_in), act(4, n, n_in), wide(n, 768), wide(n, 1),
            wide(n, 768), act(n, 768), act(2, n, 256), act(2, n, 256), act(2, n, 256), act(2, n, 256), act(n, n),
            act(n, 768), act(1, n, 256), act(1, n, 256), act(1, n, 256), act(1, n, 256), act(3, n, n),
            wide(n, 768), wide(n, 1), act(n, 768), act(4, n, n_s), act(4, n, n_s), wide(n, 768), wide(n, 1),
            wide(n, 768), act(n, 768), act(n, 768),
        ]
        + [act(2, *piece(w)) for w in range(names)]
        + [act(2, *piece(w)) for w in range(names)]
        + [act(*piece(w)) for w in range(names)]
        + [act(*piece(w)) for w in range(names)]
        + [act(3, *share(w)) for w in range(names)]
        + [act(weights[w][1] // 4, weights[w][2]) for w in range(names)]
        + [
            dma((8, 3)), dma((8, 3)), dma((8, 3, 2)), dma((8, 3, 2)), dma((8, 3, 2)), dma((8, 3, 2)), dma((8,)),
            dma((names, 4)), dma((names, 4)), dma((names, 2)), dma((names, 2)), dma((names, 3)), dma((names, 3)),
            dma((names, 2)), dma((names, 2)), dma((names, 2)), dma((names, 2)), dma((names,)), dma((names,)), dma((names,)),
            dma((4, 3)), dma((4, 3)),
            dma((2, 2)), dma((2, 4)), dma((2, 4)), dma((2, 4)), dma((2, 3)), dma((2, 2)),
            dma((3,)), dma((3,)), dma((1,)), dma((1,)), dma((10,)), dma((7,)), dma((7,)),
        ],
        compiler_params=pltpu.CompilerParams(collective_id=0, has_side_effects=True, vmem_limit_bytes=VMEM_LIMIT),
        name="layers",
    )(
        lengths, tokens, cotangent, t_query.T, t_key.T, t_value.T, t_attn_out, t_ffn_in, t_ffn_out, s_ffn_in.T, s_ffn_out,
        s_query, s_key, s_value, s_attn_out,
        t_attn_bias, t_norm1_gain, t_norm1_bias, t_ffn_out_bias, t_norm2_gain, t_norm2_bias,
        s_attn_bias, s_norm1_gain, s_norm1_bias, s_ffn_out_bias, s_norm2_gain, s_norm2_bias,
        s_query_bias, s_value_bias, t_query_bias, t_value_bias, t_ffn_in_bias, s_ffn_in_bias,
    )
    results = list(results)

    if outer > 1:
        results[2] = lax.psum(results[2], "seq", axis_index_groups=groups)
        results[3:] = [lax.psum(g.astype(F32), "seq", axis_index_groups=groups).astype(BF) for g in results[3:]]

    f = functools.partial(shape, kind=F32)
    final_shapes = [
        f(2, 128, 768), f(2, 128, 768),
        f(192, 768), f(192), f(192, 768), f(192, 768), f(192), f(192, 768),
        f(768), f(768), f(768), f(768, n_in), f(n_in), f(n_in, 768), f(768), f(768), f(768),
        f(768, 384), f(384), f(768, 384), f(768, 384), f(384), f(384, 768),
        f(768), f(768), f(768), f(n_s, 768), f(n_s), f(n_s, 768), f(768), f(768), f(768),
    ]
    outs = list(
        pl.pallas_call(
            final_kernel,
            out_shape=final_shapes,
            in_specs=[IN_VMEM] * (3 + names),
            out_specs=[IN_VMEM] * len(final_shapes),
            compiler_params=pltpu.CompilerParams(vmem_limit_bytes=VMEM_LIMIT),
            name="final",
        )(*results)
    )
    for i in (2, 4, 5, 26):
        outs[i] = outs[i].T
    if outer > 1:
        y = lax.axis_index("seq") // 2
        for i, axis in ((11, 1), (12, 0), (13, 0), (26, 1), (27, 0), (28, 0)):
            width = outs[i].shape[axis] // outer
            outs[i] = lax.dynamic_slice_in_dim(outs[i], y * width, width, axis)
    return tuple(outs)


def solution(mesh):
    seqs = P(("row", "seq"), "head", None)
    col, line, row_spec = P(None, "head"), P("head"), P("head", None)
    fcol, fline, frow = P(None, ("head", "seq")), P(("head", "seq")), P(("head", "seq"), None)
    rep = P()
    teacher = (col, line, col, col, line, row_spec, rep, rep, rep, fcol, fline, frow, rep, rep, rep)
    student = (rep,) * 9 + (fcol, fline, frow, rep, rep, rep)
    return jax.shard_map(
        body,
        mesh=mesh,
        in_specs=(seqs, P(("row", "seq")), seqs) + teacher + student,
        out_specs=(seqs, seqs) + teacher + student,
        check_vma=False,
    )
```

```python
import functools

import jax
import jax.numpy as jnp
from jax import lax
from jax.experimental import pallas as pl
from jax.experimental.pallas import tpu as pltpu
from jax.sharding import PartitionSpec as P

MESH = pl.DeviceIdType.MESH
F32 = jnp.float32
BF = jnp.bfloat16
EPS = 1e-5
MASKED = -1000000000.0
VMEM_LIMIT = 63 << 20


class Place:
    def __init__(self):
        self.r = lax.axis_index("row")
        self.z = lax.axis_index("head")
        self.s = lax.axis_index("seq")
        self.c = lax.rem(self.s, 2)

    def core(self):
        return (self.r, self.z, self.s + 1 - 2 * self.c)

    def line_index(self, step):
        return lax.rem(self.z + step + 4, 4)

    def line(self, step):
        return (self.r, self.line_index(step), self.s)

    def plane_index(self, k):
        if k == 1:
            return self.r + 1 - 2 * lax.rem(self.r, 2)
        if k == 2:
            return lax.rem(self.r + 2, 4)
        return 3 - self.r

    def plane(self, k):
        return (self.plane_index(k), self.z, self.s)


def greet(me):
    barrier = pltpu.get_barrier_semaphore()
    others = [me.core()] + [me.line(i) for i in (1, 2, 3)] + [me.plane(k) for k in (1, 2, 3)]
    for other in others:
        pl.semaphore_signal(barrier, inc=1, device_id=other, device_id_type=MESH)
    pl.semaphore_wait(barrier, len(others))


def remote(src, dst, send_sem, recv_sem, device):
    return pltpu.make_async_remote_copy(
        src_ref=src, dst_ref=dst, send_sem=send_sem, recv_sem=recv_sem, device_id=device, device_id_type=MESH
    )


def rows_of(index, count, unit=16):
    return pl.ds(pl.multiple_of(index * count, unit), count)


class Gather:
    def __init__(self, me, shards, sems):
        self.me, self.shards = me, shards
        self.zs, self.zr, self.ps, self.pr, self.fs, self.fr, self.ls, self.hs = sems
        self.inner = jnp.logical_and(me.z >= 1, me.z <= 2)
        self.across = {1: me.z != 3, 2: me.z >= 0, 3: me.z != 0}

    def only(self, w, cond):
        return (lambda f: pl.when(cond)(f)) if self.shards[w][2] == 2 else (lambda f: f())

    def slot(self, w, index):
        return index % 2 if self.shards[w][2] == 2 else index

    def quarter(self, w, r):
        return rows_of(r, self.shards[w][0].shape[0] // 4)

    def part(self, w, frm, r, half=None):
        dst = self.shards[w][1]
        count, cols = dst.shape[1] // 4, dst.shape[2]
        slot = self.slot(w, frm)
        if half is None:
            return dst.at[slot, rows_of(r, count)]
        if cols == 768:
            return dst.at[slot, rows_of(r, count), pl.ds(half * 384, 384)]
        return dst.at[slot, rows_of(2 * r + half, count // 2)]

    def begin(self, parts, ahead):
        me = self.me
        self.parts, self.ahead, self.turn = parts, ahead, 0
        for w, (src, dst, count) in enumerate(self.shards):

            @self.only(w, me.z // 2 == me.c)
            def _():
                pltpu.make_async_copy(src, dst.at[self.slot(w, me.z)], self.ls.at[w]).start()

        for i in range(ahead):
            self.send(i)

    def send(self, i):
        me = self.me
        if i >= len(self.parts):
            return
        for w, d in self.parts[i]:

            @self.only(w, me.z // 2 == me.c)
            def _():
                @pl.when(self.across[d])
                def _():
                    self.line_copy(w, d).start()

    def advance(self, until):
        while self.turn < until:
            i = self.turn
            if i < len(self.parts):
                self.to_plane(self.parts[i])
                self.send(i + self.ahead)
            if 0 <= i - 1 < len(self.parts):
                self.onward(self.parts[i - 1])
            self.turn += 1

    def line_copy(self, w, d):
        me = self.me
        return remote(
            self.shards[w][0].at[self.quarter(w, me.r)],
            self.part(w, me.z, me.r),
            self.zs.at[w, d - 1],
            self.zr.at[w, d - 1],
            me.line(d),
        )

    def end_copy(self, w):
        me = self.me
        ref = self.part(w, me.line_index(-2), me.r)
        return remote(ref, ref, self.hs.at[w], self.zr.at[w, jnp.clip(2 * me.z - 2, 0, 2)], (me.r, jnp.clip(3 * (me.z - 1), 0, 3), me.s))

    def plane_copy(self, w, d, k):
        me = self.me
        ref = self.part(w, me.line_index(-d), me.r)
        return remote(ref, ref, self.ps.at[w, d - 1, k - 1], self.pr.at[w, d - 1, k - 1], me.plane(k))

    def on_copy(self, w, d, k):
        me = self.me
        ref = self.part(w, me.line_index(-d), me.plane_index(3 - k), k - 1)
        return remote(ref, ref, self.fs.at[w, d - 1, k - 1], self.fr.at[w, d - 1, k - 1], me.plane(k))

    def each(self, part, step):
        for w, d in part:

            @self.only(w, self.me.line_index(-d) // 2 == self.me.c)
            def _():
                step(w, d)

    def to_plane(self, ws):
        def step(w, d):
            self.line_copy(w, d).wait_recv()
            if d == 2:

                @pl.when(self.inner)
                def _():
                    self.end_copy(w).start()

            self.plane_copy(w, d, 1).start()
            self.plane_copy(w, d, 2).start()

        self.each(ws, step)

    def onward(self, ws):
        def step(w, d):
            for k in (1, 2):
                self.plane_copy(w, d, k).wait_recv()
                self.on_copy(w, d, 3 - k).start()

        self.each(ws, step)

    def ready(self, ws):
        def step(w, d):
            for k in (1, 2):
                self.on_copy(w, d, k).wait_recv()

        self.each([(w, d) for w in ws for d in (1, 2, 3)], step)
        for w in ws:
            src, dst, count = self.shards[w]

            @self.only(w, self.me.z // 2 == self.me.c)
            def _():
                pltpu.make_async_copy(src, dst.at[0], self.ls.at[w]).wait()

    def drain(self, ws):
        def step(w, d):
            if d == 2:

                @pl.when(self.inner)
                def _():
                    self.end_copy(w).wait_send()

            for k in (1, 2):
                self.plane_copy(w, d, k).wait_send()
                self.on_copy(w, d, k).wait_send()

        self.each([(w, d) for w in ws for d in (1, 2, 3)], step)
        for w in ws:

            @self.only(w, self.me.z // 2 == self.me.c)
            def _():
                for d in (1, 2, 3):

                    @pl.when(self.across[d])
                    def _():
                        self.line_copy(w, d).wait_send()


PAIR, OWNER, EVERY = 0, 1, 2
KINDS = (OWNER,) * 2 + (EVERY,) + (OWNER,) * 4 + (PAIR,) * 4


def piece_shape(dims):
    count, rows, cols = dims
    return (count, rows // 4, cols // 2) if cols == 768 else (count, rows // 8, cols)


class Reduce:
    def __init__(self, me, grads, outs, kinds, chunks, bufs, sems):
        self.me, self.grads, self.outs, self.kinds, self.chunks = me, grads, outs, kinds, chunks
        self.RA, self.RB, self.RC, self.RD, self.RZ, self.SUM = bufs
        (self.as_, self.ar, self.bs, self.br, self.zs, self.zr, self.gs, self.gr, self.fs, self.fr, self.ls,
         self.cs, self.cr, self.ns, self.nr) = sems
        self.mx, self.my = lax.rem(me.r, 2), me.r // 2
        self.owner = me.z // 2 == me.c
        self.made = self.launched = self.turn = 0

    def quarter(self, w):
        return self.grads[w].shape[1] // 4

    def piece(self, w, t, half):
        g = self.grads[w]
        q, cols = self.quarter(w), g.shape[2]
        if cols == 768:
            return g.at[:, rows_of(t, q), pl.ds(half * 384, 384)]
        return g.at[:, rows_of(2 * t + half, q // 2)]

    def first_copy(self, w, half, other):
        if half == 0:
            t, k, land = 2 * other + 1 - self.mx, 1, self.RA
        else:
            t, k, land = 2 * (1 - self.my) + other, 2, self.RB
        i = 2 * half + other
        return remote(
            self.piece(w, t, half), land[w].at[other], self.as_.at[w, i], self.ar.at[w, i], self.me.plane(k)
        )

    def start(self, ws):
        for w in ws:
            for other in (0, 1):
                for half in (0, 1):
                    self.first_copy(w, half, other).start()

    def kept(self, w, half, other):
        t = 2 * other + self.mx if half == 0 else 2 * self.my + other
        return self.piece(w, t, half)

    def second_copy(self, w, half):
        if half == 0:
            return remote(
                self.piece(w, 2 * (1 - self.my) + self.mx, 0), self.RC[w], self.bs.at[w, 0], self.br.at[w, 0], self.me.plane(2)
            )
        return remote(
            self.piece(w, 2 * self.my + 1 - self.mx, 1), self.RD[w], self.bs.at[w, 1], self.br.at[w, 1], self.me.plane(1)
        )

    def add_into(self, target, ref):
        target[...] = (target[...].astype(F32) + ref[...].astype(F32)).astype(BF)

    def second(self, ws):
        for w in ws:
            for other in (0, 1):
                for half in (0, 1):
                    self.first_copy(w, half, other).wait()
            for half, land in ((0, self.RA), (1, self.RB)):

                @pl.loop(0, 2)
                def _(other):
                    self.add_into(self.kept(w, half, other), land[w].at[other])

                self.second_copy(w, half).start()

    def along(self, ws):
        me = self.me
        for w in ws:
            for half, land in ((0, self.RC), (1, self.RD)):
                self.second_copy(w, half).wait()
                self.add_into(self.piece(w, me.r, half), land[w])
            if self.kinds[w] == PAIR:
                for u in range(2):

                    @pl.when(2 * me.c + u != me.z)
                    def _():
                        self.unit_copy(w, u).start()

            else:
                for d in (1, 2, 3):
                    self.line_copy(w, d).start()

    def unit_copy(self, w, u):
        me = self.me
        target = 2 * me.c + u
        slot = lax.rem(target - me.z + 3, 4)
        slot = jnp.minimum(slot, 2)
        return remote(
            self.grads[w].at[u, rows_of(me.r, self.quarter(w))],
            self.RZ[w].at[slot],
            self.zs.at[w, u],
            self.zr.at[w, slot],
            (me.r, target, me.s),
        )

    def line_copy(self, w, d):
        me = self.me
        q = self.quarter(w)
        src = self.grads[w].at[me.line_index(d), rows_of(me.r, q)]
        return remote(src, self.RZ[w].at[d - 1], self.zs.at[w, d - 1], self.zr.at[w, d - 1], me.line(d))

    def near_copy(self, w, d):
        mine = self.SUM[w].at[self.me.z]
        return remote(mine, mine, self.ns.at[w, d - 1], self.nr.at[w, d - 1], self.me.line(d))

    def out_part(self, w, t, half=None):
        out, q = self.outs[w], self.quarter(w)
        if self.kinds[w] == EVERY:
            rows = rows_of(t, q) if half is None else rows_of(2 * t + half, q // 2)
            return out.at[0, :, rows]
        if half is None:
            return out.at[rows_of(t, q)]
        if out.shape[1] == 768:
            return out.at[rows_of(t, q), pl.ds(half * 384, 384)]
        return out.at[rows_of(2 * t + half, q // 2)]

    def plane_copy(self, w, k):
        me = self.me
        return remote(self.SUM[w], self.out_part(w, me.r), self.gs.at[w, k - 1], self.gr.at[w, k - 1], me.plane(k))

    def on_copy(self, w, k):
        ref = self.out_part(w, self.me.plane_index(3 - k), k - 1)
        return remote(ref, ref, self.fs.at[w, k - 1], self.fr.at[w, k - 1], self.me.plane(k))

    def own_copy(self, w):
        return pltpu.make_async_copy(self.SUM[w], self.out_part(w, self.me.r), self.ls.at[w])

    def core_copy(self, w):
        if self.kinds[w] == EVERY:
            return remote(self.outs[w].at[0], self.outs[w].at[1], self.cs.at[w], self.cr.at[w], self.me.core())
        return remote(self.outs[w], self.outs[w], self.cs.at[w], self.cr.at[w], self.me.core())

    def only(self, w):
        return (lambda f: pl.when(self.owner)(f)) if self.kinds[w] == PAIR else (lambda f: f())

    def spread_start(self, w):
        self.own_copy(w).start()
        self.plane_copy(w, 1).start()
        self.plane_copy(w, 2).start()

    def spread(self, ws):
        me = self.me
        for w in ws:
            q = self.quarter(w)
            kind = self.kinds[w]
            if kind == PAIR:
                for u in range(2):

                    @pl.when(2 * me.c + u != me.z)
                    def _():
                        self.unit_copy(w, u).wait_send()

                @pl.when(self.owner)
                def _():
                    for d in (1, 2, 3):
                        remote(self.RZ[w].at[0], self.RZ[w].at[d - 1], self.zs.at[w, 0], self.zr.at[w, d - 1], me.core()).wait_recv()
                    own = self.grads[w].at[me.z % 2, rows_of(me.r, q)]
                    self.SUM[w][...] = add_up([own] + [self.RZ[w].at[d] for d in range(3)]).astype(BF)
                    self.spread_start(w)

                continue
            for d in (1, 2, 3):
                self.line_copy(w, d).wait()
            own = self.grads[w].at[me.z, rows_of(me.r, q)]
            total = add_up([own] + [self.RZ[w].at[d] for d in range(3)]).astype(BF)
            if kind == EVERY:
                self.SUM[w][me.z] = total
                for d in (1, 2, 3):
                    self.near_copy(w, d).start()
            else:
                self.SUM[w][...] = total
                self.spread_start(w)

    def spread_near(self, ws):
        for w in ws:
            for d in (1, 2, 3):
                self.near_copy(w, d).wait()
            self.spread_start(w)

    def onward(self, ws):
        for w in ws:

            @self.only(w)
            def _():
                for k in (1, 2):
                    self.plane_copy(w, k).wait()
                    self.on_copy(w, 3 - k).start()

    def finish(self, ws):
        for w in ws:

            @self.only(w)
            def _():
                self.own_copy(w).wait()
                for k in (1, 2):
                    self.on_copy(w, k).wait()
                if self.kinds[w] != OWNER:
                    self.core_copy(w).start()

    def end(self):
        for w, kind in enumerate(self.kinds):
            if kind == PAIR:

                @pl.when(self.owner)
                def _():
                    self.core_copy(w).wait_send()

                @pl.when(jnp.logical_not(self.owner))
                def _():
                    self.core_copy(w).wait_recv()

            elif kind == EVERY:
                self.core_copy(w).wait()

    def launch(self, upto):
        while self.launched < min(upto, self.made, len(self.chunks)):
            self.start(self.chunks[self.launched])
            self.launched += 1

    def ready(self, made, ahead):
        self.made = made
        self.launch(self.turn + ahead)

    def step(self, ahead):
        i = self.turn

        def at(back, every=None):
            chunk = self.chunks[i - back] if 0 <= i - back < len(self.chunks) else ()
            return [w for w in chunk if every is None or every == (self.kinds[w] == EVERY)]

        self.second(at(0))
        self.turn += 1
        self.launch(self.turn + ahead)
        self.along(at(1))
        self.spread(at(2))
        self.spread_near(at(3, True))
        self.onward(at(3, False) + at(4, True))
        self.finish(at(4, False) + at(5, True))

    def rest(self, ahead):
        while self.turn < len(self.chunks) + 4:
            self.step(ahead)


def add_up(refs):
    total = refs[0][...].astype(F32)
    for ref in refs[1:]:
        total = total + ref[...].astype(F32)
    return total


def nn(a, b):
    return lax.dot_general(a, b, (((1,), (0,)), ((), ())), preferred_element_type=F32)


def nt(a, b):
    return lax.dot_general(a, b, (((1,), (1,)), ((), ())), preferred_element_type=F32)


def tn(a, b):
    return lax.dot_general(a, b, (((0,), (0,)), ((), ())), preferred_element_type=F32)


def norm_parts(value):
    center = value - jnp.mean(value, axis=-1, keepdims=True)
    spread = jnp.mean(center * center, axis=-1, keepdims=True)
    rstd = lax.rsqrt(spread + EPS)
    return center * rstd, rstd


def norm_grad(xh, rstd, gain, dy):
    scaled = dy * gain
    mean_one = jnp.mean(scaled, axis=-1, keepdims=True)
    mean_two = jnp.mean(scaled * xh, axis=-1, keepdims=True)
    return (scaled - mean_one - xh * mean_two) * rstd


def col_sum(value):
    return jnp.sum(value, axis=0, keepdims=True)


class Swap:
    def __init__(self, me, send, recv, ssem, rsem, chunks):
        self.me, self.send, self.recv, self.ssem, self.rsem = me, send, recv, ssem, rsem
        self.rows = send.shape[1] // chunks
        self.chunks = chunks
        self.turn = 0

    def copy(self, slot, i):
        rows = rows_of(i, self.rows)
        return remote(
            self.send.at[slot, rows],
            self.recv.at[slot, rows],
            self.ssem.at[slot, i],
            self.rsem.at[slot, i],
            self.me.core(),
        )

    def run(self, part, between, post):
        slot = self.turn % 2
        self.turn += 1

        @pl.loop(0, self.chunks)
        def _(i):
            rows = rows_of(i, self.rows)
            self.send[slot, rows] = part(rows).astype(BF)
            self.copy(slot, i).start()

        if between is not None:
            between()

        @pl.loop(0, self.chunks)
        def _(i):
            rows = rows_of(i, self.rows)
            self.copy(slot, i).wait()
            total = self.send[slot, rows].astype(F32) + self.recv[slot, rows].astype(F32)
            post(i, rows, total)


class Layer:
    def __init__(self, **kw):
        self.__dict__.update(kw)


def head_mask(layer, i, c):
    h = lax.rem(i, 3)
    half = jnp.where(h == 2, layer.third(c), lax.rem(h, 2))
    lane = lax.broadcasted_iota(jnp.int32, (1, 128), 1) // 64
    mask = jnp.where(lane == half, 1.0, 0.0).astype(BF)
    return i // 3, pl.ds(pl.multiple_of((h // 2) * 128, 128), 128), mask


def forward(layer, me, swap, bias_row, prm, hook, done):
    L, c = layer, me.c
    units = L.q.shape[0]

    hook("qkv")
    project = nt if L.flip_attn else nn

    @pl.loop(0, units)
    def _(u):
        x = L.x[...]
        n = L.width
        L.q[u, :, :n] = ((project(x, L.wq[u]) + L.bias_q(u)).astype(BF) * 0.125).astype(BF)
        L.k[u, :, :n] = project(x, L.wk[u]).astype(BF)
        L.v[u, :, :n] = (project(x, L.wv[u]) + L.bias_v(u)).astype(BF)
        if n < 256:
            pad = jnp.zeros((x.shape[0], 256 - n), BF)
            L.q[u, :, n:] = pad
            L.k[u, :, n:] = pad
            L.v[u, :, n:] = pad
        L.o[u] = jnp.zeros(L.o.shape[1:], BF)

    hook("heads")

    def heads(lo, hi):
        @pl.loop(lo, hi)
        def _(i):
            u, cols, mask = head_mask(L, i, c)
            k = L.k[u, :, cols]
            v = L.v[u, :, cols] * mask
            for ch in range(4):
                rows = pl.ds(ch * 128, 128)
                scores = nt(L.q[u, rows, cols] * mask, k) + bias_row[0:1, :]
                top = jnp.max(scores, axis=-1, keepdims=True)
                expo = jnp.exp(scores - top)
                inv = 1.0 / jnp.sum(expo, axis=-1, keepdims=True)
                probs = (expo * inv).astype(BF)
                L.p[i, rows] = probs
                L.o[u, rows, cols] = L.o[u, rows, cols] + nn(probs, v).astype(BF)

    heads(0, 3)
    if units == 2:
        hook("middle")
        heads(3, 6)
    hook("attn")

    def attn_part(rows):
        n = L.width
        total = nn(L.o[0, rows, :n], L.wo[0])
        for u in range(1, units):
            total = total + nn(L.o[u, rows, :n], L.wo[u])
        return total

    def attn_post(i, rows, total):
        value = L.x[rows].astype(F32) + total + prm[L.prow : L.prow + 1, :]
        xh, rstd = norm_parts(value)
        L.xh1[rows] = xh
        L.rs1[rows] = rstd
        L.a[rows] = (xh * prm[L.prow + 1 : L.prow + 2, :] + prm[L.prow + 2 : L.prow + 3, :]).astype(BF)

    swap.run(attn_part, None, attn_post)
    hook("ffn_in")
    enter = nt if L.flip_in else nn

    @pl.loop(0, 4)
    def _(j):
        pre = enter(L.a[...], L.wi[j]) + L.bias_i(j)
        sq = pre * pre
        t = jnp.tanh(0.7978845608028654 * pre * (1.0 + 0.044715 * sq))
        half = 0.5 * (1.0 + t)
        L.g[j] = (pre * half).astype(BF)
        slope = half + 0.5 * pre * (1.0 - t * t) * (0.7978845608028654 + 0.7978845608028654 * 0.134145 * sq)
        L.gp[j] = slope.astype(BF)

    hook("ffn_out")

    def ffn_part(rows):
        total = nn(L.g[0, rows], L.wf[0])
        for j in range(1, 4):
            total = total + nn(L.g[j, rows], L.wf[j])
        return total

    def ffn_post(i, rows, total):
        value = L.a[rows].astype(F32) + total + prm[L.prow + 3 : L.prow + 4, :]
        xh, rstd = norm_parts(value)
        L.xh2[rows] = xh
        L.rs2[rows] = rstd
        done(rows, xh * prm[L.prow + 4 : L.prow + 5, :] + prm[L.prow + 5 : L.prow + 6, :])

    swap.run(ffn_part, None, ffn_post)


def backward(layer, me, swap, prm, sums, upstream, hook, done):
    L, c = layer, me.c
    units = L.q.shape[0]
    prow = L.prow
    n_rows = L.x.shape[0]
    hook("start")
    for i in range(6):
        sums[prow + i : prow + i + 1, :] = jnp.zeros((1, 768), F32)

    @pl.loop(0, n_rows // 128)
    def _(i):
        rows = rows_of(i, 128)
        dy = upstream(rows)
        xh = L.xh2[rows]
        sums[prow + 4 : prow + 5, :] += col_sum(dy * xh)
        sums[prow + 5 : prow + 6, :] += col_sum(dy)
        df = norm_grad(xh, L.rs2[rows], prm[prow + 4 : prow + 5, :], dy)
        low = df.astype(BF)
        sums[prow + 3 : prow + 4, :] += col_sum(low.astype(F32))
        L.df[rows] = df
        L.dr[rows] = low

    @pl.loop(0, 4)
    def _(j):
        dpre = (nt(L.dr[...], L.wf[j]) * L.gp[j].astype(F32)).astype(BF)
        L.gp[j] = dpre
        n = dpre.shape[1]
        sums[pl.ds(L.brow + j, 1), :n] = col_sum(dpre.astype(F32))
        L.wf[j] = tn(L.g[j], L.dr[...]).astype(BF)

    hook("out_grads")
    leave = nn if L.flip_in else nt

    def ffn_part(rows):
        total = leave(L.gp[0, rows], L.wi[0])
        for j in range(1, 4):
            total = total + leave(L.gp[j, rows], L.wi[j])
        return total

    def ffn_weights():
        @pl.loop(0, 4)
        def _(j):
            if L.flip_in:
                L.wi[j] = tn(L.gp[j], L.a[...]).astype(BF)
            else:
                L.wi[j] = tn(L.a[...], L.gp[j]).astype(BF)

        hook("ffn_grads")

    def ffn_post(i, rows, total):
        da = L.df[rows] + total
        xh = L.xh1[rows]
        sums[prow + 1 : prow + 2, :] += col_sum(da * xh)
        sums[prow + 2 : prow + 3, :] += col_sum(da)
        dh = norm_grad(xh, L.rs1[rows], prm[prow + 1 : prow + 2, :], da)
        low = dh.astype(BF)
        sums[prow : prow + 1, :] += col_sum(low.astype(F32))
        L.df[rows] = dh
        L.dr[rows] = low

    swap.run(ffn_part, ffn_weights, ffn_post)
    hook("attn")

    @pl.loop(0, units)
    def _(u):
        n = L.width
        L.do[u, :, :n] = nt(L.dr[...], L.wo[u]).astype(BF)
        if n < 256:
            L.do[u, :, n:] = jnp.zeros((n_rows, 256 - n), BF)
        for ref in (L.dq, L.dk, L.dv):
            ref[u] = jnp.zeros(ref.shape[1:], BF)

    @pl.loop(0, 3 * units)
    def _(i):
        u, cols, mask = head_mask(L, i, c)
        k = L.k[u, :, cols] * mask
        v = L.v[u, :, cols]
        for ch in range(4):
            rows = pl.ds(ch * 128, 128)
            d_probs = nt(L.do[u, rows, cols] * mask, v)
            probs = L.p[i, rows].astype(F32)
            both = probs * d_probs
            d_scores = (both - probs * jnp.sum(both, axis=-1, keepdims=True)).astype(BF)
            L.ds[rows] = d_scores
            L.dq[u, rows, cols] = L.dq[u, rows, cols] + (nn(d_scores, k) * 0.125).astype(BF)
        L.dv[u, :, cols] = L.dv[u, :, cols] + tn(L.p[i], L.do[u, :, cols] * mask).astype(BF)
        L.dk[u, :, cols] = L.dk[u, :, cols] + tn(L.ds[...], L.q[u, :, cols] * mask).astype(BF)

    hook("heads_done")
    back = nn if L.flip_attn else nt

    def attn_part(rows):
        n = L.width
        total = None
        for u in range(units):
            for grad, weight in ((L.dq, L.wq), (L.dk, L.wk), (L.dv, L.wv)):
                term = back(grad[u, rows, :n], weight[u])
                total = term if total is None else total + term
        return total

    def attn_weights():
        if L.pack is not None:
            L.pack()
            sums[L.qrow : L.qrow + 1, :256] = col_sum(L.dq[0].astype(F32))
            sums[L.qrow + 1 : L.qrow + 2, :256] = col_sum(L.dv[0].astype(F32))
            hook("attn_grads")
            return

        @pl.loop(0, units)
        def _(u):
            n = L.width
            L.wo[u] = tn(L.o[u, :, :n], L.dr[...]).astype(BF)
            x = L.x[...]
            for grad, out in ((L.dq, L.wq), (L.dk, L.wk), (L.dv, L.wv)):
                out[u] = tn(grad[u, :, :n], x).astype(BF)
            sums[pl.ds(L.qrow + u, 1), :256] = col_sum(L.dq[u].astype(F32))
            sums[pl.ds(L.qrow + units + u, 1), :256] = col_sum(L.dv[u].astype(F32))

        hook("attn_grads")

    def attn_post(i, rows, total):
        done(rows, L.df[rows] + total)

    swap.run(attn_part, attn_weights, attn_post)


class Sequences:
    def __init__(self, me, pairs, sems):
        self.me, self.pairs = me, pairs
        self.xs, self.xr, self.fs, self.fr = sems
        self.owner = me.z // 2 == me.c

    def send(self, a):
        me = self.me
        src, dst = self.pairs[a]
        for j in range(2):
            target = 2 * me.c + j

            @pl.when(target != me.z)
            def _():
                remote(src.at[j], dst.at[rows_of(me.z, 128)], self.xs.at[a, j], self.xr.at[a, me.z], (me.r, target, me.s)).start()

            @pl.when(target == me.z)
            def _():
                pltpu.make_async_copy(src.at[j], dst.at[rows_of(me.z, 128)], self.xr.at[a, me.z]).start()

    def core_copy(self, a, frm, i):
        dst = self.pairs[a][1].at[rows_of(frm, 128)]
        return remote(dst, dst, self.fs.at[a, i], self.fr.at[a, frm], self.me.core())

    def take(self, a):
        me = self.me
        src, dst = self.pairs[a]

        @pl.when(self.owner)
        def _():
            pltpu.make_async_copy(src.at[0], dst.at[rows_of(me.z, 128)], self.xr.at[a, me.z]).wait()
            self.core_copy(a, me.z, 0).start()
            for d in (1, 2, 3):
                frm = me.line_index(-d)
                remote(src.at[0], dst.at[rows_of(frm, 128)], self.xs.at[a, 0], self.xr.at[a, frm], me.core()).wait_recv()
                self.core_copy(a, frm, d).start()

        @pl.when(jnp.logical_not(self.owner))
        def _():
            for i in range(4):
                self.core_copy(a, i, i).wait_recv()

    def drain(self, a):
        me = self.me
        src, dst = self.pairs[a]
        for j in range(2):

            @pl.when(2 * me.c + j != me.z)
            def _():
                remote(src.at[j], dst.at[rows_of(me.z, 128)], self.xs.at[a, j], self.xr.at[a, me.z], me.core()).wait_send()

        @pl.when(self.owner)
        def _():
            for i in range(4):
                self.core_copy(a, i, i).wait_send()


class Home:
    def __init__(self, me, pairs, sems):
        self.me, self.pairs = me, pairs
        self.ys, self.yr = sems
        self.owner = me.z // 2 == me.c

    def send(self, a):
        me = self.me
        src, dst = self.pairs[a]

        @pl.when(self.owner)
        def _():
            pltpu.make_async_copy(src.at[rows_of(me.z, 128)], dst.at[me.z % 2], self.yr.at[a, me.z % 2]).start()
            for d in (1, 2, 3):
                remote(
                    src.at[rows_of(me.line_index(d), 128)],
                    dst.at[me.z % 2],
                    self.ys.at[a, d - 1],
                    self.yr.at[a, me.z % 2],
                    me.line(d),
                ).start()

    def drain(self, a):
        me = self.me
        src, dst = self.pairs[a]

        @pl.when(self.owner)
        def _():
            for d in (1, 2, 3):
                remote(src.at[rows_of(0, 128)], dst.at[0], self.ys.at[a, d - 1], self.yr.at[a, 0], me.core()).wait_send()

        for j in range(2):
            chip = 2 * me.c + j

            @pl.when(chip == me.z)
            def _():
                pltpu.make_async_copy(src.at[rows_of(0, 128)], dst.at[j], self.yr.at[a, j]).wait()

            @pl.when(chip != me.z)
            def _():
                remote(src.at[rows_of(0, 128)], dst.at[j], self.ys.at[a, 0], self.yr.at[a, j], me.core()).wait_recv()


def row(ref):
    return ref[...].astype(F32).reshape(1, ref.shape[0])


def main_kernel(*refs):
    me = Place()
    z, c = me.z, me.c
    lens = refs[0]
    (tok, cot, tq, tk, tv, to, ti, tf, si, sf, SQ, SK, SV, SO) = refs[1:15]
    vectors = refs[15:27]
    sqb, svb, tqb, tvb, tib, sib = refs[27:33]
    (YO, DO, SUMS) = refs[33:36]
    outs = refs[36:45]
    rest = list(refs[45:])

    def take(count):
        head, rest[:] = rest[:count], rest[count:]
        return head

    WQ, WK, WV, WO, WI, WF, SI, SF, wsq, wsk, wsv, wso = weights = take(12)
    X, CT, LN, PACK, BP, PRM, SM, sml, both, SG, BX, RBX = take(12)
    bias_row, send, recv, ssem, rsem = take(5)
    q, k, v, o, p, xh1, rs1, a, g, gp, xh2, rs2, df, dr, do, dq, dk, dv, ds = take(19)
    x2, q2, k2, v2, o2, p2, xh12, rs12, a2, g2, gp2, xh22, rs22, dx2, Y, DX = take(16)
    bufs = [take(len(KINDS)) for _ in range(6)]
    gather_sems = take(8)
    reduce_sems = take(15)
    seq_sems, home_sems = take(4), take(2)
    pks, pkr, lcs, lcr, sls, sms, smr, hcs, hcr = take(9)

    LN[0] = jnp.full(LN.shape[1:], lens[z % 2].astype(F32))
    PACK[...] = jnp.zeros(PACK.shape, F32)
    PACK[0:1, 0:192] = row(tqb)
    PACK[1:2, :] = row(tib)
    PACK[2:3, 0 : sib.shape[0]] = row(sib)
    PACK[3:4, 0:192] = row(tvb)
    greet(me)
    owner = z // 2 == c

    sequences = Sequences(me, ((tok, X), (cot, CT)), seq_sems)
    home = Home(me, ((Y, YO), (DX, DO)), home_sems)
    gather = Gather(
        me,
        ((tq, WQ, 2), (tk, WK, 2), (tv, WV, 2), (to, WO, 2), (ti, WI, 4), (tf, WF, 4), (si, SI, 4), (sf, SF, 4)),
        gather_sems,
    )

    pack_copies = [remote(PACK, BP.at[z], pks.at[d - 1], pkr.at[d - 1], me.line(d)) for d in (1, 2, 3)]
    for copy in pack_copies:
        copy.start()
    far_first = (2, 1, 3)
    gather.begin(
        [[(w, d) for d in far_first] for w in (0, 1, 2, 3)]
        + [[(4, d)] for d in far_first]
        + [[(5, d)] for d in far_first]
        + [[(w, d) for d in far_first] for w in (6, 7)],
        3,
    )
    lens_copy = remote(LN.at[0], LN.at[1], lcs.at[0], lcr.at[0], me.core())

    @pl.when(owner)
    def _():
        lens_copy.start()

    first = pl.ds(pl.multiple_of(c * 256, 128), 128)
    local = []
    for i, (src, dst) in enumerate(((SQ, wsq), (SK, wsk), (SV, wsv))):
        local.append((src.at[:, first], dst.at[0, :, pl.ds(0, 128)]))
        local.append((src.at[:, pl.ds(128, 128)], dst.at[0, :, pl.ds(128, 128)]))
    local.append((SO.at[first], wso.at[0, pl.ds(0, 128)]))
    local.append((SO.at[pl.ds(128, 128)], wso.at[0, pl.ds(128, 128)]))
    local.append((PACK, BP.at[z]))
    local = [pltpu.make_async_copy(src, dst, sls.at[i]) for i, (src, dst) in enumerate(local)]
    for copy in local:
        copy.start()
    for i, ref in enumerate(vectors):
        PRM[i : i + 1, :] = row(ref)
    PRM[12:13, 0:384] = row(sqb)
    PRM[12:13, 384:768] = row(svb)
    SM[...] = jnp.zeros(SM.shape, F32)

    @pl.when(owner)
    def _():
        lens_copy.wait_send()

    @pl.when(jnp.logical_not(owner))
    def _():
        lens_copy.wait_recv()

    n_keys = X.shape[0]
    position = lax.broadcasted_iota(jnp.int32, (8, n_keys), 1).astype(F32)
    length = jnp.where(owner, LN[0], LN[1])
    bias_row[...] = jnp.where(position < length[:, 0:1], 0.0, MASKED)
    s_bias = pl.ds(pl.multiple_of(c * 256, 128), 128)
    v_bias = pl.ds(pl.multiple_of(384 + c * 256, 128), 128)

    teacher = Layer(
        x=X, wq=WQ, wk=WK, wv=WV, wo=WO, wi=WI, wf=WF, q=q, k=k, v=v, o=o, p=p, xh1=xh1, rs1=rs1, a=a, g=g, gp=gp,
        xh2=xh2, rs2=rs2, df=df, dr=dr, do=do, dq=dq, dk=dk, dv=dv, ds=ds, prow=0, qrow=12, brow=16,
        width=192, flip_attn=True, flip_in=False,
        bias_q=lambda u: BP[2 * c + u, 0:1, 0:192],
        bias_v=lambda u: BP[2 * c + u, 3:4, 0:192],
        bias_i=lambda j: BP[j, 1:2, :],
        third=lambda c: 0, pack=None,
    )
    student = Layer(
        x=x2, wq=wsq, wk=wsk, wv=wsv, wo=wso, wi=SI, wf=SF, q=q2, k=k2, v=v2, o=o2, p=p2, xh1=xh12, rs1=rs12, a=a2,
        g=g2, gp=gp2, xh2=xh22, rs2=rs22, df=df, dr=dr, do=do, dq=dq, dk=dk, dv=dv, ds=ds, prow=6, qrow=24, brow=20,
        width=256, flip_attn=False, flip_in=True,
        bias_q=lambda u: jnp.concatenate([PRM[12:13, s_bias], PRM[12:13, 128:256]], axis=1),
        bias_v=lambda u: jnp.concatenate([PRM[12:13, v_bias], PRM[12:13, 512:640]], axis=1),
        bias_i=lambda j: BP[j, 2:3, 0 : SI.shape[1]],
        third=lambda c: c, pack=lambda: pack_student(),
    )
    swap = Swap(me, send, recv, ssem, rsem, 4)
    far_half, near_half = rows_of(1 - c, 384), rows_of(c, 384)
    half_copy = remote(BX.at[:, far_half], RBX, hcs.at[0], hcr.at[0], me.core())

    def pack_student():
        x = x2[...]
        for i, grad in enumerate((dq, dk, dv)):
            value = tn(x, grad[0]).astype(BF)
            SG[i, 0:768] = value[:, 0:128]
            BX[i] = value[:, 128:256]
        value = tn(o2[0], dr[...]).astype(BF)
        for b in range(6):
            cols = slice(128 * b, 128 * b + 128)
            SG[3, 128 * b : 128 * b + 128] = value[0:128, cols]
            for h in range(2):
                BX[3, 384 * h + 64 * b : 384 * h + 64 * b + 64] = value[128 + 64 * h : 192 + 64 * h, cols]
        half_copy.start()

    def join_halves():
        half_copy.wait()
        SG[:, 768:1152] = (BX[:, near_half].astype(F32) + RBX[...].astype(F32)).astype(BF)

    def teacher_hook(name):
        if name == "qkv":
            gather.advance(3)
            sequences.send(0)
            gather.advance(6)
            sequences.take(0)
            gather.advance(7)
            for copy in pack_copies:
                copy.wait()
            for copy in local:
                copy.wait()
            gather.ready((0, 1, 2))
        if name == "heads":
            gather.advance(7)
        if name == "middle":
            gather.advance(9)
        if name == "attn":
            gather.advance(10)
            gather.ready((3,))
            sequences.send(1)
        if name == "ffn_in":
            gather.advance(11)
            gather.ready((4,))
        if name == "ffn_out":
            gather.advance(12)
            gather.ready((5,))

    def student_hook(name):
        if name == "qkv":
            gather.advance(13)
        if name == "ffn_in":
            gather.ready((6,))
        if name == "ffn_out":
            gather.ready((7,))
            sequences.take(1)

    def to_student(rows, value):
        x2[rows] = value.astype(BF)

    def to_output(rows, value):
        Y[rows] = value.astype(BF)

    def between(rows, value):
        dx2[rows] = value

    def to_grad(rows, value):
        DX[rows] = value.astype(BF)

    forward(teacher, me, swap, bias_row, PRM, teacher_hook, to_student)
    forward(student, me, swap, bias_row, PRM, student_hook, to_output)
    home.send(0)
    gather.drain(range(8))
    sequences.drain(0)
    sequences.drain(1)

    low, high = pl.ds(0, WF.shape[1] // 2), pl.ds(WF.shape[1] // 2, WF.shape[1] // 2)
    top, bottom = pl.ds(0, 384), pl.ds(384, 384)
    grads = [SF, SI, SG, WF.at[:, low], WF.at[:, high], WI.at[:, top], WI.at[:, bottom], WQ, WK, WV, WO]
    lands = [outs[7], outs[6], outs[8], outs[5].at[low], outs[5].at[high], outs[4].at[top], outs[4].at[bottom],
             outs[0], outs[1], outs[2], outs[3]]
    total = Reduce(
        me, grads, lands, KINDS, ((0,), (1,), (2,), (3,), (4,), (5,), (6,), (10,), (7, 8), (9,)), bufs, reduce_sems
    )
    AHEAD = 2

    def student_back(name):
        if name == "out_grads":
            total.ready(1, AHEAD)
        if name == "ffn_grads":
            total.ready(2, AHEAD)

    def teacher_back(name):
        if name == "start":
            join_halves()
            total.ready(3, 3)
            total.step(AHEAD)
        if name == "out_grads":
            total.ready(5, 3)
        if name == "ffn_grads":
            total.ready(7, 3)
        if name == "attn":
            total.step(AHEAD)
        if name == "heads_done":
            total.step(AHEAD)
            total.step(AHEAD)
        if name == "attn_grads":
            total.ready(10, AHEAD)

    backward(student, me, swap, PRM, SM, lambda rows: CT[rows].astype(F32), student_back, between)
    backward(teacher, me, swap, PRM, SM, lambda rows: dx2[rows], teacher_back, to_grad)
    home.send(1)

    sml[0] = SM[...].astype(BF)
    for d in (1, 2, 3):
        remote(sml.at[0], sml.at[d], sms.at[d - 1], smr.at[d - 1], me.line(d)).start()
    total.step(AHEAD)
    for d in (1, 2, 3):
        remote(sml.at[0], sml.at[d], sms.at[d - 1], smr.at[d - 1], me.line(d)).wait()
    sml[4] = add_up([sml.at[i] for i in range(4)]).astype(BF)
    for k in (1, 2, 3):
        remote(sml.at[4], sml.at[4 + k], sms.at[2 + k], smr.at[2 + k], me.plane(k)).start()
    total.step(AHEAD)
    for k in (1, 2, 3):
        remote(sml.at[4], sml.at[4 + k], sms.at[2 + k], smr.at[2 + k], me.plane(k)).wait()
    both[0] = add_up([sml.at[4 + i] for i in range(4)])
    other_sums = remote(both.at[0], both.at[1], sms.at[6], smr.at[6], me.core())
    other_sums.start()
    total.step(AHEAD)
    other_sums.wait()
    both_sums = pltpu.make_async_copy(both, SUMS, sls.at[9])
    both_sums.start()
    total.rest(AHEAD)
    total.end()
    home.drain(0)
    home.drain(1)
    both_sums.wait()


def final_kernel(*refs):
    z = lax.axis_index("head")
    c = lax.rem(lax.axis_index("seq"), 2)
    YO, DO, SUMS = refs[:3]
    grads = refs[3:12]
    outs = refs[12:]
    outs[0][...] = YO[...].astype(F32)
    outs[1][...] = DO[...].astype(F32)
    for at, w in ((2, 0), (4, 1), (5, 2), (7, 3), (11, 4), (13, 5), (26, 6), (28, 7)):
        outs[at][...] = grads[w][...].astype(F32)
    near = pl.ds(pl.multiple_of(c * 256, 128), 128)
    far = pl.ds(pl.multiple_of((1 - c) * 256, 128), 128)
    packed = grads[8]
    for i, at in enumerate((17, 19, 20)):
        for side, cols, half in ((0, near, c), (1, far, 1 - c)):
            outs[at][:, cols] = packed[side, i, 0:768].astype(F32)
            outs[at][rows_of(half, 384), 128:256] = packed[side, i, 768:1152].astype(F32)
    for side, first, half in ((0, near, c), (1, far, 1 - c)):
        for b in range(6):
            cols = pl.ds(128 * b, 128)
            outs[22][first, cols] = packed[side, 3, 128 * b : 128 * b + 128].astype(F32)
            outs[22][pl.ds(128 + 64 * half, 64), cols] = packed[side, 3, 768 + 64 * b : 832 + 64 * b].astype(F32)

    def put(at, value):
        outs[at][...] = value.reshape(value.shape[1])

    for i, at in enumerate((8, 9, 10, 14, 15, 16, 23, 24, 25, 29, 30, 31)):
        put(at, SUMS[0, i : i + 1, :])
    side = jnp.where(z // 2 == c, 0, 1)
    put(3, SUMS[side, pl.ds(12 + z % 2, 1), 0:192])
    put(6, SUMS[side, pl.ds(14 + z % 2, 1), 0:192])
    put(12, SUMS[0, pl.ds(16 + z, 1), 0 : outs[12].shape[0]])
    put(27, SUMS[0, pl.ds(20 + z, 1), 0 : outs[27].shape[0]])
    for at, r in ((18, 24), (21, 25)):
        low = jnp.where(c == 0, SUMS[0, r : r + 1, 0:128], SUMS[1, r : r + 1, 0:128])
        high = jnp.where(c == 0, SUMS[1, r : r + 1, 0:128], SUMS[0, r : r + 1, 0:128])
        middle = SUMS[0, r : r + 1, 128:256] + SUMS[1, r : r + 1, 128:256]
        put(at, jnp.concatenate([low, middle, high], axis=1))


ANYWHERE = pl.BlockSpec(memory_space=pl.ANY)
IN_VMEM = pl.BlockSpec(memory_space=pltpu.VMEM)


def shape(*dims, kind=BF):
    return jax.ShapeDtypeStruct(dims, kind)


def body(
    tokens, lengths, cotangent,
    t_query, t_query_bias, t_key, t_value, t_value_bias, t_attn_out, t_attn_bias, t_norm1_gain, t_norm1_bias,
    t_ffn_in, t_ffn_in_bias, t_ffn_out, t_ffn_out_bias, t_norm2_gain, t_norm2_bias,
    s_query, s_query_bias, s_key, s_value, s_value_bias, s_attn_out, s_attn_bias, s_norm1_gain, s_norm1_bias,
    s_ffn_in, s_ffn_in_bias, s_ffn_out, s_ffn_out_bias, s_norm2_gain, s_norm2_bias,
):
    seq_size = lax.axis_size("seq")
    outer = seq_size // 2
    groups = [[2 * y + core for y in range(outer)] for core in range(2)]

    def widen(value, axis):
        if outer == 1:
            return value
        return lax.all_gather(value, "seq", axis=axis, tiled=True, axis_index_groups=groups)

    t_ffn_in, t_ffn_in_bias, t_ffn_out = widen(t_ffn_in, 1), widen(t_ffn_in_bias, 0), widen(t_ffn_out, 0)
    s_ffn_in, s_ffn_in_bias, s_ffn_out = widen(s_ffn_in, 1), widen(s_ffn_in_bias, 0), widen(s_ffn_out, 0)
    n_in, n_s = t_ffn_in.shape[1], s_ffn_in.shape[1]
    n = 4 * tokens.shape[1]

    dma = pltpu.SemaphoreType.DMA
    act = lambda *dims, kind=BF: pltpu.VMEM(dims, kind)
    wide = lambda *dims: pltpu.VMEM(dims, F32)
    weights = [
        (2, 192, 768), (2, 192, 768), (2, 192, 768), (2, 192, 768),
        (4, 768, n_in), (4, n_in, 768), (4, n_s, 768), (4, n_s, 768),
        (1, 768, 256), (1, 768, 256), (1, 768, 256), (1, 256, 768),
    ]
    names = len(weights)

    parts = [weights[7], weights[6], (4, 1152, 128), (4, n_in // 2, 768), (4, n_in // 2, 768), (4, 384, n_in), (4, 384, n_in),
             weights[0], weights[1], weights[2], weights[3]]
    pieces = [piece_shape(dims) for dims in parts]
    many = len(parts)

    results = pl.pallas_call(
        main_kernel,
        out_shape=[shape(2, 128, 768), shape(2, 128, 768), shape(2, 32, 768, kind=F32)]
        + [shape(*d[1:]) for d in weights[:8]]
        + [shape(2, 4, 1152, 128)],
        in_specs=[pl.BlockSpec(memory_space=pltpu.SMEM)] + [ANYWHERE] * 14 + [IN_VMEM] * 18,
        out_specs=[ANYWHERE] * 12,
        scratch_shapes=[act(*d) for d in weights]
        + [
            act(n, 768), act(n, 768), wide(2, 8, 128), wide(8, n_in), wide(4, 8, n_in), wide(16, 768), wide(32, 768), act(8, 32, 768), wide(2, 32, 768),
            act(4, 1152, 128), act(4, 768, 128), act(4, 384, 128),
            wide(8, n), act(2, n, 768), act(2, n, 768), dma((2, 4)), dma((2, 4)),
            act(2, n, 256), act(2, n, 256), act(2, n, 256), act(2, n, 256), act(6, n, n),
            wide(n, 768), wide(n, 1), act(n, 768), act(4, n, n_in), act(4, n, n_in), wide(n, 768), wide(n, 1),
            wide(n, 768), act(n, 768), act(2, n, 256), act(2, n, 256), act(2, n, 256), act(2, n, 256), act(n, n),
            act(n, 768), act(1, n, 256), act(1, n, 256), act(1, n, 256), act(1, n, 256), act(3, n, n),
            wide(n, 768), wide(n, 1), act(n, 768), act(4, n, n_s), act(4, n, n_s), wide(n, 768), wide(n, 1),
            wide(n, 768), act(n, 768), act(n, 768),
        ]
        + [act(2, *p) for p in pieces]
        + [act(2, *p) for p in pieces]
        + [act(*p) for p in pieces]
        + [act(*p) for p in pieces]
        + [act(3, dims[1] // 4, dims[2]) for dims in parts]
        + [act(4, 288, 128) if kind == EVERY else act(d[1] // 4, d[2]) for d, kind in zip(parts, KINDS)]
        + [
            dma((8, 3)), dma((8, 3)), dma((8, 3, 2)), dma((8, 3, 2)), dma((8, 3, 2)), dma((8, 3, 2)), dma((8,)), dma((8,)),
            dma((many, 4)), dma((many, 4)), dma((many, 2)), dma((many, 2)), dma((many, 3)), dma((many, 3)),
            dma((many, 2)), dma((many, 2)), dma((many, 2)), dma((many, 2)), dma((many,)), dma((many,)), dma((many,)),
            dma((many, 3)), dma((many, 3)),
            dma((2, 2)), dma((2, 4)), dma((2, 4)), dma((2, 4)), dma((2, 3)), dma((2, 2)),
            dma((3,)), dma((3,)), dma((1,)), dma((1,)), dma((10,)), dma((7,)), dma((7,)), dma((1,)), dma((1,)),
        ],
        compiler_params=pltpu.CompilerParams(collective_id=0, has_side_effects=True, vmem_limit_bytes=VMEM_LIMIT),
        name="layers",
    )(
        lengths, tokens, cotangent, t_query.T, t_key.T, t_value.T, t_attn_out, t_ffn_in, t_ffn_out, s_ffn_in.T, s_ffn_out,
        s_query, s_key, s_value, s_attn_out,
        t_attn_bias, t_norm1_gain, t_norm1_bias, t_ffn_out_bias, t_norm2_gain, t_norm2_bias,
        s_attn_bias, s_norm1_gain, s_norm1_bias, s_ffn_out_bias, s_norm2_gain, s_norm2_bias,
        s_query_bias, s_value_bias, t_query_bias, t_value_bias, t_ffn_in_bias, s_ffn_in_bias,
    )
    results = list(results)

    if outer > 1:
        results[2] = lax.psum(results[2], "seq", axis_index_groups=groups)
        results[3:] = [lax.psum(g.astype(F32), "seq", axis_index_groups=groups).astype(BF) for g in results[3:]]

    f = functools.partial(shape, kind=F32)
    final_shapes = [
        f(2, 128, 768), f(2, 128, 768),
        f(192, 768), f(192), f(192, 768), f(192, 768), f(192), f(192, 768),
        f(768), f(768), f(768), f(768, n_in), f(n_in), f(n_in, 768), f(768), f(768), f(768),
        f(768, 384), f(384), f(768, 384), f(768, 384), f(384), f(384, 768),
        f(768), f(768), f(768), f(n_s, 768), f(n_s), f(n_s, 768), f(768), f(768), f(768),
    ]
    outs = list(
        pl.pallas_call(
            final_kernel,
            out_shape=final_shapes,
            in_specs=[IN_VMEM] * 12,
            out_specs=[IN_VMEM] * len(final_shapes),
            compiler_params=pltpu.CompilerParams(vmem_limit_bytes=VMEM_LIMIT),
            name="final",
        )(*results)
    )
    for i in (2, 4, 5, 26):
        outs[i] = outs[i].T
    if outer > 1:
        y = lax.axis_index("seq") // 2
        for i, axis in ((11, 1), (12, 0), (13, 0), (26, 1), (27, 0), (28, 0)):
            width = outs[i].shape[axis] // outer
            outs[i] = lax.dynamic_slice_in_dim(outs[i], y * width, width, axis)
    return tuple(outs)


def solution(mesh):
    seqs = P(("row", "seq"), "head", None)
    col, line, row_spec = P(None, "head"), P("head"), P("head", None)
    fcol, fline, frow = P(None, ("head", "seq")), P(("head", "seq")), P(("head", "seq"), None)
    rep = P()
    teacher = (col, line, col, col, line, row_spec, rep, rep, rep, fcol, fline, frow, rep, rep, rep)
    student = (rep,) * 9 + (fcol, fline, frow, rep, rep, rep)
    return jax.shard_map(
        body,
        mesh=mesh,
        in_specs=(seqs, P(("row", "seq")), seqs) + teacher + student,
        out_specs=(seqs, seqs) + teacher + student,
        check_vma=False,
    )
```

```python
import functools

import jax
import jax.numpy as jnp
from jax import lax
from jax.experimental import pallas as pl
from jax.experimental.pallas import tpu as pltpu
from jax.sharding import PartitionSpec as P

MESH = pl.DeviceIdType.MESH
F32 = jnp.float32
BF = jnp.bfloat16
EPS = 1e-5
MASKED = -1000000000.0
VMEM_LIMIT = 63 << 20


class Place:
    def __init__(self):
        self.r = lax.axis_index("row")
        self.z = lax.axis_index("head")
        self.s = lax.axis_index("seq")
        self.c = lax.rem(self.s, 2)

    def core(self):
        return (self.r, self.z, self.s + 1 - 2 * self.c)

    def line_index(self, step):
        return lax.rem(self.z + step + 4, 4)

    def line(self, step):
        return (self.r, self.line_index(step), self.s)

    def plane_index(self, k):
        if k == 1:
            return self.r + 1 - 2 * lax.rem(self.r, 2)
        if k == 2:
            return lax.rem(self.r + 2, 4)
        return 3 - self.r

    def plane(self, k):
        return (self.plane_index(k), self.z, self.s)


def greet(me):
    barrier = pltpu.get_barrier_semaphore()
    others = [me.core()] + [me.line(i) for i in (1, 2, 3)] + [me.plane(k) for k in (1, 2, 3)]
    for other in others:
        pl.semaphore_signal(barrier, inc=1, device_id=other, device_id_type=MESH)
    pl.semaphore_wait(barrier, len(others))


def remote(src, dst, send_sem, recv_sem, device):
    return pltpu.make_async_remote_copy(
        src_ref=src, dst_ref=dst, send_sem=send_sem, recv_sem=recv_sem, device_id=device, device_id_type=MESH
    )


def rows_of(index, count, unit=16):
    return pl.ds(pl.multiple_of(index * count, unit), count)


class Gather:
    def __init__(self, me, shards, sems):
        self.me, self.shards = me, shards
        self.zs, self.zr, self.ps, self.pr, self.fs, self.fr, self.ls, self.hs = sems
        self.inner = jnp.logical_and(me.z >= 1, me.z <= 2)
        self.across = {1: me.z != 3, 2: me.z >= 0, 3: me.z != 0}

    def only(self, w, cond):
        return (lambda f: pl.when(cond)(f)) if self.shards[w][2] == 2 else (lambda f: f())

    def slot(self, w, index):
        return index % 2 if self.shards[w][2] == 2 else index

    def quarter(self, w, r):
        return rows_of(r, self.shards[w][0].shape[0] // 4)

    def part(self, w, frm, r, half=None):
        dst = self.shards[w][1]
        count, cols = dst.shape[1] // 4, dst.shape[2]
        slot = self.slot(w, frm)
        if half is None:
            return dst.at[slot, rows_of(r, count)]
        if cols == 768:
            return dst.at[slot, rows_of(r, count), pl.ds(half * 384, 384)]
        return dst.at[slot, rows_of(2 * r + half, count // 2)]

    def begin(self, parts, ahead):
        me = self.me
        self.parts, self.ahead, self.turn = parts, ahead, 0
        for w, (src, dst, count) in enumerate(self.shards):

            @self.only(w, me.z // 2 == me.c)
            def _():
                pltpu.make_async_copy(src, dst.at[self.slot(w, me.z)], self.ls.at[w]).start()

        for i in range(ahead):
            self.send(i)

    def send(self, i):
        me = self.me
        if i >= len(self.parts):
            return
        for w, d in self.parts[i]:

            @self.only(w, me.z // 2 == me.c)
            def _():
                @pl.when(self.across[d])
                def _():
                    self.line_copy(w, d).start()

    def advance(self, until):
        while self.turn < until:
            i = self.turn
            if i < len(self.parts):
                self.to_plane(self.parts[i])
                self.send(i + self.ahead)
            if 0 <= i - 1 < len(self.parts):
                self.onward(self.parts[i - 1])
            self.turn += 1

    def line_copy(self, w, d):
        me = self.me
        return remote(
            self.shards[w][0].at[self.quarter(w, me.r)],
            self.part(w, me.z, me.r),
            self.zs.at[w, d - 1],
            self.zr.at[w, d - 1],
            me.line(d),
        )

    def end_copy(self, w):
        me = self.me
        ref = self.part(w, me.line_index(-2), me.r)
        return remote(ref, ref, self.hs.at[w], self.zr.at[w, jnp.clip(2 * me.z - 2, 0, 2)], (me.r, jnp.clip(3 * (me.z - 1), 0, 3), me.s))

    def plane_copy(self, w, d, k):
        me = self.me
        ref = self.part(w, me.line_index(-d), me.r)
        return remote(ref, ref, self.ps.at[w, d - 1, k - 1], self.pr.at[w, d - 1, k - 1], me.plane(k))

    def on_copy(self, w, d, k):
        me = self.me
        ref = self.part(w, me.line_index(-d), me.plane_index(3 - k), k - 1)
        return remote(ref, ref, self.fs.at[w, d - 1, k - 1], self.fr.at[w, d - 1, k - 1], me.plane(k))

    def each(self, part, step):
        for w, d in part:

            @self.only(w, self.me.line_index(-d) // 2 == self.me.c)
            def _():
                step(w, d)

    def to_plane(self, ws):
        def step(w, d):
            self.line_copy(w, d).wait_recv()
            if d == 2:

                @pl.when(self.inner)
                def _():
                    self.end_copy(w).start()

            self.plane_copy(w, d, 1).start()
            self.plane_copy(w, d, 2).start()

        self.each(ws, step)

    def onward(self, ws):
        def step(w, d):
            for k in (1, 2):
                self.plane_copy(w, d, k).wait_recv()
                self.on_copy(w, d, 3 - k).start()

        self.each(ws, step)

    def ready(self, ws):
        def step(w, d):
            for k in (1, 2):
                self.on_copy(w, d, k).wait_recv()

        self.each([(w, d) for w in ws for d in (1, 2, 3)], step)
        for w in ws:
            src, dst, count = self.shards[w]

            @self.only(w, self.me.z // 2 == self.me.c)
            def _():
                pltpu.make_async_copy(src, dst.at[0], self.ls.at[w]).wait()

    def drain(self, ws):
        def step(w, d):
            if d == 2:

                @pl.when(self.inner)
                def _():
                    self.end_copy(w).wait_send()

            for k in (1, 2):
                self.plane_copy(w, d, k).wait_send()
                self.on_copy(w, d, k).wait_send()

        self.each([(w, d) for w in ws for d in (1, 2, 3)], step)
        for w in ws:

            @self.only(w, self.me.z // 2 == self.me.c)
            def _():
                for d in (1, 2, 3):

                    @pl.when(self.across[d])
                    def _():
                        self.line_copy(w, d).wait_send()


PAIR, OWNER, EVERY = 0, 1, 2
KINDS = (OWNER,) * 2 + (EVERY,) + (OWNER,) * 4 + (PAIR,) * 4


def piece_shape(dims):
    count, rows, cols = dims
    return (count, rows // 4, cols // 2) if cols == 768 else (count, rows // 8, cols)


class Reduce:
    def __init__(self, me, grads, outs, kinds, chunks, bufs, sems):
        self.me, self.grads, self.outs, self.kinds, self.chunks = me, grads, outs, kinds, chunks
        self.RA, self.RB, self.RC, self.RD, self.RZ, self.SUM = bufs
        (self.as_, self.ar, self.bs, self.br, self.zs, self.zr, self.gs, self.gr, self.fs, self.fr, self.ls,
         self.cs, self.cr, self.ns, self.nr) = sems
        self.mx, self.my = lax.rem(me.r, 2), me.r // 2
        self.owner = me.z // 2 == me.c
        self.made = self.launched = self.turn = 0

    def quarter(self, w):
        return self.grads[w].shape[1] // 4

    def piece(self, w, t, half):
        g = self.grads[w]
        q, cols = self.quarter(w), g.shape[2]
        if cols == 768:
            return g.at[:, rows_of(t, q), pl.ds(half * 384, 384)]
        return g.at[:, rows_of(2 * t + half, q // 2)]

    def first_copy(self, w, half, other):
        if half == 0:
            t, k, land = 2 * other + 1 - self.mx, 1, self.RA
        else:
            t, k, land = 2 * (1 - self.my) + other, 2, self.RB
        i = 2 * half + other
        return remote(
            self.piece(w, t, half), land[w].at[other], self.as_.at[w, i], self.ar.at[w, i], self.me.plane(k)
        )

    def start(self, ws):
        for w in ws:
            for other in (0, 1):
                for half in (0, 1):
                    self.first_copy(w, half, other).start()

    def kept(self, w, half, other):
        t = 2 * other + self.mx if half == 0 else 2 * self.my + other
        return self.piece(w, t, half)

    def second_copy(self, w, half):
        if half == 0:
            return remote(
                self.piece(w, 2 * (1 - self.my) + self.mx, 0), self.RC[w], self.bs.at[w, 0], self.br.at[w, 0], self.me.plane(2)
            )
        return remote(
            self.piece(w, 2 * self.my + 1 - self.mx, 1), self.RD[w], self.bs.at[w, 1], self.br.at[w, 1], self.me.plane(1)
        )

    def add_into(self, target, ref):
        target[...] = (target[...].astype(F32) + ref[...].astype(F32)).astype(BF)

    def second(self, ws):
        for w in ws:
            for other in (0, 1):
                for half in (0, 1):
                    self.first_copy(w, half, other).wait()
            for half, land in ((0, self.RA), (1, self.RB)):

                @pl.loop(0, 2)
                def _(other):
                    self.add_into(self.kept(w, half, other), land[w].at[other])

                self.second_copy(w, half).start()

    def along(self, ws):
        me = self.me
        for w in ws:
            for half, land in ((0, self.RC), (1, self.RD)):
                self.second_copy(w, half).wait()
                self.add_into(self.piece(w, me.r, half), land[w])
            if self.kinds[w] == PAIR:
                for u in range(2):

                    @pl.when(2 * me.c + u != me.z)
                    def _():
                        self.unit_copy(w, u).start()

            else:
                for d in (1, 2, 3):
                    self.line_copy(w, d).start()

    def unit_copy(self, w, u):
        me = self.me
        target = 2 * me.c + u
        slot = lax.rem(target - me.z + 3, 4)
        slot = jnp.minimum(slot, 2)
        return remote(
            self.grads[w].at[u, rows_of(me.r, self.quarter(w))],
            self.RZ[w].at[slot],
            self.zs.at[w, u],
            self.zr.at[w, slot],
            (me.r, target, me.s),
        )

    def line_copy(self, w, d):
        me = self.me
        q = self.quarter(w)
        src = self.grads[w].at[me.line_index(d), rows_of(me.r, q)]
        return remote(src, self.RZ[w].at[d - 1], self.zs.at[w, d - 1], self.zr.at[w, d - 1], me.line(d))

    def near_copy(self, w, d):
        mine = self.SUM[w].at[self.me.z]
        return remote(mine, mine, self.ns.at[w, d - 1], self.nr.at[w, d - 1], self.me.line(d))

    def out_part(self, w, t, half=None):
        out, q = self.outs[w], self.quarter(w)
        if self.kinds[w] == EVERY:
            rows = rows_of(t, q) if half is None else rows_of(2 * t + half, q // 2)
            return out.at[0, :, rows]
        if half is None:
            return out.at[rows_of(t, q)]
        if out.shape[1] == 768:
            return out.at[rows_of(t, q), pl.ds(half * 384, 384)]
        return out.at[rows_of(2 * t + half, q // 2)]

    def plane_copy(self, w, k):
        me = self.me
        return remote(self.SUM[w], self.out_part(w, me.r), self.gs.at[w, k - 1], self.gr.at[w, k - 1], me.plane(k))

    def on_copy(self, w, k):
        ref = self.out_part(w, self.me.plane_index(3 - k), k - 1)
        return remote(ref, ref, self.fs.at[w, k - 1], self.fr.at[w, k - 1], self.me.plane(k))

    def own_copy(self, w):
        return pltpu.make_async_copy(self.SUM[w], self.out_part(w, self.me.r), self.ls.at[w])

    def core_copy(self, w):
        if self.kinds[w] == EVERY:
            return remote(self.outs[w].at[0], self.outs[w].at[1], self.cs.at[w], self.cr.at[w], self.me.core())
        return remote(self.outs[w], self.outs[w], self.cs.at[w], self.cr.at[w], self.me.core())

    def only(self, w):
        return (lambda f: pl.when(self.owner)(f)) if self.kinds[w] == PAIR else (lambda f: f())

    def spread_start(self, w):
        self.own_copy(w).start()
        self.plane_copy(w, 1).start()
        self.plane_copy(w, 2).start()

    def spread(self, ws):
        me = self.me
        for w in ws:
            q = self.quarter(w)
            kind = self.kinds[w]
            if kind == PAIR:
                for u in range(2):

                    @pl.when(2 * me.c + u != me.z)
                    def _():
                        self.unit_copy(w, u).wait_send()

                @pl.when(self.owner)
                def _():
                    for d in (1, 2, 3):
                        remote(self.RZ[w].at[0], self.RZ[w].at[d - 1], self.zs.at[w, 0], self.zr.at[w, d - 1], me.core()).wait_recv()
                    own = self.grads[w].at[me.z % 2, rows_of(me.r, q)]
                    self.SUM[w][...] = add_up([own] + [self.RZ[w].at[d] for d in range(3)]).astype(BF)
                    self.spread_start(w)

                continue
            for d in (1, 2, 3):
                self.line_copy(w, d).wait()
            own = self.grads[w].at[me.z, rows_of(me.r, q)]
            total = add_up([own] + [self.RZ[w].at[d] for d in range(3)]).astype(BF)
            if kind == EVERY:
                self.SUM[w][me.z] = total
                for d in (1, 2, 3):
                    self.near_copy(w, d).start()
            else:
                self.SUM[w][...] = total
                self.spread_start(w)

    def spread_near(self, ws):
        for w in ws:
            for d in (1, 2, 3):
                self.near_copy(w, d).wait()
            self.spread_start(w)

    def onward(self, ws):
        for w in ws:

            @self.only(w)
            def _():
                for k in (1, 2):
                    self.plane_copy(w, k).wait()
                    self.on_copy(w, 3 - k).start()

    def finish(self, ws):
        for w in ws:

            @self.only(w)
            def _():
                self.own_copy(w).wait()
                for k in (1, 2):
                    self.on_copy(w, k).wait()
                if self.kinds[w] != OWNER:
                    self.core_copy(w).start()

    def end(self):
        for w, kind in enumerate(self.kinds):
            if kind == PAIR:

                @pl.when(self.owner)
                def _():
                    self.core_copy(w).wait_send()

                @pl.when(jnp.logical_not(self.owner))
                def _():
                    self.core_copy(w).wait_recv()

            elif kind == EVERY:
                self.core_copy(w).wait()

    def launch(self, upto):
        while self.launched < min(upto, self.made, len(self.chunks)):
            self.start(self.chunks[self.launched])
            self.launched += 1

    def ready(self, made, ahead):
        self.made = made
        self.launch(self.turn + ahead)

    def step(self, ahead):
        i = self.turn
        if self.made <= i < len(self.chunks):
            return

        def at(back, every=None):
            chunk = self.chunks[i - back] if 0 <= i - back < len(self.chunks) else ()
            return [w for w in chunk if every is None or every == (self.kinds[w] == EVERY)]

        self.second(at(0))
        self.turn += 1
        self.launch(self.turn + ahead)
        self.along(at(1))
        self.spread(at(2))
        self.spread_near(at(3, True))
        self.onward(at(3, False) + at(4, True))
        self.finish(at(4, False) + at(5, True))

    def rest(self, ahead):
        while self.turn < len(self.chunks) + 4:
            self.step(ahead)


def add_up(refs):
    total = refs[0][...].astype(F32)
    for ref in refs[1:]:
        total = total + ref[...].astype(F32)
    return total


def nn(a, b):
    return lax.dot_general(a, b, (((1,), (0,)), ((), ())), preferred_element_type=F32)


def nt(a, b):
    return lax.dot_general(a, b, (((1,), (1,)), ((), ())), preferred_element_type=F32)


def tn(a, b):
    return lax.dot_general(a, b, (((0,), (0,)), ((), ())), preferred_element_type=F32)


def norm_parts(value):
    center = value - jnp.mean(value, axis=-1, keepdims=True)
    spread = jnp.mean(center * center, axis=-1, keepdims=True)
    rstd = lax.rsqrt(spread + EPS)
    return center * rstd, rstd


def norm_grad(xh, rstd, gain, dy):
    scaled = dy * gain
    mean_one = jnp.mean(scaled, axis=-1, keepdims=True)
    mean_two = jnp.mean(scaled * xh, axis=-1, keepdims=True)
    return (scaled - mean_one - xh * mean_two) * rstd


def col_sum(value):
    return jnp.sum(value, axis=0, keepdims=True)


class Swap:
    def __init__(self, me, send, recv, ssem, rsem, chunks):
        self.me, self.send, self.recv, self.ssem, self.rsem = me, send, recv, ssem, rsem
        self.rows = send.shape[1] // chunks
        self.chunks = chunks
        self.turn = 0

    def copy(self, slot, i):
        rows = rows_of(i, self.rows)
        return remote(
            self.send.at[slot, rows],
            self.recv.at[slot, rows],
            self.ssem.at[slot, i],
            self.rsem.at[slot, i],
            self.me.core(),
        )

    def run(self, part, between, post):
        slot = self.turn % 2
        self.turn += 1

        @pl.loop(0, self.chunks)
        def _(i):
            rows = rows_of(i, self.rows)
            self.send[slot, rows] = part(rows).astype(BF)
            self.copy(slot, i).start()

        if between is not None:
            between()

        @pl.loop(0, self.chunks)
        def _(i):
            rows = rows_of(i, self.rows)
            self.copy(slot, i).wait()
            total = self.send[slot, rows].astype(F32) + self.recv[slot, rows].astype(F32)
            post(i, rows, total)


class Layer:
    def __init__(self, **kw):
        self.__dict__.update(kw)


def head_mask(layer, i, c):
    h = lax.rem(i, 3)
    half = jnp.where(h == 2, layer.third(c), lax.rem(h, 2))
    lane = lax.broadcasted_iota(jnp.int32, (1, 128), 1) // 64
    mask = jnp.where(lane == half, 1.0, 0.0).astype(BF)
    return i // 3, pl.ds(pl.multiple_of((h // 2) * 128, 128), 128), mask


def forward(layer, me, swap, bias_row, prm, hook, done):
    L, c = layer, me.c
    units = L.q.shape[0]

    hook("qkv")
    project = nt if L.flip_attn else nn

    @pl.loop(0, units)
    def _(u):
        x = L.x[...]
        n = L.width
        L.q[u, :, :n] = ((project(x, L.wq[u]) + L.bias_q(u)).astype(BF) * 0.125).astype(BF)
        L.k[u, :, :n] = project(x, L.wk[u]).astype(BF)
        L.v[u, :, :n] = (project(x, L.wv[u]) + L.bias_v(u)).astype(BF)
        if n < 256:
            pad = jnp.zeros((x.shape[0], 256 - n), BF)
            L.q[u, :, n:] = pad
            L.k[u, :, n:] = pad
            L.v[u, :, n:] = pad
        L.o[u] = jnp.zeros(L.o.shape[1:], BF)

    hook("heads")

    def heads(lo, hi):
        @pl.loop(lo, hi)
        def _(i):
            u, cols, mask = head_mask(L, i, c)
            k = L.k[u, :, cols]
            v = L.v[u, :, cols] * mask
            for ch in range(4):
                rows = pl.ds(ch * 128, 128)
                scores = nt(L.q[u, rows, cols] * mask, k) + bias_row[0:1, :]
                top = jnp.max(scores, axis=-1, keepdims=True)
                expo = jnp.exp(scores - top)
                inv = 1.0 / jnp.sum(expo, axis=-1, keepdims=True)
                probs = (expo * inv).astype(BF)
                L.p[i, rows] = probs
                L.o[u, rows, cols] = L.o[u, rows, cols] + nn(probs, v).astype(BF)

    heads(0, 3)
    if units == 2:
        hook("middle")
        heads(3, 6)
    hook("attn")

    def attn_part(rows):
        n = L.width
        total = nn(L.o[0, rows, :n], L.wo[0])
        for u in range(1, units):
            total = total + nn(L.o[u, rows, :n], L.wo[u])
        return total

    def attn_post(i, rows, total):
        value = L.x[rows].astype(F32) + total + prm[L.prow : L.prow + 1, :]
        xh, rstd = norm_parts(value)
        L.xh1[rows] = xh
        L.rs1[rows] = rstd
        L.a[rows] = (xh * prm[L.prow + 1 : L.prow + 2, :] + prm[L.prow + 2 : L.prow + 3, :]).astype(BF)

    swap.run(attn_part, None, attn_post)
    hook("ffn_in")
    enter = nt if L.flip_in else nn

    @pl.loop(0, 4)
    def _(j):
        pre = enter(L.a[...], L.wi[j]) + L.bias_i(j)
        sq = pre * pre
        t = jnp.tanh(0.7978845608028654 * pre * (1.0 + 0.044715 * sq))
        half = 0.5 * (1.0 + t)
        L.g[j] = (pre * half).astype(BF)
        slope = half + 0.5 * pre * (1.0 - t * t) * (0.7978845608028654 + 0.7978845608028654 * 0.134145 * sq)
        L.gp[j] = slope.astype(BF)

    hook("ffn_out")

    def ffn_part(rows):
        total = nn(L.g[0, rows], L.wf[0])
        for j in range(1, 4):
            total = total + nn(L.g[j, rows], L.wf[j])
        return total

    def ffn_post(i, rows, total):
        value = L.a[rows].astype(F32) + total + prm[L.prow + 3 : L.prow + 4, :]
        xh, rstd = norm_parts(value)
        L.xh2[rows] = xh
        L.rs2[rows] = rstd
        done(rows, xh * prm[L.prow + 4 : L.prow + 5, :] + prm[L.prow + 5 : L.prow + 6, :])

    swap.run(ffn_part, None, ffn_post)


def backward(layer, me, swap, prm, sums, upstream, hook, done):
    L, c = layer, me.c
    units = L.q.shape[0]
    prow = L.prow
    n_rows = L.x.shape[0]
    hook("start")
    for i in range(6):
        sums[prow + i : prow + i + 1, :] = jnp.zeros((1, 768), F32)

    @pl.loop(0, n_rows // 128)
    def _(i):
        rows = rows_of(i, 128)
        dy = upstream(rows)
        xh = L.xh2[rows]
        sums[prow + 4 : prow + 5, :] += col_sum(dy * xh)
        sums[prow + 5 : prow + 6, :] += col_sum(dy)
        df = norm_grad(xh, L.rs2[rows], prm[prow + 4 : prow + 5, :], dy)
        low = df.astype(BF)
        sums[prow + 3 : prow + 4, :] += col_sum(low.astype(F32))
        L.df[rows] = df
        L.dr[rows] = low

    @pl.loop(0, 4)
    def _(j):
        dpre = (nt(L.dr[...], L.wf[j]) * L.gp[j].astype(F32)).astype(BF)
        L.gp[j] = dpre
        n = dpre.shape[1]
        sums[pl.ds(L.brow + j, 1), :n] = col_sum(dpre.astype(F32))
        L.wf[j] = tn(L.g[j], L.dr[...]).astype(BF)

    hook("out_grads")
    leave = nn if L.flip_in else nt

    def ffn_part(rows):
        total = leave(L.gp[0, rows], L.wi[0])
        for j in range(1, 4):
            total = total + leave(L.gp[j, rows], L.wi[j])
        return total

    def ffn_weights():
        @pl.loop(0, 4)
        def _(j):
            if L.flip_in:
                L.wi[j] = tn(L.gp[j], L.a[...]).astype(BF)
            else:
                L.wi[j] = tn(L.a[...], L.gp[j]).astype(BF)

        hook("ffn_grads")

    def ffn_post(i, rows, total):
        da = L.df[rows] + total
        xh = L.xh1[rows]
        sums[prow + 1 : prow + 2, :] += col_sum(da * xh)
        sums[prow + 2 : prow + 3, :] += col_sum(da)
        dh = norm_grad(xh, L.rs1[rows], prm[prow + 1 : prow + 2, :], da)
        low = dh.astype(BF)
        sums[prow : prow + 1, :] += col_sum(low.astype(F32))
        L.df[rows] = dh
        L.dr[rows] = low

    swap.run(ffn_part, ffn_weights, ffn_post)
    hook("attn")

    @pl.loop(0, units)
    def _(u):
        n = L.width
        L.do[u, :, :n] = nt(L.dr[...], L.wo[u]).astype(BF)
        if n < 256:
            L.do[u, :, n:] = jnp.zeros((n_rows, 256 - n), BF)
        for ref in (L.dq, L.dk, L.dv):
            ref[u] = jnp.zeros(ref.shape[1:], BF)

    def heads(lo, hi):
        @pl.loop(lo, hi)
        def _(i):
            u, cols, mask = head_mask(L, i, c)
            k = L.k[u, :, cols] * mask
            v = L.v[u, :, cols]
            for ch in range(4):
                rows = pl.ds(ch * 128, 128)
                d_probs = nt(L.do[u, rows, cols] * mask, v)
                probs = L.p[i, rows].astype(F32)
                both = probs * d_probs
                d_scores = (both - probs * jnp.sum(both, axis=-1, keepdims=True)).astype(BF)
                L.ds[rows] = d_scores
                L.dq[u, rows, cols] = L.dq[u, rows, cols] + (nn(d_scores, k) * 0.125).astype(BF)
            L.dv[u, :, cols] = L.dv[u, :, cols] + tn(L.p[i], L.do[u, :, cols] * mask).astype(BF)
            L.dk[u, :, cols] = L.dk[u, :, cols] + tn(L.ds[...], L.q[u, :, cols] * mask).astype(BF)

    heads(0, 3)
    if units == 2:
        hook("middle")
        heads(3, 6)
    hook("heads_done")
    back = nn if L.flip_attn else nt

    def attn_part(rows):
        n = L.width
        total = None
        for u in range(units):
            for grad, weight in ((L.dq, L.wq), (L.dk, L.wk), (L.dv, L.wv)):
                term = back(grad[u, rows, :n], weight[u])
                total = term if total is None else total + term
        return total

    def attn_weights():
        if L.pack is not None:
            L.pack()
            sums[L.qrow : L.qrow + 1, :256] = col_sum(L.dq[0].astype(F32))
            sums[L.qrow + 1 : L.qrow + 2, :256] = col_sum(L.dv[0].astype(F32))
            hook("attn_grads")
            return

        @pl.loop(0, units)
        def _(u):
            n = L.width
            L.wo[u] = tn(L.o[u, :, :n], L.dr[...]).astype(BF)
            x = L.x[...]
            for grad, out in ((L.dq, L.wq), (L.dk, L.wk), (L.dv, L.wv)):
                out[u] = tn(grad[u, :, :n], x).astype(BF)
            sums[pl.ds(L.qrow + u, 1), :256] = col_sum(L.dq[u].astype(F32))
            sums[pl.ds(L.qrow + units + u, 1), :256] = col_sum(L.dv[u].astype(F32))

        hook("attn_grads")

    def attn_post(i, rows, total):
        done(rows, L.df[rows] + total)

    swap.run(attn_part, attn_weights, attn_post)


class Sequences:
    def __init__(self, me, pairs, sems):
        self.me, self.pairs = me, pairs
        self.xs, self.xr, self.fs, self.fr = sems
        self.owner = me.z // 2 == me.c

    def send(self, a):
        me = self.me
        src, dst = self.pairs[a]
        for j in range(2):
            target = 2 * me.c + j

            @pl.when(target != me.z)
            def _():
                remote(src.at[j], dst.at[rows_of(me.z, 128)], self.xs.at[a, j], self.xr.at[a, me.z], (me.r, target, me.s)).start()

            @pl.when(target == me.z)
            def _():
                pltpu.make_async_copy(src.at[j], dst.at[rows_of(me.z, 128)], self.xr.at[a, me.z]).start()

    def core_copy(self, a, frm, i):
        dst = self.pairs[a][1].at[rows_of(frm, 128)]
        return remote(dst, dst, self.fs.at[a, i], self.fr.at[a, frm], self.me.core())

    def take(self, a):
        me = self.me
        src, dst = self.pairs[a]

        @pl.when(self.owner)
        def _():
            pltpu.make_async_copy(src.at[0], dst.at[rows_of(me.z, 128)], self.xr.at[a, me.z]).wait()
            self.core_copy(a, me.z, 0).start()
            for d in (1, 2, 3):
                frm = me.line_index(-d)
                remote(src.at[0], dst.at[rows_of(frm, 128)], self.xs.at[a, 0], self.xr.at[a, frm], me.core()).wait_recv()
                self.core_copy(a, frm, d).start()

        @pl.when(jnp.logical_not(self.owner))
        def _():
            for i in range(4):
                self.core_copy(a, i, i).wait_recv()

    def drain(self, a):
        me = self.me
        src, dst = self.pairs[a]
        for j in range(2):

            @pl.when(2 * me.c + j != me.z)
            def _():
                remote(src.at[j], dst.at[rows_of(me.z, 128)], self.xs.at[a, j], self.xr.at[a, me.z], me.core()).wait_send()

        @pl.when(self.owner)
        def _():
            for i in range(4):
                self.core_copy(a, i, i).wait_send()


class Home:
    def __init__(self, me, pairs, sems):
        self.me, self.pairs = me, pairs
        self.ys, self.yr = sems
        self.owner = me.z // 2 == me.c

    def send(self, a):
        me = self.me
        src, dst = self.pairs[a]

        @pl.when(self.owner)
        def _():
            pltpu.make_async_copy(src.at[rows_of(me.z, 128)], dst.at[me.z % 2], self.yr.at[a, me.z % 2]).start()
            for d in (1, 2, 3):
                remote(
                    src.at[rows_of(me.line_index(d), 128)],
                    dst.at[me.z % 2],
                    self.ys.at[a, d - 1],
                    self.yr.at[a, me.z % 2],
                    me.line(d),
                ).start()

    def drain(self, a):
        me = self.me
        src, dst = self.pairs[a]

        @pl.when(self.owner)
        def _():
            for d in (1, 2, 3):
                remote(src.at[rows_of(0, 128)], dst.at[0], self.ys.at[a, d - 1], self.yr.at[a, 0], me.core()).wait_send()

        for j in range(2):
            chip = 2 * me.c + j

            @pl.when(chip == me.z)
            def _():
                pltpu.make_async_copy(src.at[rows_of(0, 128)], dst.at[j], self.yr.at[a, j]).wait()

            @pl.when(chip != me.z)
            def _():
                remote(src.at[rows_of(0, 128)], dst.at[j], self.ys.at[a, 0], self.yr.at[a, j], me.core()).wait_recv()


def row(ref):
    return ref[...].astype(F32).reshape(1, ref.shape[0])


def main_kernel(*refs):
    me = Place()
    z, c = me.z, me.c
    lens = refs[0]
    (tok, cot, tq, tk, tv, to, ti, tf, si, sf, SQ, SK, SV, SO) = refs[1:15]
    vectors = refs[15:27]
    sqb, svb, tqb, tvb, tib, sib = refs[27:33]
    (YO, DO, SUMS) = refs[33:36]
    outs = refs[36:45]
    rest = list(refs[45:])

    def take(count):
        head, rest[:] = rest[:count], rest[count:]
        return head

    WQ, WK, WV, WO, WI, WF, SI, SF, wsq, wsk, wsv, wso = weights = take(12)
    X, CT, LN, PACK, BP, PRM, SM, sml, both, SG, BX, RBX = take(12)
    bias_row, send, recv, ssem, rsem = take(5)
    q, k, v, o, p, xh1, rs1, a, g, gp, xh2, rs2, df, dr, do, dq, dk, dv, ds = take(19)
    x2, q2, k2, v2, o2, p2, xh12, rs12, a2, g2, gp2, xh22, rs22, dx2, Y, DX = take(16)
    bufs = [take(len(KINDS)) for _ in range(6)]
    gather_sems = take(8)
    reduce_sems = take(15)
    seq_sems, home_sems = take(4), take(2)
    pks, pkr, lcs, lcr, sls, sms, smr, hcs, hcr = take(9)

    LN[0] = jnp.full(LN.shape[1:], lens[z % 2].astype(F32))
    PACK[...] = jnp.zeros(PACK.shape, F32)
    PACK[0:1, 0:192] = row(tqb)
    PACK[1:2, :] = row(tib)
    PACK[2:3, 0 : sib.shape[0]] = row(sib)
    PACK[3:4, 0:192] = row(tvb)
    greet(me)
    owner = z // 2 == c

    sequences = Sequences(me, ((tok, X), (cot, CT)), seq_sems)
    home = Home(me, ((Y, YO), (DX, DO)), home_sems)
    gather = Gather(
        me,
        ((tq, WQ, 2), (tk, WK, 2), (tv, WV, 2), (to, WO, 2), (ti, WI, 4), (tf, WF, 4), (si, SI, 4), (sf, SF, 4)),
        gather_sems,
    )

    pack_copies = [remote(PACK, BP.at[z], pks.at[d - 1], pkr.at[d - 1], me.line(d)) for d in (1, 2, 3)]
    for copy in pack_copies:
        copy.start()
    far_first = (2, 1, 3)
    gather.begin(
        [[(w, d) for d in far_first] for w in (0, 1, 2, 3)]
        + [[(4, d)] for d in far_first]
        + [[(5, d)] for d in far_first]
        + [[(w, d) for d in far_first] for w in (6, 7)],
        3,
    )
    lens_copy = remote(LN.at[0], LN.at[1], lcs.at[0], lcr.at[0], me.core())

    @pl.when(owner)
    def _():
        lens_copy.start()

    first = pl.ds(pl.multiple_of(c * 256, 128), 128)
    local = []
    for i, (src, dst) in enumerate(((SQ, wsq), (SK, wsk), (SV, wsv))):
        local.append((src.at[:, first], dst.at[0, :, pl.ds(0, 128)]))
        local.append((src.at[:, pl.ds(128, 128)], dst.at[0, :, pl.ds(128, 128)]))
    local.append((SO.at[first], wso.at[0, pl.ds(0, 128)]))
    local.append((SO.at[pl.ds(128, 128)], wso.at[0, pl.ds(128, 128)]))
    local.append((PACK, BP.at[z]))
    local = [pltpu.make_async_copy(src, dst, sls.at[i]) for i, (src, dst) in enumerate(local)]
    for copy in local:
        copy.start()
    for i, ref in enumerate(vectors):
        PRM[i : i + 1, :] = row(ref)
    PRM[12:13, 0:384] = row(sqb)
    PRM[12:13, 384:768] = row(svb)
    SM[...] = jnp.zeros(SM.shape, F32)

    @pl.when(owner)
    def _():
        lens_copy.wait_send()

    @pl.when(jnp.logical_not(owner))
    def _():
        lens_copy.wait_recv()

    n_keys = X.shape[0]
    position = lax.broadcasted_iota(jnp.int32, (8, n_keys), 1).astype(F32)
    length = jnp.where(owner, LN[0], LN[1])
    bias_row[...] = jnp.where(position < length[:, 0:1], 0.0, MASKED)
    s_bias = pl.ds(pl.multiple_of(c * 256, 128), 128)
    v_bias = pl.ds(pl.multiple_of(384 + c * 256, 128), 128)

    teacher = Layer(
        x=X, wq=WQ, wk=WK, wv=WV, wo=WO, wi=WI, wf=WF, q=q, k=k, v=v, o=o, p=p, xh1=xh1, rs1=rs1, a=a, g=g, gp=gp,
        xh2=xh2, rs2=rs2, df=df, dr=dr, do=do, dq=dq, dk=dk, dv=dv, ds=ds, prow=0, qrow=12, brow=16,
        width=192, flip_attn=True, flip_in=False,
        bias_q=lambda u: BP[2 * c + u, 0:1, 0:192],
        bias_v=lambda u: BP[2 * c + u, 3:4, 0:192],
        bias_i=lambda j: BP[j, 1:2, :],
        third=lambda c: 0, pack=None,
    )
    student = Layer(
        x=x2, wq=wsq, wk=wsk, wv=wsv, wo=wso, wi=SI, wf=SF, q=q2, k=k2, v=v2, o=o2, p=p2, xh1=xh12, rs1=rs12, a=a2,
        g=g2, gp=gp2, xh2=xh22, rs2=rs22, df=df, dr=dr, do=do, dq=dq, dk=dk, dv=dv, ds=ds, prow=6, qrow=24, brow=20,
        width=256, flip_attn=False, flip_in=True,
        bias_q=lambda u: jnp.concatenate([PRM[12:13, s_bias], PRM[12:13, 128:256]], axis=1),
        bias_v=lambda u: jnp.concatenate([PRM[12:13, v_bias], PRM[12:13, 512:640]], axis=1),
        bias_i=lambda j: BP[j, 2:3, 0 : SI.shape[1]],
        third=lambda c: c, pack=lambda: pack_student(),
    )
    swap = Swap(me, send, recv, ssem, rsem, 4)
    far_half, near_half = rows_of(1 - c, 384), rows_of(c, 384)
    half_copy = remote(BX.at[:, far_half], RBX, hcs.at[0], hcr.at[0], me.core())

    def pack_student():
        x = x2[...]
        for i, grad in enumerate((dq, dk, dv)):
            value = tn(x, grad[0]).astype(BF)
            SG[i, 0:768] = value[:, 0:128]
            BX[i] = value[:, 128:256]
        value = tn(o2[0], dr[...]).astype(BF)
        for b in range(6):
            cols = slice(128 * b, 128 * b + 128)
            SG[3, 128 * b : 128 * b + 128] = value[0:128, cols]
            for h in range(2):
                BX[3, 384 * h + 64 * b : 384 * h + 64 * b + 64] = value[128 + 64 * h : 192 + 64 * h, cols]
        half_copy.start()

    def join_halves():
        half_copy.wait()
        SG[:, 768:1152] = (BX[:, near_half].astype(F32) + RBX[...].astype(F32)).astype(BF)

    def teacher_hook(name):
        if name == "qkv":
            gather.advance(3)
            sequences.send(0)
            gather.advance(6)
            sequences.take(0)
            gather.advance(7)
            for copy in pack_copies:
                copy.wait()
            for copy in local:
                copy.wait()
            gather.ready((0, 1, 2))
        if name == "heads":
            gather.advance(7)
        if name == "middle":
            gather.advance(9)
        if name == "attn":
            gather.advance(10)
            gather.ready((3,))
            sequences.send(1)
        if name == "ffn_in":
            gather.advance(11)
            gather.ready((4,))
        if name == "ffn_out":
            gather.advance(12)
            gather.ready((5,))

    def student_hook(name):
        if name == "qkv":
            gather.advance(13)
        if name == "ffn_in":
            gather.ready((6,))
        if name == "ffn_out":
            gather.ready((7,))
            sequences.take(1)

    def to_student(rows, value):
        x2[rows] = value.astype(BF)

    def to_output(rows, value):
        Y[rows] = value.astype(BF)

    def between(rows, value):
        dx2[rows] = value

    def to_grad(rows, value):
        DX[rows] = value.astype(BF)

    forward(teacher, me, swap, bias_row, PRM, teacher_hook, to_student)
    forward(student, me, swap, bias_row, PRM, student_hook, to_output)
    home.send(0)
    gather.drain(range(8))
    sequences.drain(0)
    sequences.drain(1)

    low, high = pl.ds(0, WF.shape[1] // 2), pl.ds(WF.shape[1] // 2, WF.shape[1] // 2)
    top, bottom = pl.ds(0, 384), pl.ds(384, 384)
    grads = [SF, SI, SG, WF.at[:, low], WF.at[:, high], WI.at[:, top], WI.at[:, bottom], WQ, WK, WV, WO]
    lands = [outs[7], outs[6], outs[8], outs[5].at[low], outs[5].at[high], outs[4].at[top], outs[4].at[bottom],
             outs[0], outs[1], outs[2], outs[3]]
    total = Reduce(
        me, grads, lands, KINDS, ((0, 1), (2,), (3, 4), (5, 6), (7, 8, 9, 10)), bufs, reduce_sems
    )
    AHEAD = 2

    def student_back(name):
        if name == "out_grads":
            total.ready(0, AHEAD)
        if name == "ffn_grads":
            total.ready(1, AHEAD)

    def teacher_back(name):
        if name == "start":
            join_halves()
            total.ready(2, AHEAD)
            total.step(AHEAD)
        if name == "out_grads":
            total.ready(3, AHEAD)
        if name == "ffn_grads":
            total.ready(4, AHEAD)
        if name == "attn":
            total.step(AHEAD)
        if name == "middle":
            total.step(AHEAD)
        if name == "heads_done":
            total.step(AHEAD)
        if name == "attn_grads":
            total.ready(5, AHEAD)

    backward(student, me, swap, PRM, SM, lambda rows: CT[rows].astype(F32), student_back, between)
    backward(teacher, me, swap, PRM, SM, lambda rows: dx2[rows], teacher_back, to_grad)
    home.send(1)

    sml[0] = SM[...].astype(BF)
    for d in (1, 2, 3):
        remote(sml.at[0], sml.at[d], sms.at[d - 1], smr.at[d - 1], me.line(d)).start()
    total.step(AHEAD)
    for d in (1, 2, 3):
        remote(sml.at[0], sml.at[d], sms.at[d - 1], smr.at[d - 1], me.line(d)).wait()
    sml[4] = add_up([sml.at[i] for i in range(4)]).astype(BF)
    for k in (1, 2, 3):
        remote(sml.at[4], sml.at[4 + k], sms.at[2 + k], smr.at[2 + k], me.plane(k)).start()
    total.step(AHEAD)
    for k in (1, 2, 3):
        remote(sml.at[4], sml.at[4 + k], sms.at[2 + k], smr.at[2 + k], me.plane(k)).wait()
    both[0] = add_up([sml.at[4 + i] for i in range(4)])
    other_sums = remote(both.at[0], both.at[1], sms.at[6], smr.at[6], me.core())
    other_sums.start()
    total.step(AHEAD)
    other_sums.wait()
    both_sums = pltpu.make_async_copy(both, SUMS, sls.at[9])
    both_sums.start()
    total.rest(AHEAD)
    total.end()
    home.drain(0)
    home.drain(1)
    both_sums.wait()


def final_kernel(*refs):
    z = lax.axis_index("head")
    c = lax.rem(lax.axis_index("seq"), 2)
    YO, DO, SUMS = refs[:3]
    grads = refs[3:12]
    outs = refs[12:]
    outs[0][...] = YO[...].astype(F32)
    outs[1][...] = DO[...].astype(F32)
    for at, w in ((2, 0), (4, 1), (5, 2), (7, 3), (11, 4), (13, 5), (26, 6), (28, 7)):
        outs[at][...] = grads[w][...].astype(F32)
    near = pl.ds(pl.multiple_of(c * 256, 128), 128)
    far = pl.ds(pl.multiple_of((1 - c) * 256, 128), 128)
    packed = grads[8]
    for i, at in enumerate((17, 19, 20)):
        for side, cols, half in ((0, near, c), (1, far, 1 - c)):
            outs[at][:, cols] = packed[side, i, 0:768].astype(F32)
            outs[at][rows_of(half, 384), 128:256] = packed[side, i, 768:1152].astype(F32)
    for side, first, half in ((0, near, c), (1, far, 1 - c)):
        for b in range(6):
            cols = pl.ds(128 * b, 128)
            outs[22][first, cols] = packed[side, 3, 128 * b : 128 * b + 128].astype(F32)
            outs[22][pl.ds(128 + 64 * half, 64), cols] = packed[side, 3, 768 + 64 * b : 832 + 64 * b].astype(F32)

    def put(at, value):
        outs[at][...] = value.reshape(value.shape[1])

    for i, at in enumerate((8, 9, 10, 14, 15, 16, 23, 24, 25, 29, 30, 31)):
        put(at, SUMS[0, i : i + 1, :])
    side = jnp.where(z // 2 == c, 0, 1)
    put(3, SUMS[side, pl.ds(12 + z % 2, 1), 0:192])
    put(6, SUMS[side, pl.ds(14 + z % 2, 1), 0:192])
    put(12, SUMS[0, pl.ds(16 + z, 1), 0 : outs[12].shape[0]])
    put(27, SUMS[0, pl.ds(20 + z, 1), 0 : outs[27].shape[0]])
    for at, r in ((18, 24), (21, 25)):
        low = jnp.where(c == 0, SUMS[0, r : r + 1, 0:128], SUMS[1, r : r + 1, 0:128])
        high = jnp.where(c == 0, SUMS[1, r : r + 1, 0:128], SUMS[0, r : r + 1, 0:128])
        middle = SUMS[0, r : r + 1, 128:256] + SUMS[1, r : r + 1, 128:256]
        put(at, jnp.concatenate([low, middle, high], axis=1))


ANYWHERE = pl.BlockSpec(memory_space=pl.ANY)
IN_VMEM = pl.BlockSpec(memory_space=pltpu.VMEM)


def shape(*dims, kind=BF):
    return jax.ShapeDtypeStruct(dims, kind)


def body(
    tokens, lengths, cotangent,
    t_query, t_query_bias, t_key, t_value, t_value_bias, t_attn_out, t_attn_bias, t_norm1_gain, t_norm1_bias,
    t_ffn_in, t_ffn_in_bias, t_ffn_out, t_ffn_out_bias, t_norm2_gain, t_norm2_bias,
    s_query, s_query_bias, s_key, s_value, s_value_bias, s_attn_out, s_attn_bias, s_norm1_gain, s_norm1_bias,
    s_ffn_in, s_ffn_in_bias, s_ffn_out, s_ffn_out_bias, s_norm2_gain, s_norm2_bias,
):
    seq_size = lax.axis_size("seq")
    outer = seq_size // 2
    groups = [[2 * y + core for y in range(outer)] for core in range(2)]

    def widen(value, axis):
        if outer == 1:
            return value
        return lax.all_gather(value, "seq", axis=axis, tiled=True, axis_index_groups=groups)

    t_ffn_in, t_ffn_in_bias, t_ffn_out = widen(t_ffn_in, 1), widen(t_ffn_in_bias, 0), widen(t_ffn_out, 0)
    s_ffn_in, s_ffn_in_bias, s_ffn_out = widen(s_ffn_in, 1), widen(s_ffn_in_bias, 0), widen(s_ffn_out, 0)
    n_in, n_s = t_ffn_in.shape[1], s_ffn_in.shape[1]
    n = 4 * tokens.shape[1]

    dma = pltpu.SemaphoreType.DMA
    act = lambda *dims, kind=BF: pltpu.VMEM(dims, kind)
    wide = lambda *dims: pltpu.VMEM(dims, F32)
    weights = [
        (2, 192, 768), (2, 192, 768), (2, 192, 768), (2, 192, 768),
        (4, 768, n_in), (4, n_in, 768), (4, n_s, 768), (4, n_s, 768),
        (1, 768, 256), (1, 768, 256), (1, 768, 256), (1, 256, 768),
    ]
    names = len(weights)

    parts = [weights[7], weights[6], (4, 1152, 128), (4, n_in // 2, 768), (4, n_in // 2, 768), (4, 384, n_in), (4, 384, n_in),
             weights[0], weights[1], weights[2], weights[3]]
    pieces = [piece_shape(dims) for dims in parts]
    many = len(parts)

    results = pl.pallas_call(
        main_kernel,
        out_shape=[shape(2, 128, 768), shape(2, 128, 768), shape(2, 32, 768, kind=F32)]
        + [shape(*d[1:]) for d in weights[:8]]
        + [shape(2, 4, 1152, 128)],
        in_specs=[pl.BlockSpec(memory_space=pltpu.SMEM)] + [ANYWHERE] * 14 + [IN_VMEM] * 18,
        out_specs=[ANYWHERE] * 12,
        scratch_shapes=[act(*d) for d in weights]
        + [
            act(n, 768), act(n, 768), wide(2, 8, 128), wide(8, n_in), wide(4, 8, n_in), wide(16, 768), wide(32, 768), act(8, 32, 768), wide(2, 32, 768),
            act(4, 1152, 128), act(4, 768, 128), act(4, 384, 128),
            wide(8, n), act(2, n, 768), act(2, n, 768), dma((2, 4)), dma((2, 4)),
            act(2, n, 256), act(2, n, 256), act(2, n, 256), act(2, n, 256), act(6, n, n),
            wide(n, 768), wide(n, 1), act(n, 768), act(4, n, n_in), act(4, n, n_in), wide(n, 768), wide(n, 1),
            wide(n, 768), act(n, 768), act(2, n, 256), act(2, n, 256), act(2, n, 256), act(2, n, 256), act(n, n),
            act(n, 768), act(1, n, 256), act(1, n, 256), act(1, n, 256), act(1, n, 256), act(3, n, n),
            wide(n, 768), wide(n, 1), act(n, 768), act(4, n, n_s), act(4, n, n_s), wide(n, 768), wide(n, 1),
            wide(n, 768), act(n, 768), act(n, 768),
        ]
        + [act(2, *p) for p in pieces]
        + [act(2, *p) for p in pieces]
        + [act(*p) for p in pieces]
        + [act(*p) for p in pieces]
        + [act(3, dims[1] // 4, dims[2]) for dims in parts]
        + [act(4, 288, 128) if kind == EVERY else act(d[1] // 4, d[2]) for d, kind in zip(parts, KINDS)]
        + [
            dma((8, 3)), dma((8, 3)), dma((8, 3, 2)), dma((8, 3, 2)), dma((8, 3, 2)), dma((8, 3, 2)), dma((8,)), dma((8,)),
            dma((many, 4)), dma((many, 4)), dma((many, 2)), dma((many, 2)), dma((many, 3)), dma((many, 3)),
            dma((many, 2)), dma((many, 2)), dma((many, 2)), dma((many, 2)), dma((many,)), dma((many,)), dma((many,)),
            dma((many, 3)), dma((many, 3)),
            dma((2, 2)), dma((2, 4)), dma((2, 4)), dma((2, 4)), dma((2, 3)), dma((2, 2)),
            dma((3,)), dma((3,)), dma((1,)), dma((1,)), dma((10,)), dma((7,)), dma((7,)), dma((1,)), dma((1,)),
        ],
        compiler_params=pltpu.CompilerParams(collective_id=0, has_side_effects=True, vmem_limit_bytes=VMEM_LIMIT),
        name="layers",
    )(
        lengths, tokens, cotangent, t_query.T, t_key.T, t_value.T, t_attn_out, t_ffn_in, t_ffn_out, s_ffn_in.T, s_ffn_out,
        s_query, s_key, s_value, s_attn_out,
        t_attn_bias, t_norm1_gain, t_norm1_bias, t_ffn_out_bias, t_norm2_gain, t_norm2_bias,
        s_attn_bias, s_norm1_gain, s_norm1_bias, s_ffn_out_bias, s_norm2_gain, s_norm2_bias,
        s_query_bias, s_value_bias, t_query_bias, t_value_bias, t_ffn_in_bias, s_ffn_in_bias,
    )
    results = list(results)

    if outer > 1:
        results[2] = lax.psum(results[2], "seq", axis_index_groups=groups)
        results[3:] = [lax.psum(g.astype(F32), "seq", axis_index_groups=groups).astype(BF) for g in results[3:]]

    f = functools.partial(shape, kind=F32)
    final_shapes = [
        f(2, 128, 768), f(2, 128, 768),
        f(192, 768), f(192), f(192, 768), f(192, 768), f(192), f(192, 768),
        f(768), f(768), f(768), f(768, n_in), f(n_in), f(n_in, 768), f(768), f(768), f(768),
        f(768, 384), f(384), f(768, 384), f(768, 384), f(384), f(384, 768),
        f(768), f(768), f(768), f(n_s, 768), f(n_s), f(n_s, 768), f(768), f(768), f(768),
    ]
    outs = list(
        pl.pallas_call(
            final_kernel,
            out_shape=final_shapes,
            in_specs=[IN_VMEM] * 12,
            out_specs=[IN_VMEM] * len(final_shapes),
            compiler_params=pltpu.CompilerParams(vmem_limit_bytes=VMEM_LIMIT),
            name="final",
        )(*results)
    )
    for i in (2, 4, 5, 26):
        outs[i] = outs[i].T
    if outer > 1:
        y = lax.axis_index("seq") // 2
        for i, axis in ((11, 1), (12, 0), (13, 0), (26, 1), (27, 0), (28, 0)):
            width = outs[i].shape[axis] // outer
            outs[i] = lax.dynamic_slice_in_dim(outs[i], y * width, width, axis)
    return tuple(outs)


def solution(mesh):
    seqs = P(("row", "seq"), "head", None)
    col, line, row_spec = P(None, "head"), P("head"), P("head", None)
    fcol, fline, frow = P(None, ("head", "seq")), P(("head", "seq")), P(("head", "seq"), None)
    rep = P()
    teacher = (col, line, col, col, line, row_spec, rep, rep, rep, fcol, fline, frow, rep, rep, rep)
    student = (rep,) * 9 + (fcol, fline, frow, rep, rep, rep)
    return jax.shard_map(
        body,
        mesh=mesh,
        in_specs=(seqs, P(("row", "seq")), seqs) + teacher + student,
        out_specs=(seqs, seqs) + teacher + student,
        check_vma=False,
    )
```

```python
import functools

import jax
import jax.numpy as jnp
from jax import lax
from jax.experimental import pallas as pl
from jax.experimental.pallas import tpu as pltpu
from jax.sharding import PartitionSpec as P

MESH = pl.DeviceIdType.MESH
F32 = jnp.float32
BF = jnp.bfloat16
EPS = 1e-5
MASKED = -1000000000.0
VMEM_LIMIT = 63 << 20


class Place:
    def __init__(self):
        self.r = lax.axis_index("row")
        self.z = lax.axis_index("head")
        self.s = lax.axis_index("seq")
        self.c = lax.rem(self.s, 2)

    def core(self):
        return (self.r, self.z, self.s + 1 - 2 * self.c)

    def line_index(self, step):
        return lax.rem(self.z + step + 4, 4)

    def line(self, step):
        return (self.r, self.line_index(step), self.s)

    def plane_index(self, k):
        if k == 1:
            return self.r + 1 - 2 * lax.rem(self.r, 2)
        if k == 2:
            return lax.rem(self.r + 2, 4)
        return 3 - self.r

    def plane(self, k):
        return (self.plane_index(k), self.z, self.s)


def greet(me):
    barrier = pltpu.get_barrier_semaphore()
    others = [me.core()] + [me.line(i) for i in (1, 2, 3)] + [me.plane(k) for k in (1, 2, 3)]
    for other in others:
        pl.semaphore_signal(barrier, inc=1, device_id=other, device_id_type=MESH)
    pl.semaphore_wait(barrier, len(others))


def remote(src, dst, send_sem, recv_sem, device):
    return pltpu.make_async_remote_copy(
        src_ref=src, dst_ref=dst, send_sem=send_sem, recv_sem=recv_sem, device_id=device, device_id_type=MESH
    )


def rows_of(index, count, unit=16):
    return pl.ds(pl.multiple_of(index * count, unit), count)


class Gather:
    def __init__(self, me, shards, sems):
        self.me, self.shards = me, shards
        self.zs, self.zr, self.ps, self.pr, self.fs, self.fr, self.ls, self.hs = sems
        self.inner = jnp.logical_and(me.z >= 1, me.z <= 2)
        self.across = {1: me.z != 3, 2: me.z >= 0, 3: me.z != 0}

    def only(self, w, cond):
        return (lambda f: pl.when(cond)(f)) if self.shards[w][2] == 2 else (lambda f: f())

    def slot(self, w, index):
        return index % 2 if self.shards[w][2] == 2 else index

    def quarter(self, w, r):
        return rows_of(r, self.shards[w][0].shape[0] // 4)

    def part(self, w, frm, r, half=None):
        dst = self.shards[w][1]
        count, cols = dst.shape[1] // 4, dst.shape[2]
        slot = self.slot(w, frm)
        if half is None:
            return dst.at[slot, rows_of(r, count)]
        if cols == 768:
            return dst.at[slot, rows_of(r, count), pl.ds(half * 384, 384)]
        return dst.at[slot, rows_of(2 * r + half, count // 2)]

    def begin(self, parts, ahead):
        me = self.me
        self.parts, self.ahead, self.turn = parts, ahead, 0
        for w, (src, dst, count) in enumerate(self.shards):

            @self.only(w, me.z // 2 == me.c)
            def _():
                pltpu.make_async_copy(src, dst.at[self.slot(w, me.z)], self.ls.at[w]).start()

        for i in range(ahead):
            self.send(i)

    def send(self, i):
        me = self.me
        if i >= len(self.parts):
            return
        for w, d in self.parts[i]:

            @self.only(w, me.z // 2 == me.c)
            def _():
                @pl.when(self.across[d])
                def _():
                    self.line_copy(w, d).start()

    def advance(self, until):
        while self.turn < until:
            i = self.turn
            if i < len(self.parts):
                self.to_plane(self.parts[i])
                self.send(i + self.ahead)
            if 0 <= i - 1 < len(self.parts):
                self.onward(self.parts[i - 1])
            self.turn += 1

    def line_copy(self, w, d):
        me = self.me
        return remote(
            self.shards[w][0].at[self.quarter(w, me.r)],
            self.part(w, me.z, me.r),
            self.zs.at[w, d - 1],
            self.zr.at[w, d - 1],
            me.line(d),
        )

    def end_copy(self, w):
        me = self.me
        ref = self.part(w, me.line_index(-2), me.r)
        return remote(ref, ref, self.hs.at[w], self.zr.at[w, jnp.clip(2 * me.z - 2, 0, 2)], (me.r, jnp.clip(3 * (me.z - 1), 0, 3), me.s))

    def plane_copy(self, w, d, k):
        me = self.me
        ref = self.part(w, me.line_index(-d), me.r)
        return remote(ref, ref, self.ps.at[w, d - 1, k - 1], self.pr.at[w, d - 1, k - 1], me.plane(k))

    def on_copy(self, w, d, k):
        me = self.me
        ref = self.part(w, me.line_index(-d), me.plane_index(3 - k), k - 1)
        return remote(ref, ref, self.fs.at[w, d - 1, k - 1], self.fr.at[w, d - 1, k - 1], me.plane(k))

    def each(self, part, step):
        for w, d in part:

            @self.only(w, self.me.line_index(-d) // 2 == self.me.c)
            def _():
                step(w, d)

    def to_plane(self, ws):
        def step(w, d):
            self.line_copy(w, d).wait_recv()
            if d == 2:

                @pl.when(self.inner)
                def _():
                    self.end_copy(w).start()

            self.plane_copy(w, d, 1).start()
            self.plane_copy(w, d, 2).start()

        self.each(ws, step)

    def onward(self, ws):
        def step(w, d):
            for k in (1, 2):
                self.plane_copy(w, d, k).wait_recv()
                self.on_copy(w, d, 3 - k).start()

        self.each(ws, step)

    def ready(self, ws):
        def step(w, d):
            for k in (1, 2):
                self.on_copy(w, d, k).wait_recv()

        self.each([(w, d) for w in ws for d in (1, 2, 3)], step)
        for w in ws:
            src, dst, count = self.shards[w]

            @self.only(w, self.me.z // 2 == self.me.c)
            def _():
                pltpu.make_async_copy(src, dst.at[0], self.ls.at[w]).wait()

    def drain(self, ws):
        def step(w, d):
            if d == 2:

                @pl.when(self.inner)
                def _():
                    self.end_copy(w).wait_send()

            for k in (1, 2):
                self.plane_copy(w, d, k).wait_send()
                self.on_copy(w, d, k).wait_send()

        self.each([(w, d) for w in ws for d in (1, 2, 3)], step)
        for w in ws:

            @self.only(w, self.me.z // 2 == self.me.c)
            def _():
                for d in (1, 2, 3):

                    @pl.when(self.across[d])
                    def _():
                        self.line_copy(w, d).wait_send()


PAIR, OWNER, EVERY = 0, 1, 2
KINDS = (OWNER,) * 2 + (EVERY,) + (OWNER,) * 4 + (PAIR,) * 4


def piece_shape(dims):
    count, rows, cols = dims
    return (count, rows // 4, cols // 2) if cols == 768 else (count, rows // 8, cols)


class Reduce:
    def __init__(self, me, grads, outs, kinds, chunks, bufs, sems):
        self.me, self.grads, self.outs, self.kinds, self.chunks = me, grads, outs, kinds, chunks
        self.RA, self.RB, self.RC, self.RD, self.RZ, self.SUM = bufs
        (self.as_, self.ar, self.bs, self.br, self.zs, self.zr, self.gs, self.gr, self.fs, self.fr, self.ls,
         self.cs, self.cr, self.ns, self.nr) = sems
        self.mx, self.my = lax.rem(me.r, 2), me.r // 2
        self.owner = me.z // 2 == me.c
        self.made = self.launched = self.turn = 0

    def quarter(self, w):
        return self.grads[w].shape[1] // 4

    def piece(self, w, t, half):
        g = self.grads[w]
        q, cols = self.quarter(w), g.shape[2]
        if cols == 768:
            return g.at[:, rows_of(t, q), pl.ds(half * 384, 384)]
        return g.at[:, rows_of(2 * t + half, q // 2)]

    def first_copy(self, w, half, other):
        if half == 0:
            t, k, land = 2 * other + 1 - self.mx, 1, self.RA
        else:
            t, k, land = 2 * (1 - self.my) + other, 2, self.RB
        i = 2 * half + other
        return remote(
            self.piece(w, t, half), land[w].at[other], self.as_.at[w, i], self.ar.at[w, i], self.me.plane(k)
        )

    def start(self, ws):
        for w in ws:
            for other in (0, 1):
                for half in (0, 1):
                    self.first_copy(w, half, other).start()

    def kept(self, w, half, other):
        t = 2 * other + self.mx if half == 0 else 2 * self.my + other
        return self.piece(w, t, half)

    def second_copy(self, w, half):
        if half == 0:
            return remote(
                self.piece(w, 2 * (1 - self.my) + self.mx, 0), self.RC[w], self.bs.at[w, 0], self.br.at[w, 0], self.me.plane(2)
            )
        return remote(
            self.piece(w, 2 * self.my + 1 - self.mx, 1), self.RD[w], self.bs.at[w, 1], self.br.at[w, 1], self.me.plane(1)
        )

    def add_into(self, target, ref):
        target[...] = (target[...].astype(F32) + ref[...].astype(F32)).astype(BF)

    def second(self, ws):
        for w in ws:
            for other in (0, 1):
                for half in (0, 1):
                    self.first_copy(w, half, other).wait()
            for half, land in ((0, self.RA), (1, self.RB)):

                @pl.loop(0, 2)
                def _(other):
                    self.add_into(self.kept(w, half, other), land[w].at[other])

                self.second_copy(w, half).start()

    def along(self, ws):
        me = self.me
        for w in ws:
            for half, land in ((0, self.RC), (1, self.RD)):
                self.second_copy(w, half).wait()
                self.add_into(self.piece(w, me.r, half), land[w])
            if self.kinds[w] == PAIR:
                for u in range(2):

                    @pl.when(2 * me.c + u != me.z)
                    def _():
                        self.unit_copy(w, u).start()

            else:
                for d in (1, 2, 3):
                    self.line_copy(w, d).start()

    def unit_copy(self, w, u):
        me = self.me
        target = 2 * me.c + u
        slot = lax.rem(target - me.z + 3, 4)
        slot = jnp.minimum(slot, 2)
        return remote(
            self.grads[w].at[u, rows_of(me.r, self.quarter(w))],
            self.RZ[w].at[slot],
            self.zs.at[w, u],
            self.zr.at[w, slot],
            (me.r, target, me.s),
        )

    def line_copy(self, w, d):
        me = self.me
        q = self.quarter(w)
        src = self.grads[w].at[me.line_index(d), rows_of(me.r, q)]
        return remote(src, self.RZ[w].at[d - 1], self.zs.at[w, d - 1], self.zr.at[w, d - 1], me.line(d))

    def near_copy(self, w, d):
        mine = self.SUM[w].at[self.me.z]
        return remote(mine, mine, self.ns.at[w, d - 1], self.nr.at[w, d - 1], self.me.line(d))

    def out_part(self, w, t, half=None):
        out, q = self.outs[w], self.quarter(w)
        if self.kinds[w] == EVERY:
            rows = rows_of(t, q) if half is None else rows_of(2 * t + half, q // 2)
            return out.at[0, :, rows]
        if half is None:
            return out.at[rows_of(t, q)]
        if out.shape[1] == 768:
            return out.at[rows_of(t, q), pl.ds(half * 384, 384)]
        return out.at[rows_of(2 * t + half, q // 2)]

    def plane_copy(self, w, k):
        me = self.me
        return remote(self.SUM[w], self.out_part(w, me.r), self.gs.at[w, k - 1], self.gr.at[w, k - 1], me.plane(k))

    def on_copy(self, w, k):
        ref = self.out_part(w, self.me.plane_index(3 - k), k - 1)
        return remote(ref, ref, self.fs.at[w, k - 1], self.fr.at[w, k - 1], self.me.plane(k))

    def own_copy(self, w):
        return pltpu.make_async_copy(self.SUM[w], self.out_part(w, self.me.r), self.ls.at[w])

    def core_copy(self, w):
        if self.kinds[w] == EVERY:
            return remote(self.outs[w].at[0], self.outs[w].at[1], self.cs.at[w], self.cr.at[w], self.me.core())
        return remote(self.outs[w], self.outs[w], self.cs.at[w], self.cr.at[w], self.me.core())

    def only(self, w):
        return (lambda f: pl.when(self.owner)(f)) if self.kinds[w] == PAIR else (lambda f: f())

    def spread_start(self, w):
        self.own_copy(w).start()
        self.plane_copy(w, 1).start()
        self.plane_copy(w, 2).start()

    def spread(self, ws):
        me = self.me
        for w in ws:
            q = self.quarter(w)
            kind = self.kinds[w]
            if kind == PAIR:
                for u in range(2):

                    @pl.when(2 * me.c + u != me.z)
                    def _():
                        self.unit_copy(w, u).wait_send()

                @pl.when(self.owner)
                def _():
                    for d in (1, 2, 3):
                        remote(self.RZ[w].at[0], self.RZ[w].at[d - 1], self.zs.at[w, 0], self.zr.at[w, d - 1], me.core()).wait_recv()
                    own = self.grads[w].at[me.z % 2, rows_of(me.r, q)]
                    self.SUM[w][...] = add_up([own] + [self.RZ[w].at[d] for d in range(3)]).astype(BF)
                    self.spread_start(w)

                continue
            for d in (1, 2, 3):
                self.line_copy(w, d).wait()
            own = self.grads[w].at[me.z, rows_of(me.r, q)]
            total = add_up([own] + [self.RZ[w].at[d] for d in range(3)]).astype(BF)
            if kind == EVERY:
                self.SUM[w][me.z] = total
                for d in (1, 2, 3):
                    self.near_copy(w, d).start()
            else:
                self.SUM[w][...] = total
                self.spread_start(w)

    def spread_near(self, ws):
        for w in ws:
            for d in (1, 2, 3):
                self.near_copy(w, d).wait()
            self.spread_start(w)

    def onward(self, ws):
        for w in ws:

            @self.only(w)
            def _():
                for k in (1, 2):
                    self.plane_copy(w, k).wait()
                    self.on_copy(w, 3 - k).start()

    def finish(self, ws):
        for w in ws:

            @self.only(w)
            def _():
                self.own_copy(w).wait()
                for k in (1, 2):
                    self.on_copy(w, k).wait()
                if self.kinds[w] != OWNER:
                    self.core_copy(w).start()

    def end(self):
        for w, kind in enumerate(self.kinds):
            if kind == PAIR:

                @pl.when(self.owner)
                def _():
                    self.core_copy(w).wait_send()

                @pl.when(jnp.logical_not(self.owner))
                def _():
                    self.core_copy(w).wait_recv()

            elif kind == EVERY:
                self.core_copy(w).wait()

    def launch(self, upto):
        while self.launched < min(upto, self.made, len(self.chunks)):
            self.start(self.chunks[self.launched])
            self.launched += 1

    def ready(self, made, ahead):
        self.made = made
        self.launch(self.turn + ahead)

    def step(self, ahead):
        i = self.turn
        if self.made <= i < len(self.chunks):
            return

        def at(back, every=None):
            chunk = self.chunks[i - back] if 0 <= i - back < len(self.chunks) else ()
            return [w for w in chunk if every is None or every == (self.kinds[w] == EVERY)]

        self.second(at(0))
        self.turn += 1
        self.launch(self.turn + ahead)
        self.along(at(1))
        self.spread(at(2))
        self.spread_near(at(3, True))
        self.onward(at(3, False) + at(4, True))
        self.finish(at(4, False) + at(5, True))

    def rest(self, ahead):
        while self.turn < len(self.chunks) + 4:
            self.step(ahead)


def add_up(refs):
    total = refs[0][...].astype(F32)
    for ref in refs[1:]:
        total = total + ref[...].astype(F32)
    return total


def nn(a, b):
    return lax.dot_general(a, b, (((1,), (0,)), ((), ())), preferred_element_type=F32)


def nt(a, b):
    return lax.dot_general(a, b, (((1,), (1,)), ((), ())), preferred_element_type=F32)


def tn(a, b):
    return lax.dot_general(a, b, (((0,), (0,)), ((), ())), preferred_element_type=F32)


def norm_parts(value):
    center = value - jnp.mean(value, axis=-1, keepdims=True)
    spread = jnp.mean(center * center, axis=-1, keepdims=True)
    rstd = lax.rsqrt(spread + EPS)
    return center * rstd, rstd


def norm_grad(xh, rstd, gain, dy):
    scaled = dy * gain
    mean_one = jnp.mean(scaled, axis=-1, keepdims=True)
    mean_two = jnp.mean(scaled * xh, axis=-1, keepdims=True)
    return (scaled - mean_one - xh * mean_two) * rstd


def col_sum(value):
    return jnp.sum(value, axis=0, keepdims=True)


class Swap:
    def __init__(self, me, send, recv, ssem, rsem, chunks):
        self.me, self.send, self.recv, self.ssem, self.rsem = me, send, recv, ssem, rsem
        self.rows = send.shape[1] // chunks
        self.chunks = chunks
        self.turn = 0

    def copy(self, slot, i):
        rows = rows_of(i, self.rows)
        return remote(
            self.send.at[slot, rows],
            self.recv.at[slot, rows],
            self.ssem.at[slot, i],
            self.rsem.at[slot, i],
            self.me.core(),
        )

    def run(self, part, between, post):
        slot = self.turn % 2
        self.turn += 1

        @pl.loop(0, self.chunks)
        def _(i):
            rows = rows_of(i, self.rows)
            self.send[slot, rows] = part(rows).astype(BF)
            self.copy(slot, i).start()

        if between is not None:
            between()

        @pl.loop(0, self.chunks)
        def _(i):
            rows = rows_of(i, self.rows)
            self.copy(slot, i).wait()
            total = self.send[slot, rows].astype(F32) + self.recv[slot, rows].astype(F32)
            post(i, rows, total)


class Layer:
    def __init__(self, **kw):
        self.__dict__.update(kw)


def head_mask(layer, i, c):
    h = lax.rem(i, 3)
    half = jnp.where(h == 2, layer.third(c), lax.rem(h, 2))
    lane = lax.broadcasted_iota(jnp.int32, (1, 128), 1) // 64
    mask = jnp.where(lane == half, 1.0, 0.0).astype(BF)
    return i // 3, pl.ds(pl.multiple_of((h // 2) * 128, 128), 128), mask


def forward(layer, me, swap, bias_row, prm, hook, done):
    L, c = layer, me.c
    units = L.q.shape[0]

    hook("qkv")
    project = nt if L.flip_attn else nn

    @pl.loop(0, units)
    def _(u):
        x = L.x[...]
        n = L.width
        L.q[u, :, :n] = ((project(x, L.wq[u]) + L.bias_q(u)).astype(BF) * 0.125).astype(BF)
        L.k[u, :, :n] = project(x, L.wk[u]).astype(BF)
        L.v[u, :, :n] = (project(x, L.wv[u]) + L.bias_v(u)).astype(BF)
        if n < 256:
            pad = jnp.zeros((x.shape[0], 256 - n), BF)
            L.q[u, :, n:] = pad
            L.k[u, :, n:] = pad
            L.v[u, :, n:] = pad
        L.o[u] = jnp.zeros(L.o.shape[1:], BF)

    hook("heads")

    def heads(lo, hi):
        @pl.loop(lo, hi)
        def _(i):
            u, cols, mask = head_mask(L, i, c)
            k = L.k[u, :, cols]
            v = L.v[u, :, cols] * mask
            for ch in range(4):
                rows = pl.ds(ch * 128, 128)
                scores = nt(L.q[u, rows, cols] * mask, k) + bias_row[0:1, :]
                top = jnp.max(scores, axis=-1, keepdims=True)
                expo = jnp.exp(scores - top)
                inv = 1.0 / jnp.sum(expo, axis=-1, keepdims=True)
                probs = (expo * inv).astype(BF)
                L.p[i, rows] = probs
                L.o[u, rows, cols] = L.o[u, rows, cols] + nn(probs, v).astype(BF)

    heads(0, 3)
    if units == 2:
        hook("middle")
        heads(3, 6)
    hook("attn")

    def attn_part(rows):
        n = L.width
        total = nn(L.o[0, rows, :n], L.wo[0])
        for u in range(1, units):
            total = total + nn(L.o[u, rows, :n], L.wo[u])
        return total

    def attn_post(i, rows, total):
        value = L.x[rows].astype(F32) + total + prm[L.prow : L.prow + 1, :]
        xh, rstd = norm_parts(value)
        L.xh1[rows] = xh
        L.rs1[rows] = rstd
        L.a[rows] = (xh * prm[L.prow + 1 : L.prow + 2, :] + prm[L.prow + 2 : L.prow + 3, :]).astype(BF)

    swap.run(attn_part, None, attn_post)
    hook("ffn_in")
    enter = nt if L.flip_in else nn

    @pl.loop(0, 4)
    def _(j):
        pre = enter(L.a[...], L.wi[j]) + L.bias_i(j)
        sq = pre * pre
        t = jnp.tanh(0.7978845608028654 * pre * (1.0 + 0.044715 * sq))
        half = 0.5 * (1.0 + t)
        L.g[j] = (pre * half).astype(BF)
        slope = half + 0.5 * pre * (1.0 - t * t) * (0.7978845608028654 + 0.7978845608028654 * 0.134145 * sq)
        L.gp[j] = slope.astype(BF)

    hook("ffn_out")

    def ffn_part(rows):
        total = nn(L.g[0, rows], L.wf[0])
        for j in range(1, 4):
            total = total + nn(L.g[j, rows], L.wf[j])
        return total

    def ffn_post(i, rows, total):
        value = L.a[rows].astype(F32) + total + prm[L.prow + 3 : L.prow + 4, :]
        xh, rstd = norm_parts(value)
        L.xh2[rows] = xh
        L.rs2[rows] = rstd
        done(rows, xh * prm[L.prow + 4 : L.prow + 5, :] + prm[L.prow + 5 : L.prow + 6, :])

    swap.run(ffn_part, None, ffn_post)


def backward(layer, me, swap, prm, sums, upstream, hook, done):
    L, c = layer, me.c
    units = L.q.shape[0]
    prow = L.prow
    n_rows = L.x.shape[0]
    hook("start")
    for i in range(6):
        sums[prow + i : prow + i + 1, :] = jnp.zeros((1, 768), F32)

    @pl.loop(0, n_rows // 128)
    def _(i):
        rows = rows_of(i, 128)
        dy = upstream(rows)
        xh = L.xh2[rows]
        sums[prow + 4 : prow + 5, :] += col_sum(dy * xh)
        sums[prow + 5 : prow + 6, :] += col_sum(dy)
        df = norm_grad(xh, L.rs2[rows], prm[prow + 4 : prow + 5, :], dy)
        low = df.astype(BF)
        sums[prow + 3 : prow + 4, :] += col_sum(low.astype(F32))
        L.df[rows] = df
        L.dr[rows] = low

    @pl.loop(0, 4)
    def _(j):
        dpre = (nt(L.dr[...], L.wf[j]) * L.gp[j].astype(F32)).astype(BF)
        L.gp[j] = dpre
        n = dpre.shape[1]
        sums[pl.ds(L.brow + j, 1), :n] = col_sum(dpre.astype(F32))
        L.wf[j] = tn(L.g[j], L.dr[...]).astype(BF)

    hook("out_grads")
    leave = nn if L.flip_in else nt

    def ffn_part(rows):
        total = leave(L.gp[0, rows], L.wi[0])
        for j in range(1, 4):
            total = total + leave(L.gp[j, rows], L.wi[j])
        return total

    def ffn_weights():
        @pl.loop(0, 4)
        def _(j):
            if L.flip_in:
                L.wi[j] = tn(L.gp[j], L.a[...]).astype(BF)
            else:
                L.wi[j] = tn(L.a[...], L.gp[j]).astype(BF)

        hook("ffn_grads")

    def ffn_post(i, rows, total):
        da = L.df[rows] + total
        xh = L.xh1[rows]
        sums[prow + 1 : prow + 2, :] += col_sum(da * xh)
        sums[prow + 2 : prow + 3, :] += col_sum(da)
        dh = norm_grad(xh, L.rs1[rows], prm[prow + 1 : prow + 2, :], da)
        low = dh.astype(BF)
        sums[prow : prow + 1, :] += col_sum(low.astype(F32))
        L.df[rows] = dh
        L.dr[rows] = low

    swap.run(ffn_part, ffn_weights, ffn_post)
    hook("attn")

    @pl.loop(0, units)
    def _(u):
        n = L.width
        L.do[u, :, :n] = nt(L.dr[...], L.wo[u]).astype(BF)
        if n < 256:
            L.do[u, :, n:] = jnp.zeros((n_rows, 256 - n), BF)
        for ref in (L.dq, L.dk, L.dv):
            ref[u] = jnp.zeros(ref.shape[1:], BF)

    def heads(lo, hi):
        @pl.loop(lo, hi)
        def _(i):
            u, cols, mask = head_mask(L, i, c)
            k = L.k[u, :, cols] * mask
            v = L.v[u, :, cols]
            for ch in range(4):
                rows = pl.ds(ch * 128, 128)
                d_probs = nt(L.do[u, rows, cols] * mask, v)
                probs = L.p[i, rows].astype(F32)
                both = probs * d_probs
                d_scores = (both - probs * jnp.sum(both, axis=-1, keepdims=True)).astype(BF)
                L.ds[rows] = d_scores
                L.dq[u, rows, cols] = L.dq[u, rows, cols] + (nn(d_scores, k) * 0.125).astype(BF)
            L.dv[u, :, cols] = L.dv[u, :, cols] + tn(L.p[i], L.do[u, :, cols] * mask).astype(BF)
            L.dk[u, :, cols] = L.dk[u, :, cols] + tn(L.ds[...], L.q[u, :, cols] * mask).astype(BF)

    heads(0, 3)
    if units == 2:
        hook("middle")
        heads(3, 6)
    hook("heads_done")
    back = nn if L.flip_attn else nt

    def attn_part(rows):
        n = L.width
        total = None
        for u in range(units):
            for grad, weight in ((L.dq, L.wq), (L.dk, L.wk), (L.dv, L.wv)):
                term = back(grad[u, rows, :n], weight[u])
                total = term if total is None else total + term
        return total

    def attn_weights():
        if L.pack is not None:
            L.pack()
            sums[L.qrow : L.qrow + 1, :256] = col_sum(L.dq[0].astype(F32))
            sums[L.qrow + 1 : L.qrow + 2, :256] = col_sum(L.dv[0].astype(F32))
            hook("attn_grads")
            return

        @pl.loop(0, units)
        def _(u):
            n = L.width
            L.wo[u] = tn(L.o[u, :, :n], L.dr[...]).astype(BF)
            x = L.x[...]
            for grad, out in ((L.dq, L.wq), (L.dk, L.wk), (L.dv, L.wv)):
                out[u] = tn(grad[u, :, :n], x).astype(BF)
            sums[pl.ds(L.qrow + u, 1), :256] = col_sum(L.dq[u].astype(F32))
            sums[pl.ds(L.qrow + units + u, 1), :256] = col_sum(L.dv[u].astype(F32))

        hook("attn_grads")

    def attn_post(i, rows, total):
        done(rows, L.df[rows] + total)

    swap.run(attn_part, attn_weights, attn_post)


class Sequences:
    def __init__(self, me, pairs, sems):
        self.me, self.pairs = me, pairs
        self.xs, self.xr, self.fs, self.fr = sems
        self.owner = me.z // 2 == me.c

    def send(self, a):
        me = self.me
        src, dst = self.pairs[a]
        for j in range(2):
            target = 2 * me.c + j

            @pl.when(target != me.z)
            def _():
                remote(src.at[j], dst.at[rows_of(me.z, 128)], self.xs.at[a, j], self.xr.at[a, me.z], (me.r, target, me.s)).start()

            @pl.when(target == me.z)
            def _():
                pltpu.make_async_copy(src.at[j], dst.at[rows_of(me.z, 128)], self.xr.at[a, me.z]).start()

    def core_copy(self, a, frm, i):
        dst = self.pairs[a][1].at[rows_of(frm, 128)]
        return remote(dst, dst, self.fs.at[a, i], self.fr.at[a, frm], self.me.core())

    def take(self, a):
        me = self.me
        src, dst = self.pairs[a]

        @pl.when(self.owner)
        def _():
            pltpu.make_async_copy(src.at[0], dst.at[rows_of(me.z, 128)], self.xr.at[a, me.z]).wait()
            self.core_copy(a, me.z, 0).start()
            for d in (1, 2, 3):
                frm = me.line_index(-d)
                remote(src.at[0], dst.at[rows_of(frm, 128)], self.xs.at[a, 0], self.xr.at[a, frm], me.core()).wait_recv()
                self.core_copy(a, frm, d).start()

        @pl.when(jnp.logical_not(self.owner))
        def _():
            for i in range(4):
                self.core_copy(a, i, i).wait_recv()

    def drain(self, a):
        me = self.me
        src, dst = self.pairs[a]
        for j in range(2):

            @pl.when(2 * me.c + j != me.z)
            def _():
                remote(src.at[j], dst.at[rows_of(me.z, 128)], self.xs.at[a, j], self.xr.at[a, me.z], me.core()).wait_send()

        @pl.when(self.owner)
        def _():
            for i in range(4):
                self.core_copy(a, i, i).wait_send()


class Home:
    def __init__(self, me, pairs, sems):
        self.me, self.pairs = me, pairs
        self.ys, self.yr = sems
        self.owner = me.z // 2 == me.c

    def send(self, a):
        me = self.me
        src, dst = self.pairs[a]

        @pl.when(self.owner)
        def _():
            pltpu.make_async_copy(src.at[rows_of(me.z, 128)], dst.at[me.z % 2], self.yr.at[a, me.z % 2]).start()
            for d in (1, 2, 3):
                remote(
                    src.at[rows_of(me.line_index(d), 128)],
                    dst.at[me.z % 2],
                    self.ys.at[a, d - 1],
                    self.yr.at[a, me.z % 2],
                    me.line(d),
                ).start()

    def drain(self, a):
        me = self.me
        src, dst = self.pairs[a]

        @pl.when(self.owner)
        def _():
            for d in (1, 2, 3):
                remote(src.at[rows_of(0, 128)], dst.at[0], self.ys.at[a, d - 1], self.yr.at[a, 0], me.core()).wait_send()

        for j in range(2):
            chip = 2 * me.c + j

            @pl.when(chip == me.z)
            def _():
                pltpu.make_async_copy(src.at[rows_of(0, 128)], dst.at[j], self.yr.at[a, j]).wait()

            @pl.when(chip != me.z)
            def _():
                remote(src.at[rows_of(0, 128)], dst.at[j], self.ys.at[a, 0], self.yr.at[a, j], me.core()).wait_recv()


def row(ref):
    return ref[...].astype(F32).reshape(1, ref.shape[0])


def main_kernel(*refs):
    me = Place()
    z, c = me.z, me.c
    lens = refs[0]
    (tok, cot, tq, tk, tv, to, ti, tf, si, sf, SQ, SK, SV, SO) = refs[1:15]
    vectors = refs[15:27]
    sqb, svb, tqb, tvb, tib, sib = refs[27:33]
    (YO, DO, SUMS) = refs[33:36]
    outs = refs[36:45]
    rest = list(refs[45:])

    def take(count):
        head, rest[:] = rest[:count], rest[count:]
        return head

    WQ, WK, WV, WO, WI, WF, SI, SF, wsq, wsk, wsv, wso = weights = take(12)
    X, CT, LN, PACK, BP, PRM, SM, sml, both, SG, BX, RBX = take(12)
    bias_row, send, recv, ssem, rsem = take(5)
    q, k, v, o, p, xh1, rs1, a, g, gp, xh2, rs2, df, dr, do, dq, dk, dv, ds = take(19)
    x2, q2, k2, v2, o2, p2, xh12, rs12, a2, g2, gp2, xh22, rs22, dx2, Y, DX = take(16)
    bufs = [take(len(KINDS)) for _ in range(6)]
    gather_sems = take(8)
    reduce_sems = take(15)
    seq_sems, home_sems = take(4), take(2)
    pks, pkr, lcs, lcr, sls, sms, smr, hcs, hcr = take(9)

    LN[0] = jnp.full(LN.shape[1:], lens[z % 2].astype(F32))
    PACK[...] = jnp.zeros(PACK.shape, F32)
    PACK[0:1, 0:192] = row(tqb)
    PACK[1:2, :] = row(tib)
    PACK[2:3, 0 : sib.shape[0]] = row(sib)
    PACK[3:4, 0:192] = row(tvb)
    greet(me)
    owner = z // 2 == c

    sequences = Sequences(me, ((tok, X), (cot, CT)), seq_sems)
    home = Home(me, ((Y, YO), (DX, DO)), home_sems)
    gather = Gather(
        me,
        ((tq, WQ, 2), (tk, WK, 2), (tv, WV, 2), (to, WO, 2), (ti, WI, 4), (tf, WF, 4), (si, SI, 4), (sf, SF, 4)),
        gather_sems,
    )

    pack_copies = [remote(PACK, BP.at[z], pks.at[d - 1], pkr.at[d - 1], me.line(d)) for d in (1, 2, 3)]
    for copy in pack_copies:
        copy.start()
    far_first = (2, 1, 3)
    gather.begin(
        [[(w, d) for d in far_first] for w in (0, 1, 2, 3)]
        + [[(4, d)] for d in far_first]
        + [[(5, d)] for d in far_first]
        + [[(w, d) for d in far_first] for w in (6, 7)],
        3,
    )
    lens_copy = remote(LN.at[0], LN.at[1], lcs.at[0], lcr.at[0], me.core())

    @pl.when(owner)
    def _():
        lens_copy.start()

    first = pl.ds(pl.multiple_of(c * 256, 128), 128)
    local = []
    for i, (src, dst) in enumerate(((SQ, wsq), (SK, wsk), (SV, wsv))):
        local.append((src.at[:, first], dst.at[0, :, pl.ds(0, 128)]))
        local.append((src.at[:, pl.ds(128, 128)], dst.at[0, :, pl.ds(128, 128)]))
    local.append((SO.at[first], wso.at[0, pl.ds(0, 128)]))
    local.append((SO.at[pl.ds(128, 128)], wso.at[0, pl.ds(128, 128)]))
    local.append((PACK, BP.at[z]))
    local = [pltpu.make_async_copy(src, dst, sls.at[i]) for i, (src, dst) in enumerate(local)]
    for copy in local:
        copy.start()
    for i, ref in enumerate(vectors):
        PRM[i : i + 1, :] = row(ref)
    PRM[12:13, 0:384] = row(sqb)
    PRM[12:13, 384:768] = row(svb)
    SM[...] = jnp.zeros(SM.shape, F32)

    @pl.when(owner)
    def _():
        lens_copy.wait_send()

    @pl.when(jnp.logical_not(owner))
    def _():
        lens_copy.wait_recv()

    n_keys = X.shape[0]
    position = lax.broadcasted_iota(jnp.int32, (8, n_keys), 1).astype(F32)
    length = jnp.where(owner, LN[0], LN[1])
    bias_row[...] = jnp.where(position < length[:, 0:1], 0.0, MASKED)
    s_bias = pl.ds(pl.multiple_of(c * 256, 128), 128)
    v_bias = pl.ds(pl.multiple_of(384 + c * 256, 128), 128)

    teacher = Layer(
        x=X, wq=WQ, wk=WK, wv=WV, wo=WO, wi=WI, wf=WF, q=q, k=k, v=v, o=o, p=p, xh1=xh1, rs1=rs1, a=a, g=g, gp=gp,
        xh2=xh2, rs2=rs2, df=df, dr=dr, do=do, dq=dq, dk=dk, dv=dv, ds=ds, prow=0, qrow=12, brow=16,
        width=192, flip_attn=True, flip_in=False,
        bias_q=lambda u: BP[2 * c + u, 0:1, 0:192],
        bias_v=lambda u: BP[2 * c + u, 3:4, 0:192],
        bias_i=lambda j: BP[j, 1:2, :],
        third=lambda c: 0, pack=None,
    )
    student = Layer(
        x=x2, wq=wsq, wk=wsk, wv=wsv, wo=wso, wi=SI, wf=SF, q=q2, k=k2, v=v2, o=o2, p=p2, xh1=xh12, rs1=rs12, a=a2,
        g=g2, gp=gp2, xh2=xh22, rs2=rs22, df=df, dr=dr, do=do, dq=dq, dk=dk, dv=dv, ds=ds, prow=6, qrow=24, brow=20,
        width=256, flip_attn=False, flip_in=True,
        bias_q=lambda u: jnp.concatenate([PRM[12:13, s_bias], PRM[12:13, 128:256]], axis=1),
        bias_v=lambda u: jnp.concatenate([PRM[12:13, v_bias], PRM[12:13, 512:640]], axis=1),
        bias_i=lambda j: BP[j, 2:3, 0 : SI.shape[1]],
        third=lambda c: c, pack=lambda: pack_student(),
    )
    swap = Swap(me, send, recv, ssem, rsem, 4)
    far_half, near_half = rows_of(1 - c, 384), rows_of(c, 384)
    half_copy = remote(BX.at[:, far_half], RBX, hcs.at[0], hcr.at[0], me.core())

    def pack_student():
        x = x2[...]
        for i, grad in enumerate((dq, dk, dv)):
            value = tn(x, grad[0]).astype(BF)
            SG[i, 0:768] = value[:, 0:128]
            BX[i] = value[:, 128:256]
        value = tn(o2[0], dr[...]).astype(BF)
        for b in range(6):
            cols = slice(128 * b, 128 * b + 128)
            SG[3, 128 * b : 128 * b + 128] = value[0:128, cols]
            for h in range(2):
                BX[3, 384 * h + 64 * b : 384 * h + 64 * b + 64] = value[128 + 64 * h : 192 + 64 * h, cols]
        half_copy.start()

    def join_halves():
        half_copy.wait()
        SG[:, 768:1152] = (BX[:, near_half].astype(F32) + RBX[...].astype(F32)).astype(BF)

    def teacher_hook(name):
        if name == "qkv":
            gather.advance(3)
            sequences.send(0)
            gather.advance(6)
            sequences.take(0)
            gather.advance(7)
            for copy in pack_copies:
                copy.wait()
            for copy in local:
                copy.wait()
            gather.ready((0, 1, 2))
        if name == "heads":
            gather.advance(7)
        if name == "middle":
            gather.advance(9)
        if name == "attn":
            gather.advance(10)
            gather.ready((3,))
        if name == "ffn_in":
            gather.advance(11)
            gather.ready((4,))
        if name == "ffn_out":
            gather.advance(12)
            sequences.send(1)
            gather.ready((5,))

    def student_hook(name):
        if name == "qkv":
            gather.advance(13)
        if name == "ffn_in":
            gather.ready((6,))
        if name == "ffn_out":
            gather.ready((7,))

    def to_student(rows, value):
        x2[rows] = value.astype(BF)

    def to_output(rows, value):
        Y[rows] = value.astype(BF)

    def between(rows, value):
        dx2[rows] = value

    def to_grad(rows, value):
        DX[rows] = value.astype(BF)

    forward(teacher, me, swap, bias_row, PRM, teacher_hook, to_student)
    forward(student, me, swap, bias_row, PRM, student_hook, to_output)
    sequences.take(1)
    home.send(0)
    gather.drain(range(8))
    sequences.drain(0)
    sequences.drain(1)

    low, high = pl.ds(0, WF.shape[1] // 2), pl.ds(WF.shape[1] // 2, WF.shape[1] // 2)
    top, bottom = pl.ds(0, 384), pl.ds(384, 384)
    grads = [SF, SI, SG, WF.at[:, low], WF.at[:, high], WI.at[:, top], WI.at[:, bottom], WQ, WK, WV, WO]
    lands = [outs[7], outs[6], outs[8], outs[5].at[low], outs[5].at[high], outs[4].at[top], outs[4].at[bottom],
             outs[0], outs[1], outs[2], outs[3]]
    total = Reduce(
        me, grads, lands, KINDS, ((0, 1), (2,), (3, 4), (5, 6), (7, 8, 9, 10)), bufs, reduce_sems
    )
    AHEAD = 2

    def student_back(name):
        if name == "out_grads":
            total.ready(0, AHEAD)
        if name == "ffn_grads":
            total.ready(1, AHEAD)

    def teacher_back(name):
        if name == "start":
            join_halves()
            total.ready(2, AHEAD)
            total.step(AHEAD)
        if name == "out_grads":
            total.ready(3, AHEAD)
        if name == "ffn_grads":
            total.ready(4, AHEAD)
        if name == "attn":
            total.step(AHEAD)
        if name == "middle":
            total.step(AHEAD)
        if name == "heads_done":
            total.step(AHEAD)
        if name == "attn_grads":
            total.ready(5, AHEAD)

    backward(student, me, swap, PRM, SM, lambda rows: CT[rows].astype(F32), student_back, between)
    backward(teacher, me, swap, PRM, SM, lambda rows: dx2[rows], teacher_back, to_grad)
    home.send(1)

    sml[0] = SM[...].astype(BF)
    for d in (1, 2, 3):
        remote(sml.at[0], sml.at[d], sms.at[d - 1], smr.at[d - 1], me.line(d)).start()
    total.step(AHEAD)
    for d in (1, 2, 3):
        remote(sml.at[0], sml.at[d], sms.at[d - 1], smr.at[d - 1], me.line(d)).wait()
    sml[4] = add_up([sml.at[i] for i in range(4)]).astype(BF)
    for k in (1, 2, 3):
        remote(sml.at[4], sml.at[4 + k], sms.at[2 + k], smr.at[2 + k], me.plane(k)).start()
    total.step(AHEAD)
    for k in (1, 2, 3):
        remote(sml.at[4], sml.at[4 + k], sms.at[2 + k], smr.at[2 + k], me.plane(k)).wait()
    both[0] = add_up([sml.at[4 + i] for i in range(4)])
    other_sums = remote(both.at[0], both.at[1], sms.at[6], smr.at[6], me.core())
    other_sums.start()
    total.step(AHEAD)
    other_sums.wait()
    both_sums = pltpu.make_async_copy(both, SUMS, sls.at[9])
    both_sums.start()
    total.rest(AHEAD)
    total.end()
    home.drain(0)
    home.drain(1)
    both_sums.wait()


def final_kernel(*refs):
    z = lax.axis_index("head")
    c = lax.rem(lax.axis_index("seq"), 2)
    YO, DO, SUMS = refs[:3]
    grads = refs[3:12]
    outs = refs[12:]
    outs[0][...] = YO[...].astype(F32)
    outs[1][...] = DO[...].astype(F32)
    for at, w in ((2, 0), (4, 1), (5, 2), (7, 3), (11, 4), (13, 5), (26, 6), (28, 7)):
        outs[at][...] = grads[w][...].astype(F32)
    near = pl.ds(pl.multiple_of(c * 256, 128), 128)
    far = pl.ds(pl.multiple_of((1 - c) * 256, 128), 128)
    packed = grads[8]
    for i, at in enumerate((17, 19, 20)):
        for side, cols, half in ((0, near, c), (1, far, 1 - c)):
            outs[at][:, cols] = packed[side, i, 0:768].astype(F32)
            outs[at][rows_of(half, 384), 128:256] = packed[side, i, 768:1152].astype(F32)
    for side, first, half in ((0, near, c), (1, far, 1 - c)):
        for b in range(6):
            cols = pl.ds(128 * b, 128)
            outs[22][first, cols] = packed[side, 3, 128 * b : 128 * b + 128].astype(F32)
            outs[22][pl.ds(128 + 64 * half, 64), cols] = packed[side, 3, 768 + 64 * b : 832 + 64 * b].astype(F32)

    def put(at, value):
        outs[at][...] = value.reshape(value.shape[1])

    for i, at in enumerate((8, 9, 10, 14, 15, 16, 23, 24, 25, 29, 30, 31)):
        put(at, SUMS[0, i : i + 1, :])
    side = jnp.where(z // 2 == c, 0, 1)
    put(3, SUMS[side, pl.ds(12 + z % 2, 1), 0:192])
    put(6, SUMS[side, pl.ds(14 + z % 2, 1), 0:192])
    put(12, SUMS[0, pl.ds(16 + z, 1), 0 : outs[12].shape[0]])
    put(27, SUMS[0, pl.ds(20 + z, 1), 0 : outs[27].shape[0]])
    for at, r in ((18, 24), (21, 25)):
        low = jnp.where(c == 0, SUMS[0, r : r + 1, 0:128], SUMS[1, r : r + 1, 0:128])
        high = jnp.where(c == 0, SUMS[1, r : r + 1, 0:128], SUMS[0, r : r + 1, 0:128])
        middle = SUMS[0, r : r + 1, 128:256] + SUMS[1, r : r + 1, 128:256]
        put(at, jnp.concatenate([low, middle, high], axis=1))


ANYWHERE = pl.BlockSpec(memory_space=pl.ANY)
IN_VMEM = pl.BlockSpec(memory_space=pltpu.VMEM)


def shape(*dims, kind=BF):
    return jax.ShapeDtypeStruct(dims, kind)


def body(
    tokens, lengths, cotangent,
    t_query, t_query_bias, t_key, t_value, t_value_bias, t_attn_out, t_attn_bias, t_norm1_gain, t_norm1_bias,
    t_ffn_in, t_ffn_in_bias, t_ffn_out, t_ffn_out_bias, t_norm2_gain, t_norm2_bias,
    s_query, s_query_bias, s_key, s_value, s_value_bias, s_attn_out, s_attn_bias, s_norm1_gain, s_norm1_bias,
    s_ffn_in, s_ffn_in_bias, s_ffn_out, s_ffn_out_bias, s_norm2_gain, s_norm2_bias,
):
    seq_size = lax.axis_size("seq")
    outer = seq_size // 2
    groups = [[2 * y + core for y in range(outer)] for core in range(2)]

    def widen(value, axis):
        if outer == 1:
            return value
        return lax.all_gather(value, "seq", axis=axis, tiled=True, axis_index_groups=groups)

    t_ffn_in, t_ffn_in_bias, t_ffn_out = widen(t_ffn_in, 1), widen(t_ffn_in_bias, 0), widen(t_ffn_out, 0)
    s_ffn_in, s_ffn_in_bias, s_ffn_out = widen(s_ffn_in, 1), widen(s_ffn_in_bias, 0), widen(s_ffn_out, 0)
    n_in, n_s = t_ffn_in.shape[1], s_ffn_in.shape[1]
    n = 4 * tokens.shape[1]

    dma = pltpu.SemaphoreType.DMA
    act = lambda *dims, kind=BF: pltpu.VMEM(dims, kind)
    wide = lambda *dims: pltpu.VMEM(dims, F32)
    weights = [
        (2, 192, 768), (2, 192, 768), (2, 192, 768), (2, 192, 768),
        (4, 768, n_in), (4, n_in, 768), (4, n_s, 768), (4, n_s, 768),
        (1, 768, 256), (1, 768, 256), (1, 768, 256), (1, 256, 768),
    ]
    names = len(weights)

    parts = [weights[7], weights[6], (4, 1152, 128), (4, n_in // 2, 768), (4, n_in // 2, 768), (4, 384, n_in), (4, 384, n_in),
             weights[0], weights[1], weights[2], weights[3]]
    pieces = [piece_shape(dims) for dims in parts]
    many = len(parts)

    results = pl.pallas_call(
        main_kernel,
        out_shape=[shape(2, 128, 768), shape(2, 128, 768), shape(2, 32, 768, kind=F32)]
        + [shape(*d[1:]) for d in weights[:8]]
        + [shape(2, 4, 1152, 128)],
        in_specs=[pl.BlockSpec(memory_space=pltpu.SMEM)] + [ANYWHERE] * 14 + [IN_VMEM] * 18,
        out_specs=[ANYWHERE] * 12,
        scratch_shapes=[act(*d) for d in weights]
        + [
            act(n, 768), act(n, 768), wide(2, 8, 128), wide(8, n_in), wide(4, 8, n_in), wide(16, 768), wide(32, 768), act(8, 32, 768), wide(2, 32, 768),
            act(4, 1152, 128), act(4, 768, 128), act(4, 384, 128),
            wide(8, n), act(2, n, 768), act(2, n, 768), dma((2, 4)), dma((2, 4)),
            act(2, n, 256), act(2, n, 256), act(2, n, 256), act(2, n, 256), act(6, n, n),
            wide(n, 768), wide(n, 1), act(n, 768), act(4, n, n_in), act(4, n, n_in), wide(n, 768), wide(n, 1),
            wide(n, 768), act(n, 768), act(2, n, 256), act(2, n, 256), act(2, n, 256), act(2, n, 256), act(n, n),
            act(n, 768), act(1, n, 256), act(1, n, 256), act(1, n, 256), act(1, n, 256), act(3, n, n),
            wide(n, 768), wide(n, 1), act(n, 768), act(4, n, n_s), act(4, n, n_s), wide(n, 768), wide(n, 1),
            wide(n, 768), act(n, 768), act(n, 768),
        ]
        + [act(2, *p) for p in pieces]
        + [act(2, *p) for p in pieces]
        + [act(*p) for p in pieces]
        + [act(*p) for p in pieces]
        + [act(3, dims[1] // 4, dims[2]) for dims in parts]
        + [act(4, 288, 128) if kind == EVERY else act(d[1] // 4, d[2]) for d, kind in zip(parts, KINDS)]
        + [
            dma((8, 3)), dma((8, 3)), dma((8, 3, 2)), dma((8, 3, 2)), dma((8, 3, 2)), dma((8, 3, 2)), dma((8,)), dma((8,)),
            dma((many, 4)), dma((many, 4)), dma((many, 2)), dma((many, 2)), dma((many, 3)), dma((many, 3)),
            dma((many, 2)), dma((many, 2)), dma((many, 2)), dma((many, 2)), dma((many,)), dma((many,)), dma((many,)),
            dma((many, 3)), dma((many, 3)),
            dma((2, 2)), dma((2, 4)), dma((2, 4)), dma((2, 4)), dma((2, 3)), dma((2, 2)),
            dma((3,)), dma((3,)), dma((1,)), dma((1,)), dma((10,)), dma((7,)), dma((7,)), dma((1,)), dma((1,)),
        ],
        compiler_params=pltpu.CompilerParams(collective_id=0, has_side_effects=True, vmem_limit_bytes=VMEM_LIMIT),
        name="layers",
    )(
        lengths, tokens, cotangent, t_query.T, t_key.T, t_value.T, t_attn_out, t_ffn_in, t_ffn_out, s_ffn_in.T, s_ffn_out,
        s_query, s_key, s_value, s_attn_out,
        t_attn_bias, t_norm1_gain, t_norm1_bias, t_ffn_out_bias, t_norm2_gain, t_norm2_bias,
        s_attn_bias, s_norm1_gain, s_norm1_bias, s_ffn_out_bias, s_norm2_gain, s_norm2_bias,
        s_query_bias, s_value_bias, t_query_bias, t_value_bias, t_ffn_in_bias, s_ffn_in_bias,
    )
    results = list(results)

    if outer > 1:
        results[2] = lax.psum(results[2], "seq", axis_index_groups=groups)
        results[3:] = [lax.psum(g.astype(F32), "seq", axis_index_groups=groups).astype(BF) for g in results[3:]]

    f = functools.partial(shape, kind=F32)
    final_shapes = [
        f(2, 128, 768), f(2, 128, 768),
        f(192, 768), f(192), f(192, 768), f(192, 768), f(192), f(192, 768),
        f(768), f(768), f(768), f(768, n_in), f(n_in), f(n_in, 768), f(768), f(768), f(768),
        f(768, 384), f(384), f(768, 384), f(768, 384), f(384), f(384, 768),
        f(768), f(768), f(768), f(n_s, 768), f(n_s), f(n_s, 768), f(768), f(768), f(768),
    ]
    outs = list(
        pl.pallas_call(
            final_kernel,
            out_shape=final_shapes,
            in_specs=[IN_VMEM] * 12,
            out_specs=[IN_VMEM] * len(final_shapes),
            compiler_params=pltpu.CompilerParams(vmem_limit_bytes=VMEM_LIMIT),
            name="final",
        )(*results)
    )
    for i in (2, 4, 5, 26):
        outs[i] = outs[i].T
    if outer > 1:
        y = lax.axis_index("seq") // 2
        for i, axis in ((11, 1), (12, 0), (13, 0), (26, 1), (27, 0), (28, 0)):
            width = outs[i].shape[axis] // outer
            outs[i] = lax.dynamic_slice_in_dim(outs[i], y * width, width, axis)
    return tuple(outs)


def solution(mesh):
    seqs = P(("row", "seq"), "head", None)
    col, line, row_spec = P(None, "head"), P("head"), P("head", None)
    fcol, fline, frow = P(None, ("head", "seq")), P(("head", "seq")), P(("head", "seq"), None)
    rep = P()
    teacher = (col, line, col, col, line, row_spec, rep, rep, rep, fcol, fline, frow, rep, rep, rep)
    student = (rep,) * 9 + (fcol, fline, frow, rep, rep, rep)
    return jax.shard_map(
        body,
        mesh=mesh,
        in_specs=(seqs, P(("row", "seq")), seqs) + teacher + student,
        out_specs=(seqs, seqs) + teacher + student,
        check_vma=False,
    )
```
